32 devices in a mesh: dp: 4 (over y, core), wide: 8 (over z, x).
Axes of the slice: x: 2, y: 2, z: 4, core: 2. Of those that a mesh axis runs over, the one named last changes fastest.
Arguments:
- block_in: bfloat16 [4, 4, 8192, 512], P(None, 'dp', 'wide'), may hold values from -6 to 6
- cotangent: bfloat16 [4, 4, 8192, 512], P(None, 'dp', 'wide'), may hold values from -6 to 6
- ln1_gain: bfloat16 [512], P('wide'), may hold values from 0.5 to 1.5
- ln1_bias: bfloat16 [512], P('wide'), may hold values from -1.5 to 1.5
- qkv_weight: bfloat16 [512, 1536], P('wide'), may hold values from -0.25 to 0.25
- out_weight: bfloat16 [512, 512], P('wide'), may hold values from -0.75 to 0.75
- ln2_gain: bfloat16 [512], P('wide'), may hold values from 0.5 to 1.5
- ln2_bias: bfloat16 [512], P('wide'), may hold values from -1.5 to 1.5
- up_weight: bfloat16 [512, 2048], P('wide'), may hold values from -0.25 to 0.25
- up_bias: bfloat16 [2048], P('wide'), may hold values from -1.5 to 1.5
- down_weight: bfloat16 [2048, 512], P('wide'), may hold values from -0.125 to 0.125
- down_bias: bfloat16 [512], P('wide'), may hold values from -1.5 to 1.5
- seq_lengths: int32 [4, 4, 8], P(None, 'dp'), may hold values from 1 to 8185, as said below
Outputs:
- block_out: bfloat16 [4, 4, 8192, 512], P(None, 'dp', 'wide')
- grad_input: float32 [4, 4, 8192, 512], P(None, 'dp', 'wide')
- grad_ln1_gain: float32 [512], P('wide')
- grad_ln1_bias: float32 [512], P('wide')
- grad_qkv_weight: float32 [512, 1536], P('wide')
- grad_out_weight: float32 [512, 512], P('wide')
- grad_ln2_gain: float32 [512], P('wide')
- grad_ln2_bias: float32 [512], P('wide')
- grad_up_weight: float32 [512, 2048], P('wide')
- grad_up_bias: float32 [2048], P('wide')
- grad_down_weight: float32 [2048, 512], P('wide')
- grad_down_bias: float32 [512], P('wide')
The draws below stay inside these ranges and needn't reach their ends.
Inputs may be any that keep to these rules, and one draw needn't show every extreme that they name: `seq_lengths`: for each micro-batch and group, 8 lengths of 1 or more that sum to 8192; the fourth is the longest and begins within the group's first 1024 positions and ends within its last 1024; in every draw some group's fourth sequence is 8185 long.
All inputs are finite; a program needn't handle non-finite values.
Results may differ from the reference program's by a relative error of at most 0.019.
Values may be sent and summed in bfloat16 or wider, within the bound.
A program may use at most 320 MiB of HBM per device.

```python
import jax
import jax.numpy as jnp
from jax import lax

D = 512
HEADS = 8
HEAD = 64
FF = 2048
TOK_DEV = 1024
MICRO = 4
GROUPS = 4
SPAN = 8192


def split_parts(key, total, parts):
    cuts = jnp.sort(jax.random.randint(key, total.shape + (parts - 1,), 0, total[..., None] - parts + 1), axis=-1)
    zeros = jnp.zeros(total.shape + (1,), jnp.int32)
    edges = jnp.concatenate([zeros, cuts.astype(jnp.int32), (total[..., None] - parts).astype(jnp.int32)], axis=-1)
    return jnp.diff(edges, axis=-1) + 1


def draw_seq_lengths(key, part):
    key = jax.random.fold_in(key, 7)
    keys = jax.random.split(key, 4)
    shape = (MICRO, GROUPS)
    before = jax.random.randint(keys[0], shape, 3, TOK_DEV).astype(jnp.int32)
    after = jax.random.randint(keys[1], shape, 4, TOK_DEV).astype(jnp.int32)
    before = before.at[0, 0].set(3)
    after = after.at[0, 0].set(4)
    first = split_parts(keys[2], before, 3)
    closing = split_parts(keys[3], after, 4)
    longest = (SPAN - before - after)[..., None]
    return jnp.concatenate([first, longest, closing], axis=-1).astype(jnp.int32)


def level_of(own_key, extent, cuts, smallest, largest):
    level, own = 1.0, jax.random.fold_in(own_key, 6)
    for position, blocks in cuts:
        draws = jnp.exp(jax.random.uniform(jax.random.fold_in(own, position), (blocks,), jnp.float32, smallest / len(cuts), largest / len(cuts)))
        level = level * jnp.repeat(draws, extent[position] // blocks).reshape([-1 if axis == position else 1 for axis in range(len(extent))])
    return level


def scatter_about(stream_key, dims, scale, reach, shards=(), kind=jnp.bfloat16):
    values = scale * jax.random.normal(stream_key, dims, jnp.float32)
    if shards:
        values = values * level_of(stream_key, dims, shards, -0.22, 0.18)
    return jnp.clip(values, -reach, reach).astype(kind)


def setup_inputs(seed: int = 0) -> dict:
    arg_keys = jax.random.split(jax.random.key(seed), 14)
    block_in = scatter_about(arg_keys[0], (MICRO, GROUPS, SPAN, D), 1.0, 6.0, ((1, 4), (2, 8)))
    cotangent = scatter_about(arg_keys[1], (MICRO, GROUPS, SPAN, D), 1.0, 6.0, ((1, 4), (2, 8)))
    ln1_gain = jnp.clip(1.0 + 0.1 * jax.random.normal(arg_keys[2], (D,), jnp.float32), 0.5, 1.5).astype(jnp.bfloat16)
    ln1_bias = scatter_about(arg_keys[3], (D,), 0.3, 1.5, ((0, 8),))
    qkv_weight = scatter_about(arg_keys[4], (D, 3 * D), D ** -0.5, 0.25, ((0, 8),))
    out_weight = scatter_about(arg_keys[5], (D, D), (D * TOK_DEV // SPAN) ** -0.5, 0.75, ((0, 8),))
    ln2_gain = jnp.clip(1.0 + 0.1 * jax.random.normal(arg_keys[6], (D,), jnp.float32), 0.5, 1.5).astype(jnp.bfloat16)
    ln2_bias = scatter_about(arg_keys[7], (D,), 0.3, 1.5, ((0, 8),))
    up_weight = scatter_about(arg_keys[8], (D, FF), D ** -0.5, 0.25, ((0, 8),))
    up_bias = scatter_about(arg_keys[9], (FF,), 0.3, 1.5, ((0, 8),))
    down_weight = scatter_about(arg_keys[10], (FF, D), FF ** -0.5, 0.125, ((0, 8),))
    down_bias = scatter_about(arg_keys[11], (D,), 0.3, 1.5, ((0, 8),))
    seq_lengths = draw_seq_lengths(jax.random.fold_in(arg_keys[13], 71), 0)
    return {"block_in": block_in, "cotangent": cotangent, "ln1_gain": ln1_gain, "ln1_bias": ln1_bias, "qkv_weight": qkv_weight, "out_weight": out_weight, "ln2_gain": ln2_gain, "ln2_bias": ln2_bias, "up_weight": up_weight, "up_bias": up_bias, "down_weight": down_weight, "down_bias": down_bias, "seq_lengths": seq_lengths}


@jax.custom_vjp
def low(v):
    return lax.optimization_barrier(v.astype(jnp.bfloat16)).astype(jnp.float32)

@jax.custom_vjp
def low_back(v):
    return v

def low_keep(v):
    return (low(v), None)

def low_pass(kept, grad):
    return (grad,)

def back_keep(v):
    return (v, None)

def back_low(kept, grad):
    return (low(grad),)
low.defvjp(low_keep, low_pass)
low_back.defvjp(back_keep, back_low)
EPSILON = 1e-05
PRECISE = lax.Precision.HIGHEST

def layer_norm(values, gain, shift):
    average = lax.optimization_barrier(jnp.mean(values, axis=-1, keepdims=True))
    centred = values - average
    spread = lax.optimization_barrier(jnp.mean(centred * centred, axis=-1, keepdims=True))
    return centred * lax.rsqrt(spread + EPSILON) * gain + shift

def feature(values):
    return jax.nn.elu(values) + 1.0

def segment_starts(lengths, places):
    seq_ends = jnp.cumsum(lengths, axis=-1).astype(jnp.int32)
    closed = seq_ends[..., None, :] <= places[:, None]
    return lax.optimization_barrier(jnp.sum(jnp.where(closed, lengths[..., None, :], 0), axis=-1)).astype(jnp.int32)

def attend_block(carried_in, block_items):
    key_state, normal = carried_in
    query_feat, key_feat, values, starts, offset = block_items
    block_rows = starts.shape[-1]
    positions = jnp.arange(block_rows, dtype=jnp.int32)
    causal = positions[:, None] >= positions[None, :]
    allowed = causal[None, None] & (starts[:, None, :, None] == starts[:, None, None, :])
    raw_scores = jnp.einsum('nthe,nshe->nhts', query_feat, key_feat, precision=PRECISE)
    scores = low_back(low(jnp.where(allowed, raw_scores, 0.0)))
    sees_state = (starts < offset).astype(jnp.float32)
    carried = jnp.einsum('nthe,nhef->nthf', query_feat, low(key_state), precision=PRECISE)
    numerator = jnp.einsum('nhts,nshf->nthf', scores, values, precision=PRECISE) + sees_state[:, :, None, None] * carried
    numerator = low_back(numerator)
    denominator = jnp.transpose(lax.optimization_barrier(jnp.sum(scores, axis=-1)), (0, 2, 1)) + sees_state[:, :, None] * lax.optimization_barrier(jnp.sum(query_feat * normal[:, None], axis=-1))
    result = numerator / denominator[..., None]
    final_start = starts[:, -1]
    in_last = (starts == final_start[:, None]).astype(jnp.float32)
    carry_keep = 1.0 - (final_start >= offset).astype(jnp.float32)
    last_keys = key_feat * in_last[:, :, None, None]
    own_state = low_back(jnp.einsum('nthe,nthf->nhef', last_keys, values, precision=PRECISE))
    key_state = own_state + carry_keep[:, None, None, None] * key_state
    normal = lax.optimization_barrier(jnp.sum(last_keys, axis=1)) + carry_keep[:, None, None] * normal
    return ((key_state, normal), result)

def forward(tokens, ln1_gain, ln1_bias, qkv_weight, out_weight, ln2_gain, ln2_bias, up_weight, up_bias, down_weight, down_bias, starts):
    group_count, span_len = (tokens.shape[0], tokens.shape[1])
    normed = low(layer_norm(tokens, ln1_gain, ln1_bias))
    projected = low_back(jnp.dot(normed.reshape(-1, D), qkv_weight, precision=PRECISE))
    projected = projected.reshape(group_count, span_len, 3, HEADS, HEAD)
    query_feat = low(feature(projected[:, :, 0]))
    key_feat = low(feature(projected[:, :, 1]))
    values = low(projected[:, :, 2])
    blocks = span_len // TOK_DEV

    def split_blocks(tensor):
        return jnp.moveaxis(tensor.reshape((group_count, blocks, TOK_DEV) + tensor.shape[2:]), 1, 0)
    offsets = jnp.arange(blocks, dtype=jnp.int32) * TOK_DEV
    initial = (jnp.zeros((group_count, HEADS, HEAD, HEAD), jnp.float32), jnp.zeros((group_count, HEADS, HEAD), jnp.float32))
    _, attended = lax.scan(jax.checkpoint(attend_block), initial, (split_blocks(query_feat), split_blocks(key_feat), split_blocks(values), split_blocks(starts), offsets))
    attended = jnp.moveaxis(attended, 0, 1).reshape(group_count * span_len, D)
    mixed = low(attended)
    branch = low_back(jnp.dot(mixed, out_weight, precision=PRECISE))
    middle = tokens.reshape(-1, D) + branch
    second = low(layer_norm(middle, ln2_gain, ln2_bias))
    hidden = low_back(jnp.dot(second, up_weight, precision=PRECISE) + up_bias)
    active = low(jax.nn.gelu(hidden))
    output = low_back(jnp.dot(active, down_weight, precision=PRECISE) + down_bias)
    return (middle + output).reshape(tokens.shape)

def reference(block_in, cotangent, ln1_gain, ln1_bias, qkv_weight, out_weight, ln2_gain, ln2_bias, up_weight, up_bias, down_weight, down_bias, seq_lengths):
    weights = tuple((element.astype(jnp.float32) for element in (ln1_gain, ln1_bias, qkv_weight, out_weight, ln2_gain, ln2_bias, up_weight, up_bias, down_weight, down_bias)))
    places = jnp.arange(SPAN, dtype=jnp.int32)

    def one_micro(running, element):
        tokens, upstream, lengths = element
        starts = segment_starts(lengths, places)

        def run_block(inputs, *params):
            return forward(inputs, *params, starts)
        output, pullback = jax.vjp(run_block, tokens.astype(jnp.float32), *weights)
        gradients = pullback(upstream.astype(jnp.float32))
        running = tuple((before + gradient for before, gradient in zip(running, gradients[1:])))
        return (running, (output.astype(jnp.bfloat16), gradients[0]))
    initial = tuple((jnp.zeros(weight_item.shape, jnp.float32) for weight_item in weights))
    totals, (outputs, input_grad) = lax.scan(one_micro, initial, (block_in, cotangent, seq_lengths))
    return (outputs, input_grad, totals[0], totals[1], totals[2], totals[3], totals[4], totals[5], totals[6], totals[7], totals[8], totals[9])
```

```python
import functools

import jax
import jax.numpy as jnp
from jax import lax
from jax.experimental import pallas as pl
from jax.experimental.pallas import tpu as pltpu
from jax.sharding import PartitionSpec as P

HEADS = 8
EPSILON = 1e-05
F32 = jnp.float32
BF16 = jnp.bfloat16
CHUNK = 128
TILE = 512
FF_TILE = 512
VMEM = 60 * 1024 * 1024


def nn(a, b):
    return lax.dot_general(a, b, (((1,), (0,)), ((), ())), preferred_element_type=F32)


def nt(a, b):
    return lax.dot_general(a, b, (((1,), (1,)), ((), ())), preferred_element_type=F32)


def rows_of(row, width):
    return jnp.concatenate([row] * (width // 128), axis=1)


def start_of(lens, m, place):
    start, end = jnp.zeros_like(place), 0
    for j in range(lens.shape[1]):
        end = end + lens[m, j]
        start = start + jnp.where(end <= place, lens[m, j], 0)
    return start


def place_rows(first, count):
    return first + lax.broadcasted_iota(jnp.int32, (count, 128), 0)


def flag(condition):
    return jnp.where(condition, 1.0, 0.0)


def normed(x):
    average = jnp.mean(x, axis=-1, keepdims=True)
    centred = x - average
    spread = jnp.mean(centred * centred, axis=-1, keepdims=True)
    scale = lax.rsqrt(spread + EPSILON)
    return centred * scale, scale


def norm_back(e, xhat, scale, gain):
    a = gain * e
    return scale * (
        a - jnp.mean(a, axis=-1, keepdims=True) - xhat * jnp.mean(a * xhat, axis=-1, keepdims=True)
    )


def feature(v):
    return jnp.where(v > 0.0, v + 1.0, jnp.exp(jnp.minimum(v, 0.0)))


def column_sum(a):
    return jnp.sum(a, axis=0, keepdims=True)


def by_group(fn, *arrays):
    return jnp.concatenate(
        [fn(g, *[a[:, 256 * g : 256 * g + 256] for a in arrays]) for g in range(2)], axis=1
    )


def lane_half(shape):
    return lax.broadcasted_iota(jnp.int32, shape, 1) < 64


def pack_state(state, norm, out):
    folded = []
    for s in state:
        y = s[:, :128] + s[:, 128:]
        folded.append(y + pltpu.roll(y, 64, 1))
    out[0:256, :] = jnp.where(lane_half((256, 128)), folded[0], folded[1]).astype(out.dtype)
    row = lax.broadcasted_iota(jnp.int32, (16, 128), 0)
    tail = jnp.zeros((16, 128), F32)
    for j in range(4):
        tail = jnp.where(row == j, norm[:, 128 * j : 128 * j + 128], tail)
    out[256:272, :] = tail.astype(out.dtype)
    if out.shape[0] > 272:
        out[272:, :] = jnp.zeros((out.shape[0] - 272, 128), out.dtype)


def unpack_state(packed, ones):
    z = packed[0:256, :]
    turned = pltpu.roll(z, 64, 1)
    half = lane_half((256, 128))
    groups = []
    for part in (jnp.where(half, z, turned), jnp.where(half, turned, z)):
        groups.append(jnp.concatenate([part, part], axis=1).astype(BF16) * ones)
    tail = packed[256:272, :]
    norm = jnp.concatenate([tail[j : j + 1, :] for j in range(4)], axis=1)
    return groups, norm


MESH = pl.DeviceIdType.MESH


def place():
    dp = lax.axis_index("dp")
    return lax.rem(dp, 2), dp // 2, lax.axis_index("wide"), lax.axis_size("dp") // 2, lax.axis_size("wide")


def others(count, fn):
    def body(o, carry):
        fn(o)
        return carry

    lax.fori_loop(1, count, body, 0)


def remote(src, dst, send, recv, dp, wide):
    return pltpu.make_async_remote_copy(
        src_ref=src, dst_ref=dst, send_sem=send, recv_sem=recv, device_id=(dp, wide), device_id_type=MESH
    )


def greet():
    core, y, me, ny, n = place()
    dp = 2 * y + core
    barrier = pltpu.get_barrier_semaphore()

    def signal(d, w):
        pl.semaphore_signal(barrier, inc=1, device_id=(d, w), device_id_type=MESH)

    others(n, lambda o: signal(dp, lax.rem(me + o, n)))
    others(ny, lambda o: signal(2 * lax.rem(y + o, ny) + core, me))
    signal(2 * y + 1 - core, me)
    pl.semaphore_wait(barrier, n - 1 + ny - 1 + 1)


class Gather:
    def __init__(self, src, dst, sems):
        self.src, self.dst = src, dst
        self.near, self.send, self.recv, self.y_send, self.y_recv, self.c_send, self.c_recv = sems
        self.core, self.y, self.me, self.ny, self.n = place()
        self.dp = 2 * self.y + self.core
        each = src.shape[0]
        self.split = split_of(each)
        part = each // self.split
        if self.split == 1:
            self.rows, self.half = pl.ds(0, each), None
        else:
            at = self.core * (each // 2) + self.y * part
            self.rows = pl.ds(pl.multiple_of(at, part), part)
            self.half = pl.ds(pl.multiple_of(self.core * (each // 2), each // 2), each // 2)

    def own(self):
        return pltpu.make_async_copy(self.src.at[self.rows], self.dst.at[self.me, self.rows], self.near)

    def out(self, o):
        to = lax.rem(self.me + o, self.n)
        return remote(self.src.at[self.rows], self.dst.at[self.me, self.rows], self.send.at[o], self.recv.at[self.me], self.dp, to)

    def back(self, o):
        frm = lax.rem(self.me + o, self.n)
        part = self.dst.at[frm, self.rows]
        return remote(part, part, self.send.at[o], self.recv.at[frm], self.dp, frm)

    def start_wide(self):
        self.own().start()
        others(self.n, lambda o: self.out(o).start())

    def finish_wide(self):
        self.own().wait()
        others(self.n, lambda o: self.out(o).wait_send())
        others(self.n, lambda o: self.back(o).wait_recv())

    def along_y(self, o):
        part = self.dst.at[:, self.rows]
        to = lax.rem(self.y + o, self.ny)
        return remote(part, part, self.y_send.at[o], self.y_recv.at[self.y], 2 * to + self.core, self.me)

    def along_y_back(self, o):
        frm = lax.rem(self.y + o, self.ny)
        each = self.src.shape[0]
        part = each // self.split
        at = self.core * (each // 2) + frm * part
        ref = self.dst.at[:, pl.ds(pl.multiple_of(at, part), part)]
        return remote(ref, ref, self.y_send.at[o], self.y_recv.at[frm], 2 * frm + self.core, self.me)

    def start_y(self):
        if self.split > 1:
            others(self.ny, lambda o: self.along_y(o).start())

    def finish_y(self):
        if self.split > 1:
            others(self.ny, lambda o: self.along_y(o).wait_send())
            others(self.ny, lambda o: self.along_y_back(o).wait_recv())

    def cross(self):
        part = self.dst.at[:, self.half]
        return remote(part, part, self.c_send, self.c_recv, 2 * self.y + 1 - self.core, self.me)

    def cross_back(self):
        each = self.src.shape[0]
        at = (1 - self.core) * (each // 2)
        part = self.dst.at[:, pl.ds(pl.multiple_of(at, each // 2), each // 2)]
        return remote(part, part, self.c_send, self.c_recv, 2 * self.y + 1 - self.core, self.me)

    def start_core(self):
        if self.split > 1:
            self.cross().start()

    def finish_core(self):
        if self.split > 1:
            self.cross().wait_send()
            self.cross_back().wait_recv()


def split_of(each):
    count = lax.axis_size("dp")
    return count if each % (16 * count) == 0 else 1


def gather_sems():
    n, ny = lax.axis_size("wide"), lax.axis_size("dp") // 2
    dma = pltpu.SemaphoreType.DMA
    return [dma, dma((n,)), dma((n,)), dma((ny,)), dma((ny,)), dma, dma]


HIGH = 4


def low_count():
    return lax.axis_size("wide") // HIGH


def state_rows():
    unit = 16 * low_count()
    return -(-272 // unit) * unit


class Running:
    def __init__(self, own, upward, refs):
        self.own, self.upward = own, upward
        (self.slots, self.group, self.high, self.mine, self.spread, self.result, self.near, self.send1, self.recv1,
         self.send2, self.recv2, self.send3, self.recv3) = refs
        _, _, self.me, _, _ = place()
        self.dp = lax.axis_index("dp")
        self.lo = low_count()
        self.h, self.l = self.me // self.lo, lax.rem(self.me, self.lo)
        self.part = state_rows() // self.lo

    def slice(self, l):
        return pl.ds(pl.multiple_of(l * self.part, self.part), self.part)

    def copy1(self, o, back=False):
        other = lax.rem(self.l + o, self.lo)
        slot = other if back else self.l
        return remote(self.own, self.slots.at[slot], self.send1.at[o], self.recv1.at[slot], self.dp, self.h * self.lo + other)

    def near1(self):
        return pltpu.make_async_copy(self.own, self.slots.at[self.l], self.near.at[0])

    def start1(self):
        self.near1().start()
        others(self.lo, lambda o: self.copy1(o).start())

    def before(self, a, b):
        return a < b if self.upward else a > b

    def finish1_start2(self):
        self.near1().wait()
        others(self.lo, lambda o: self.copy1(o).wait_send())
        others(self.lo, lambda o: self.copy1(o, True).wait_recv())
        every = jnp.zeros(self.own.shape, F32)
        inner = every
        for l in range(self.lo):
            part = self.slots[l].astype(F32)
            every = every + part
            inner = inner + jnp.where(self.before(l, self.l), part, 0.0)
        self.group[...] = every.astype(BF16)
        self.result[...] = inner

        def send(o):
            other = lax.rem(self.h + o, HIGH)

            @pl.when(self.before(self.h, other))
            def _():
                self.copy2(o).start()

        others(HIGH, send)

    def copy2(self, o, back=False):
        other = lax.rem(self.h + o, HIGH)
        slot = other if back else self.h
        return remote(
            self.group.at[:, self.slice(self.l)], self.high.at[slot], self.send2.at[o], self.recv2.at[slot],
            self.dp, other * self.lo + self.l,
        )

    def finish2_start3(self):
        def wait(o):
            other = lax.rem(self.h + o, HIGH)

            @pl.when(self.before(self.h, other))
            def _():
                self.copy2(o).wait_send()

            @pl.when(self.before(other, self.h))
            def _():
                self.copy2(o, True).wait_recv()

        others(HIGH, wait)
        total = jnp.zeros(self.mine.shape, F32)
        for h in range(HIGH):
            total = total + jnp.where(self.before(h, self.h), self.high[h].astype(F32), 0.0)
        self.mine[...] = total.astype(BF16)
        self.near3().start()
        others(self.lo, lambda o: self.copy3(o).start())

    def near3(self):
        return pltpu.make_async_copy(self.mine, self.spread.at[self.l], self.near.at[1])

    def copy3(self, o, back=False):
        other = lax.rem(self.l + o, self.lo)
        slot = other if back else self.l
        return remote(self.mine, self.spread.at[slot], self.send3.at[o], self.recv3.at[slot], self.dp, self.h * self.lo + other)

    def finish3(self):
        self.near3().wait()
        others(self.lo, lambda o: self.copy3(o).wait_send())
        others(self.lo, lambda o: self.copy3(o, True).wait_recv())
        for l in range(self.lo):
            rows = slice(l * self.part, (l + 1) * self.part)
            self.result[:, rows] = self.result[:, rows] + self.spread[l].astype(F32)


def running_scratch(micro):
    lo, rows = low_count(), state_rows()
    dma = pltpu.SemaphoreType.DMA
    return [
        pltpu.VMEM((lo, micro, rows, 128), BF16),
        pltpu.VMEM((micro, rows, 128), BF16),
        pltpu.VMEM((HIGH, micro, rows // lo, 128), BF16),
        pltpu.VMEM((micro, rows // lo, 128), BF16),
        pltpu.VMEM((lo, micro, rows // lo, 128), BF16),
        pltpu.VMEM((micro, rows, 128), F32),
        dma((2,)), dma((lo,)), dma((lo,)), dma((HIGH,)), dma((HIGH,)), dma((lo,)), dma((lo,)),
    ]


def vector_tile(vectors, each):
    row = lax.broadcasted_iota(jnp.int32, (16, 128), 0)

    def padded(piece):
        return jnp.concatenate([piece.astype(F32), jnp.zeros((1, 128 - each), F32)], axis=1)

    pieces = [padded(v[...]) for v in vectors[:5]]
    hidden = vectors[5][...]
    pieces += [padded(hidden[:, each * r : each * r + each]) for r in range(hidden.shape[1] // each)]
    tile = jnp.zeros((16, 128), F32)
    for j, piece in enumerate(pieces):
        tile = jnp.where(row == j, piece, tile)
    return tile.astype(BF16)


def spread_vectors(slots, out, each):
    n = slots.shape[0]
    d = each * n
    per = 4 * each
    row = lax.broadcasted_iota(jnp.int32, (16, 128), 0)
    blocks = [jnp.zeros((16, 128), F32) for _ in range(d // 128)]
    for w in range(n):
        tile = slots[w].astype(F32)
        at = each * w
        moved = pltpu.roll(tile, at % 128, 1) if at % 128 else tile
        blocks[at // 128] = blocks[at // 128] + jnp.where(row < 5, moved, 0.0)
        for r in range(4):
            at = per * w + each * r
            to_row, lane = 5 + at // d, at % d
            only = jnp.where(row == 5 + r, tile, 0.0)
            moved = pltpu.roll(only, lane % 128, 1) if lane % 128 else only
            if to_row != 5 + r:
                moved = pltpu.roll(moved, (to_row - 5 - r) % 16, 0)
            blocks[lane // 128] = blocks[lane // 128] + moved
    for j, block in enumerate(blocks):
        out[:, 128 * j : 128 * j + 128] = block


def first_kernel(
    lens, off, x, *refs
):
    (s_qkv, s_out, s_up, s_down, v0, v1, v2, v3, v4, v5, ones,
     q_out, k_out, v_out, num_out, kc_out, states_out, state_in, w_qkv, w_out, w_up, w_down, vec_out,
     w_ref, q_all, k_all, v_all, acc, zacc, state, norm, local, tile, tiles_ref, tile_near, tile_send, tile_recv,
     save_sem, *rest) = refs
    each = s_qkv.shape[0]
    running_refs, rest = rest[:13], rest[13:]
    jobs = []
    d = x.shape[1]
    for j in range(3):
        jobs.append(Gather(s_qkv.at[:, d * j : d * j + d], w_ref.at[j], rest[7 * j : 7 * j + 7]))
    for j, (src, dst) in enumerate(((s_out, w_out), (s_up, w_up), (s_down, w_down))):
        jobs.append(Gather(src, dst, rest[21 + 7 * j : 28 + 7 * j]))
    running = Running(local, True, running_refs)
    rows = x.shape[0]
    micro = local.shape[0]
    block_rows = num_out.shape[0]
    tiles = block_rows // rows
    steps = micro * tiles
    i = pl.program_id(0)
    core, y, me, ny, n = place()
    dp = 2 * y + core

    def vec_copy(o, back=False):
        other = lax.rem(me + o, n)
        slot = other if back else me
        return remote(tile, tiles_ref.at[slot], tile_send.at[o], tile_recv.at[slot], dp, other)

    def vec_near():
        return pltpu.make_async_copy(tile, tiles_ref.at[me], tile_near)

    def save(j):
        return pltpu.make_async_copy(w_ref.at[j], w_qkv.at[:, :, d * j : d * j + d], save_sem.at[j])

    @pl.when(i == 0)
    def _():
        tile[...] = vector_tile((v0, v1, v2, v3, v4, v5), each)
        greet()
        vec_near().start()
        others(n, lambda o: vec_copy(o).start())
        for job in jobs[:3]:
            job.start_wide()

    @pl.when(i < steps)
    def _():
        xhat, _ = normed(x[...].astype(F32))

        @pl.when(i == 0)
        def _():
            vec_near().wait()
            others(n, lambda o: vec_copy(o).wait_send())
            others(n, lambda o: vec_copy(o, True).wait_recv())
            spread_vectors(tiles_ref, vec_out, each)
            for job in jobs[:3]:
                job.finish_wide()
                job.start_y()
            for job in jobs[3:]:
                job.start_wide()
            for job in jobs[:3]:
                job.finish_y()
                job.start_core()
            jobs[0].finish_core()

        h1 = (xhat * vec_out[0:1, :] + vec_out[1:2, :]).astype(BF16)
        at = pl.ds(pl.multiple_of(i * rows, rows), rows)

        def weights(j):
            return w_ref[j].reshape(d, d)

        q = feature(nn(h1, weights(0))).astype(BF16)
        q_out[...] = q
        q_all[at, :] = q

        @pl.when(i == 0)
        def _():
            jobs[1].finish_core()

        k = feature(nn(h1, weights(1))).astype(BF16)
        k_out[...] = k
        k_all[at, :] = k

        @pl.when(i == 0)
        def _():
            jobs[2].finish_core()
            for j in range(3):
                save(j).start()

        v = nn(h1, weights(2)).astype(BF16)
        v_out[...] = v
        v_all[at, :] = v
        m, t = i // tiles, lax.rem(i, tiles)
        base = off[0]
        final = start_of(lens, m, base + block_rows - 1)
        last = flag(start_of(lens, m, place_rows(base + t * rows, rows)) == final)
        k_last = k * rows_of(last.astype(BF16), d)
        k_turned = k_last.T

        @pl.when(t == 0)
        def _():
            acc[...] = jnp.zeros_like(acc)
            zacc[...] = jnp.zeros_like(zacc)

        for g in range(2):
            acc[g] += nn(k_turned[256 * g : 256 * g + 256, :], v[:, 256 * g : 256 * g + 256])
        zacc[...] += column_sum(k_last.astype(F32))

        @pl.when(t == tiles - 1)
        def _():
            mask = ones[...].astype(F32)
            pack_state([acc[0] * mask, acc[1] * mask], zacc[...], local.at[m])

    @pl.when(i == steps - 1)
    def _():
        running.start1()

    @pl.when(i == steps)
    def _():
        for job in jobs[3:5]:
            job.finish_wide()
            job.start_y()

    @pl.when(i == steps + 1)
    def _():
        running.finish1_start2()
        jobs[5].finish_wide()
        jobs[5].start_y()

    @pl.when(i == steps + 2)
    def _():
        running.finish2_start3()
        for job in jobs[3:5]:
            job.finish_y()
            job.start_core()

    @pl.when(i >= steps)
    def _():
        m = i - steps
        at = pl.ds(pl.multiple_of(m * block_rows, block_rows), block_rows)
        attend(lens, m, off[0], q_all.at[at], k_all.at[at], v_all.at[at], ones, num_out, kc_out, states_out, state, norm)

    @pl.when(i == steps + micro - 1)
    def _():
        jobs[5].finish_y()
        jobs[5].start_core()
        running.finish3()
        state_in[...] = running.result[...]
        for job in jobs[3:]:
            job.finish_core()
        for j in range(3):
            save(j).wait()


def chunk_masks(lens, m, begin, size):
    by_row = start_of(lens, m, place_rows(begin, size))
    lane = begin + lax.broadcasted_iota(jnp.int32, (8, size), 1)
    by_column = start_of(lens, m, lane)[0:1, :]
    final = start_of(lens, m, begin + size - 1)
    return by_row, by_column, final


def pair_mask():
    return flag(lane_half((16, 128))).astype(BF16)[0:1, :]


def split_pair(a, low, high):
    return jnp.concatenate([a * low, a * high], axis=0)


def attend(lens, m, base, q_ref, k_ref, v_ref, ones, num_out, kc_out, states_out, state, norm):
    rows, d = q_ref.shape
    size = CHUNK
    state[...] = jnp.zeros_like(state)
    norm[...] = jnp.zeros_like(norm)
    half = lane_half((1, 128))
    low = flag(half).astype(BF16)
    high = flag(jnp.logical_not(half)).astype(BF16)

    def step(c, carry):
        at = pl.ds(pl.multiple_of(c * size, size), size)
        begin = base + c * size
        q, k, v = q_ref[at, :], k_ref[at, :], v_ref[at, :]
        by_row, by_column, final = chunk_masks(lens, m, begin, size)
        places = lax.broadcasted_iota(jnp.int32, (size, size), 0)
        columns = lax.broadcasted_iota(jnp.int32, (size, size), 1)
        allowed = flag((places >= columns) & (by_row[:, :size] == by_column)).astype(BF16)
        allowed2 = jnp.concatenate([allowed, allowed], axis=1)
        seen = flag(by_row < begin)
        last = flag(by_row == final).astype(BF16)
        keep = jnp.where(final < begin, 1.0, 0.0)
        kc_out[at, :] = (nn(allowed, k) + rows_of(seen, d) * norm[...]).astype(BF16)
        groups = [state[g].astype(BF16) for g in range(2)]
        for g in range(2):
            states_out[c, g] = groups[g]
        q_seen = q * rows_of(seen.astype(BF16), d)
        for p in range(4):
            cut = slice(128 * p, 128 * p + 128)
            s = nt(q[:, cut], split_pair(k[:, cut], low, high)).astype(BF16) * allowed2
            inside = nn(s, split_pair(v[:, cut], low, high))
            g, side = p // 2, 128 * (p % 2)
            before = nn(q_seen[:, 256 * g : 256 * g + 256], groups[g][:, side : side + 128])
            num_out[at, cut] = (inside + before).astype(BF16)
        k_last = k * rows_of(last, d)
        k_turned = k_last.T
        mask = ones[...].astype(F32)
        for g in range(2):
            cut = slice(256 * g, 256 * g + 256)
            state[g] = keep * state[g] + nn(k_turned[cut, :], v[:, cut]) * mask
        norm[...] = keep * norm[...] + column_sum(k_last.astype(F32))
        return carry

    lax.fori_loop(0, rows // size, step, 0)


def middle_kernel(
    lens, off, q_ref, num_ref, kc_ref, x_ref, cot_ref, state_in, ones,
    w_out, vec, w_up, w_down,
    block_out, gm_out, gnum_out, gden_out, use_out, g_out, g_up, g_down, g_bias, g_up_bias,
    groups, norm, use, use_norm, acc_out, acc_up, acc_down, total, e_total, h2_ref, h2t_ref, ct_ref,
):
    m, t, tiles = pl.program_id(0), pl.program_id(1), pl.num_programs(1)
    rows, d = x_ref.shape
    first = (m == 0) & (t == 0)
    final = (m == pl.num_programs(0) - 1) & (t == tiles - 1)
    base = off[0]

    @pl.when(first)
    def _():
        acc_out[...] = jnp.zeros_like(acc_out)
        acc_up[...] = jnp.zeros_like(acc_up)
        acc_down[...] = jnp.zeros_like(acc_down)
        g_bias[...] = jnp.zeros_like(g_bias)
        g_up_bias[...] = jnp.zeros_like(g_up_bias)

    @pl.when(t == 0)
    def _():
        parts, z = unpack_state(state_in[...], ones[...])
        for g in range(2):
            groups[g] = parts[g]
        norm[...] = z
        use[...] = jnp.zeros_like(use)
        use_norm[...] = jnp.zeros_like(use_norm)

    gain, bias, down_bias = vec[2:3, :], vec[3:4, :], vec[4:5, :]
    q = q_ref[...]
    seen = flag(start_of(lens, m, place_rows(base + t * rows, rows)) < base)
    q_seen = q * rows_of(seen.astype(BF16), d)
    num = num_ref[...].astype(F32) + by_group(lambda g, a: nn(a, groups[g]), q_seen)
    kc = kc_ref[...].astype(F32) + rows_of(seen, d) * norm[...]
    den = by_group(lambda g, a: nn(a, ones[...]), (q.astype(F32) * kc).astype(BF16))
    over = 1.0 / den
    mixed = (num * over).astype(BF16)
    middle = x_ref[...].astype(F32) + nn(mixed, w_out[...])
    xhat, scale = normed(middle)
    h2 = (xhat * gain + bias).astype(BF16)
    h2_ref[...] = h2
    h2t_ref[...] = h2.T
    ct_ref[...] = cot_ref[...].T
    total[...] = middle + down_bias
    e_total[...] = jnp.zeros_like(e_total)

    def ffn(f, carry):
        cut = pl.ds(pl.multiple_of(f * FF_TILE, FF_TILE), FF_TILE)
        hidden = nn(h2_ref[...], w_up[:, cut]) + vec[pl.ds(5 + f, 1), :]
        pulled = nt(cot_ref[...], w_down[cut, :])
        square = hidden * hidden
        c0, c1 = 0.7978845608028654, 0.044715
        th = jnp.tanh(hidden * (c0 + (c0 * c1) * square))
        half_up = 0.5 + 0.5 * th
        active = (hidden * half_up).astype(BF16)
        slope = half_up + (0.5 * hidden) * (1.0 - th * th) * (c0 + (3.0 * c0 * c1) * square)
        g_hidden = slope * pulled
        g_low = g_hidden.astype(BF16)
        total[...] += nn(active, w_down[cut, :])
        e_total[...] += nt(g_low, w_up[:, cut])
        acc_down[:, cut] += nn(ct_ref[...], active)
        acc_up[:, cut] += nn(h2t_ref[...], g_low)
        g_up_bias[:, cut] += column_sum(g_hidden)
        return carry

    lax.fori_loop(0, w_up.shape[1] // FF_TILE, ffn, 0)
    block_out[...] = total[...].astype(BF16)
    e = e_total[...]
    cot = cot_ref[...].astype(F32)
    g_middle = cot + norm_back(e, xhat, scale, gain)
    gm_out[...] = g_middle
    g_bias[0:1, :] += column_sum(e * xhat)
    g_bias[1:2, :] += column_sum(e)
    g_bias[2:3, :] += column_sum(cot)
    branch = g_middle.astype(BF16)
    acc_out[...] += nn(mixed.T, branch)
    g_mixed = nt(branch, w_out[...])
    gnum = (g_mixed * over).astype(BF16)
    gnum_out[...] = gnum
    gden = -by_group(lambda g, a: nn(a, ones[...]), (g_mixed * num).astype(BF16)) * (over * over)
    gden_out[...] = gden.astype(BF16)
    turned = q_seen.T
    for g in range(2):
        cut = slice(256 * g, 256 * g + 256)
        use[g] += nn(turned[cut, :], gnum[:, cut])
    use_norm[...] += column_sum(q_seen.astype(F32) * gden)

    @pl.when(t == tiles - 1)
    def _():
        mask = ones[...].astype(F32)
        pack_state([use[0] * mask, use[1] * mask], use_norm[...], use_out)

    @pl.when(final)
    def _():
        g_out[...] = acc_out[...].astype(BF16)
        g_up[...] = acc_up[...].astype(BF16)
        g_down[...] = acc_down[...].astype(BF16)


def attend_back_kernel(
    lens, off, q_ref, k_ref, v_ref, gnum_ref, gden_ref, kc_ref, states, state_in, ones,
    gq_out, dk_out, dv_out, after, after_norm,
):
    m = pl.program_id(0)
    rows, d = q_ref.shape
    size = CHUNK
    count = rows // size
    base = off[0]
    after[...] = jnp.zeros_like(after)
    after_norm[...] = jnp.zeros_like(after_norm)
    half = lane_half((1, 128))
    low = flag(half).astype(BF16)
    high = flag(jnp.logical_not(half)).astype(BF16)
    groups_in, norm_in = unpack_state(state_in[...], ones[...])

    def step(i, carry):
        c = count - 1 - i
        at = pl.ds(pl.multiple_of(c * size, size), size)
        begin = base + c * size
        q, k, v, gnum = q_ref[at, :], k_ref[at, :], v_ref[at, :], gnum_ref[at, :]
        gden = gden_ref[at, :].astype(F32)
        by_row, by_column, final = chunk_masks(lens, m, begin, size)
        places = lax.broadcasted_iota(jnp.int32, (size, size), 0)
        columns = lax.broadcasted_iota(jnp.int32, (size, size), 1)
        same = by_row[:, :size] == by_column
        allowed = flag((places >= columns) & same).astype(BF16)
        allowed2 = jnp.concatenate([allowed, allowed], axis=1)
        turned = flag((places <= columns) & same).astype(BF16)
        turned2 = jnp.concatenate([turned, turned], axis=1)
        seen = rows_of(flag(by_row < begin).astype(BF16), d)
        seen_all = flag(by_row < base)
        last = flag(by_row == final)
        keep = jnp.where(final < begin, 1.0, 0.0)
        last_low = rows_of(last.astype(BF16), d)
        g_after = [after[g].astype(BF16) for g in range(2)]
        gnum_seen = gnum * seen
        gnum_all = gnum * rows_of(seen_all.astype(BF16), d)
        k_last, v_last = k * last_low, v * last_low
        gden_q = gden * q.astype(F32)
        dk_den = nn(turned, gden_q.astype(BF16)) + rows_of(last, d) * after_norm[...]
        dq_den = gden * (kc_ref[at, :].astype(F32) + rows_of(seen_all, d) * norm_in)
        for p in range(4):
            cut = slice(128 * p, 128 * p + 128)
            g, side = p // 2, 128 * (p % 2)
            wide = slice(256 * g, 256 * g + 256)
            edge = slice(side, side + 128)
            qp, kp, vp, gp = q[:, cut], k[:, cut], v[:, cut], gnum[:, cut]
            q2, k2 = split_pair(qp, low, high), split_pair(kp, low, high)
            v2, g2 = split_pair(vp, low, high), split_pair(gp, low, high)
            s_turned = nt(kp, q2).astype(BF16) * turned2
            gs_turned = nt(vp, g2).astype(BF16) * turned2
            gs = nt(gp, v2).astype(BF16) * allowed2
            dq = nn(gs, k2) + nt(gnum_seen[:, wide], states[c, g, edge, :])
            dq = dq + nt(gnum_all[:, wide], groups_in[g][edge, :]) + dq_den[:, cut]
            gq_out[at, cut] = (jnp.minimum(qp.astype(F32), 1.0) * dq).astype(BF16)
            dk = nn(gs_turned, q2) + nt(v_last[:, wide], g_after[g][edge, :]) + dk_den[:, cut]
            dk_out[at, cut] = dk.astype(BF16)
            dv = nn(s_turned, g2) + nn(k_last[:, wide], g_after[g][:, edge])
            dv_out[at, cut] = dv.astype(BF16)
        q_turned = (q * seen).T
        mask = ones[...].astype(F32)
        for g in range(2):
            wide = slice(256 * g, 256 * g + 256)
            after[g] = keep * after[g] + nn(q_turned[wide, :], gnum[:, wide]) * mask
        after_norm[...] = keep * after_norm[...] + column_sum(gden_q * seen.astype(F32))
        return carry

    lax.fori_loop(0, count, step, 0)


def project_back_kernel(
    lens, off, gq_ref, dk_ref, dv_ref, k_ref, v_ref, x_ref, gm_ref, state_grad, ones, vec, w,
    gx_out, g_qkv, g_bias, groups, norm, acc,
):
    m, t, tiles = pl.program_id(0), pl.program_id(1), pl.num_programs(1)
    rows, d = x_ref.shape
    base = off[0]

    @pl.when((m == 0) & (t == 0))
    def _():
        acc[...] = jnp.zeros_like(acc)
        g_bias[...] = jnp.zeros_like(g_bias)

    @pl.when(t == 0)
    def _():
        parts, z = unpack_state(state_grad[...], ones[...])
        for g in range(2):
            groups[g] = parts[g]
        norm[...] = z

    k, v = k_ref[...], v_ref[...]
    final = start_of(lens, m, base + rows * tiles - 1)
    last = flag(start_of(lens, m, place_rows(base + t * rows, rows)) == final)
    last_low = rows_of(last.astype(BF16), d)
    dk = dk_ref[...].astype(F32) + rows_of(last, d) * norm[...]
    dk = dk + by_group(lambda g, a: nt(a, groups[g]), v * last_low)
    gk = (jnp.minimum(k.astype(F32), 1.0) * dk).astype(BF16)
    gv = dv_ref[...].astype(F32) + by_group(lambda g, a: nn(a, groups[g]), k * last_low)
    gv = gv.astype(BF16)
    gq = gq_ref[...]
    gain, bias = vec[0:1, :], vec[1:2, :]
    xhat, scale = normed(x_ref[...].astype(F32))
    h1t = (xhat * gain + bias).astype(BF16).T
    e = jnp.zeros((rows, d), F32)
    for j, part in enumerate((gq, gk, gv)):
        cut = slice(d * j, d * j + d)
        acc[:, cut] += nn(h1t, part)
        e = e + nt(part, w[:, cut])
    gx_out[...] = gm_ref[...] + norm_back(e, xhat, scale, gain)
    g_bias[0:1, :] += column_sum(e * xhat)
    g_bias[1:2, :] += column_sum(e)

    @pl.when((m == pl.num_programs(0) - 1) & (t == tiles - 1))
    def _():
        g_qkv[...] = acc[...].astype(BF16)


def params(count):
    return pltpu.CompilerParams(
        dimension_semantics=("arbitrary",) * count, vmem_limit_bytes=VMEM
    )


def small():
    return pl.BlockSpec(memory_space=pltpu.SMEM)


def per_device(
    block_in, cotangent, ln1_gain, ln1_bias, qkv_weight, out_weight, ln2_gain, ln2_bias,
    up_weight, up_bias, down_weight, down_bias, seq_lengths,
):
    micro, rows, d = block_in.shape[0], block_in.shape[2], block_in.shape[3]
    ff = up_weight.shape[1]
    wide, index = lax.axis_size("wide"), lax.axis_index("wide")
    lens = seq_lengths.reshape(micro, -1)
    off = (index * rows).astype(jnp.int32).reshape(1)
    x = block_in.reshape(micro, rows, d)
    cot = cotangent.reshape(micro, rows, d)

    each = d // wide
    lane = jnp.arange(256) // 64
    ones = (lane[:, None] == lane[None, :]).astype(BF16)

    tiles = rows // TILE
    token = pl.BlockSpec((None, TILE, d), lambda m, t: (m, t, 0))
    whole = lambda shape: pl.BlockSpec(shape, lambda *_: (0,) * len(shape))
    fixed = lambda shape: pl.BlockSpec(
        shape, lambda *_: (0,) * len(shape), pipeline_mode=pl.Buffered(1)
    )
    packed = pl.BlockSpec((None, 272, 128), lambda m, *_: (m, 0, 0))
    like = lambda dtype: jax.ShapeDtypeStruct((micro, rows, d), dtype)
    packed_shape = jax.ShapeDtypeStruct((micro, 272, 128), BF16)

    block = pl.BlockSpec((None, rows, d), lambda m: (m, 0, 0))
    count = rows // CHUNK
    states_spec = pl.BlockSpec((None, count, 2, 256, 256), lambda m: (m, 0, 0, 0, 0))
    steps = micro * tiles
    early = pl.BlockSpec((None, TILE, d), lambda i: (jnp.minimum(i, steps - 1) // tiles, lax.rem(jnp.minimum(i, steps - 1), tiles), 0))
    late = lambda *shape: pl.BlockSpec(
        (None,) + shape, lambda i: (jnp.maximum(i - steps, 0),) + (0,) * len(shape)
    )
    anywhere = pl.BlockSpec(memory_space=pl.ANY)
    spread = lambda a: jax.ShapeDtypeStruct((wide,) + a.shape, BF16)
    dma = pltpu.SemaphoreType.DMA
    vectors = [a.reshape(1, -1) for a in (ln1_gain, ln1_bias, ln2_gain, ln2_bias, down_bias, up_bias)]
    state_shape = (micro, state_rows(), 128)
    (q, k, v, num, kc, states, state_in, w_qkv, w_out, w_up, w_down, vec) = pl.pallas_call(
        first_kernel,
        grid=(steps + micro,),
        in_specs=[small(), small(), early] + [anywhere] * 4 + [whole(a.shape) for a in vectors] + [whole((256, 256))],
        out_specs=[early, early, early, late(rows, d), late(rows, d), late(count, 2, 256, 256), whole(state_shape)]
        + [anywhere] * 4 + [whole((16, d))],
        out_shape=[like(BF16)] * 5 + [
            jax.ShapeDtypeStruct((micro, count, 2, 256, 256), BF16), jax.ShapeDtypeStruct(state_shape, F32),
            spread(qkv_weight), spread(out_weight), spread(up_weight), spread(down_weight),
            jax.ShapeDtypeStruct((16, d), F32),
        ],
        scratch_shapes=[pltpu.VMEM((3, wide, each, d), BF16)]
        + [pltpu.VMEM((micro * rows, d), BF16)] * 3
        + [pltpu.VMEM((2, 256, 256), F32), pltpu.VMEM((1, d), F32)] * 2
        + [
            pltpu.VMEM(state_shape, BF16), pltpu.VMEM((16, 128), BF16), pltpu.VMEM((wide, 16, 128), BF16),
            dma, dma((wide,)), dma((wide,)), dma((3,)),
        ]
        + running_scratch(micro)
        + gather_sems() * 6,
        compiler_params=pltpu.CompilerParams(
            dimension_semantics=("arbitrary",), vmem_limit_bytes=VMEM, collective_id=0, has_side_effects=True
        ),
        name="first",
    )(lens, off, x, qkv_weight, out_weight, up_weight, down_weight, *vectors, ones)
    w_qkv, w_out = w_qkv.reshape(d, 3 * d), w_out.reshape(d, d)
    w_up, w_down = w_up.reshape(d, ff), w_down.reshape(ff, d)

    ends = jnp.cumsum(lens, axis=-1)
    final_places = jnp.arange(1, wide + 1, dtype=jnp.int32) * rows - 1
    finals = jnp.sum(
        jnp.where(ends[:, None, :] <= final_places[None, :, None], lens[:, None, :], 0), axis=-1
    )
    blocks = jnp.arange(wide)
    before = jnp.concatenate([jnp.full((micro, 1), -1, finals.dtype), finals[:, :-1]], axis=1)
    mine = jnp.take(finals, index, axis=1)[:, None]
    reach_up = ((blocks > index)[None] & (before == mine)).astype(F32)

    def combine(part, reach):
        every = lax.all_gather(part, "wide").astype(F32)
        return jnp.einsum("jmrl,mj->mrl", every, reach, precision=lax.Precision.HIGHEST)

    result, g_middle, gnum, gden, use, g_out, g_up, g_down, g_vec, g_up_vec = pl.pallas_call(
        middle_kernel,
        grid=(micro, tiles),
        in_specs=[small(), small()] + [token] * 5 + [packed, whole((256, 256))] + [
            fixed((d, d)), whole((16, d)), fixed((d, ff)), fixed((ff, d)),
        ],
        out_specs=[token, token, token, token, packed, whole((d, d)), whole((d, ff)), whole((d, ff)), whole((8, d)), whole((1, ff))],
        out_shape=[
            like(BF16), like(F32), like(BF16), like(BF16), packed_shape,
            jax.ShapeDtypeStruct((d, d), BF16), jax.ShapeDtypeStruct((d, ff), BF16),
            jax.ShapeDtypeStruct((d, ff), BF16), jax.ShapeDtypeStruct((8, d), F32),
            jax.ShapeDtypeStruct((1, ff), F32),
        ],
        scratch_shapes=[
            pltpu.VMEM((2, 256, 256), BF16), pltpu.VMEM((1, d), F32),
            pltpu.VMEM((2, 256, 256), F32), pltpu.VMEM((1, d), F32),
            pltpu.VMEM((d, d), F32), pltpu.VMEM((d, ff), F32), pltpu.VMEM((d, ff), F32),
            pltpu.VMEM((TILE, d), F32), pltpu.VMEM((TILE, d), F32), pltpu.VMEM((TILE, d), BF16),
            pltpu.VMEM((d, TILE), BF16), pltpu.VMEM((d, TILE), BF16),
        ],
        compiler_params=params(2),
        name="middle",
    )(lens, off, q, num, kc, x, cot, state_in, ones, w_out, vec, w_up, w_down)

    gq, dk, dv = pl.pallas_call(
        attend_back_kernel,
        grid=(micro,),
        in_specs=[small(), small()] + [block] * 6 + [states_spec, pl.BlockSpec((None, 272, 128), lambda m: (m, 0, 0)), whole((256, 256))],
        out_specs=[block] * 3,
        out_shape=[like(BF16)] * 3,
        scratch_shapes=[pltpu.VMEM((2, 256, 256), F32), pltpu.VMEM((1, d), F32)],
        compiler_params=params(1),
        name="attend_back",
    )(lens, off, q, k, v, gnum, gden, kc, states, state_in, ones)
    state_grad = combine(use, reach_up)

    grad_input, g_qkv, g_vec_one = pl.pallas_call(
        project_back_kernel,
        grid=(micro, tiles),
        in_specs=[small(), small()] + [token] * 7 + [packed, whole((256, 256)), whole((16, d)), fixed((d, 3 * d))],
        out_specs=[token, whole((d, 3 * d)), whole((8, d))],
        out_shape=[like(F32), jax.ShapeDtypeStruct((d, 3 * d), BF16), jax.ShapeDtypeStruct((8, d), F32)],
        scratch_shapes=[pltpu.VMEM((2, 256, 256), BF16), pltpu.VMEM((1, d), F32), pltpu.VMEM((d, 3 * d), F32)],
        compiler_params=params(2),
        name="project_back",
    )(lens, off, gq, dk, dv, k, v, x, g_middle, state_grad, ones, vec, w_qkv)

    def shared(grad, axis):
        part = lax.psum_scatter(grad, "wide", scatter_dimension=axis, tiled=True)
        return lax.psum(part, "dp").astype(F32)

    g_all = jnp.concatenate(
        [a.reshape(wide, -1) for a in (g_vec_one[0], g_vec_one[1], g_vec[0], g_vec[1], g_vec[2], g_up_vec[0])], axis=1
    )
    g_all = lax.psum(g_all, ("dp", "wide"))
    g_all = lax.dynamic_index_in_dim(g_all, index, 0, keepdims=False)
    piece = [g_all[each * j : each * j + each] for j in range(5)] + [g_all[5 * each :]]
    return (
        result.reshape(block_in.shape),
        grad_input.reshape(block_in.shape),
        piece[0],
        piece[1],
        shared(g_qkv, 0),
        shared(g_out, 0),
        piece[2],
        piece[3],
        shared(g_up, 0),
        piece[5],
        shared(g_down, 1).T,
        piece[4],
    )


def solution(mesh):
    tokens = P(None, "dp", "wide", None)
    vector, matrix = P("wide"), P("wide", None)
    weights = (vector, vector, matrix, matrix, vector, vector, matrix, vector, matrix, vector)
    return jax.shard_map(
        per_device,
        mesh=mesh,
        in_specs=(tokens, tokens) + weights + (P(None, "dp", None),),
        out_specs=(tokens, tokens) + weights,
        check_vma=False,
    )
```

```python
import functools

import jax
import jax.numpy as jnp
from jax import lax
from jax.experimental import pallas as pl
from jax.experimental.pallas import tpu as pltpu
from jax.sharding import PartitionSpec as P

HEADS = 8
EPSILON = 1e-05
F32 = jnp.float32
BF16 = jnp.bfloat16
CHUNK = 128
TILE = 512
FF_TILE = 512
VMEM = 62 * 1024 * 1024


def nn(a, b):
    return lax.dot_general(a, b, (((1,), (0,)), ((), ())), preferred_element_type=F32)


def nt(a, b):
    return lax.dot_general(a, b, (((1,), (1,)), ((), ())), preferred_element_type=F32)


def rows_of(row, width):
    return jnp.concatenate([row] * (width // 128), axis=1)


def start_of(lens, m, place):
    start, end = jnp.zeros_like(place), 0
    for j in range(lens.shape[1]):
        end = end + lens[m, j]
        start = start + jnp.where(end <= place, lens[m, j], 0)
    return start


def place_rows(first, count):
    return first + lax.broadcasted_iota(jnp.int32, (count, 128), 0)


def flag(condition):
    return jnp.where(condition, 1.0, 0.0)


def normed(x):
    average = jnp.mean(x, axis=-1, keepdims=True)
    centred = x - average
    spread = jnp.mean(centred * centred, axis=-1, keepdims=True)
    scale = lax.rsqrt(spread + EPSILON)
    return centred * scale, scale


def norm_back(e, xhat, scale, gain):
    a = gain * e
    return scale * (
        a - jnp.mean(a, axis=-1, keepdims=True) - xhat * jnp.mean(a * xhat, axis=-1, keepdims=True)
    )


def feature(v):
    return jnp.where(v > 0.0, v + 1.0, jnp.exp(jnp.minimum(v, 0.0)))


def column_sum(a):
    return jnp.sum(a, axis=0, keepdims=True)


def by_group(fn, *arrays):
    return jnp.concatenate(
        [fn(g, *[a[:, 256 * g : 256 * g + 256] for a in arrays]) for g in range(2)], axis=1
    )


def lane_half(shape):
    return lax.broadcasted_iota(jnp.int32, shape, 1) < 64


def pack_state(state, norm, out):
    folded = []
    for s in state:
        y = s[:, :128] + s[:, 128:]
        folded.append(y + pltpu.roll(y, 64, 1))
    out[0:256, :] = jnp.where(lane_half((256, 128)), folded[0], folded[1]).astype(out.dtype)
    row = lax.broadcasted_iota(jnp.int32, (16, 128), 0)
    tail = jnp.zeros((16, 128), F32)
    for j in range(4):
        tail = jnp.where(row == j, norm[:, 128 * j : 128 * j + 128], tail)
    out[256:272, :] = tail.astype(out.dtype)
    if out.shape[0] > 272:
        out[272:, :] = jnp.zeros((out.shape[0] - 272, 128), out.dtype)


def unpack_state(packed, ones):
    z = packed[0:256, :]
    turned = pltpu.roll(z, 64, 1)
    half = lane_half((256, 128))
    groups = []
    for part in (jnp.where(half, z, turned), jnp.where(half, turned, z)):
        groups.append(jnp.concatenate([part, part], axis=1).astype(BF16) * ones)
    tail = packed[256:272, :]
    norm = jnp.concatenate([tail[j : j + 1, :] for j in range(4)], axis=1)
    return groups, norm


MESH = pl.DeviceIdType.MESH


def place():
    dp = lax.axis_index("dp")
    return lax.rem(dp, 2), dp // 2, lax.axis_index("wide"), lax.axis_size("dp") // 2, lax.axis_size("wide")


def others(count, fn):
    def body(o, carry):
        fn(o)
        return carry

    lax.fori_loop(1, count, body, 0)


def remote(src, dst, send, recv, dp, wide):
    return pltpu.make_async_remote_copy(
        src_ref=src, dst_ref=dst, send_sem=send, recv_sem=recv, device_id=(dp, wide), device_id_type=MESH
    )


def greet():
    core, y, me, ny, n = place()
    dp = 2 * y + core
    barrier = pltpu.get_barrier_semaphore()

    def signal(d, w):
        pl.semaphore_signal(barrier, inc=1, device_id=(d, w), device_id_type=MESH)

    others(n, lambda o: signal(dp, lax.rem(me + o, n)))
    others(ny, lambda o: signal(2 * lax.rem(y + o, ny) + core, me))
    signal(2 * y + 1 - core, me)
    pl.semaphore_wait(barrier, n - 1 + ny - 1 + 1)


class Gather:
    def __init__(self, src, dst, sems):
        self.src, self.dst = src, dst
        self.near, self.send, self.recv, self.y_send, self.y_recv, self.c_send, self.c_recv = sems
        self.core, self.y, self.me, self.ny, self.n = place()
        self.dp = 2 * self.y + self.core
        each = src.shape[0]
        self.split = split_of(each)
        part = each // self.split
        if self.split == 1:
            self.rows, self.half = pl.ds(0, each), None
        else:
            at = self.core * (each // 2) + self.y * part
            self.rows = pl.ds(pl.multiple_of(at, part), part)
            self.half = pl.ds(pl.multiple_of(self.core * (each // 2), each // 2), each // 2)

    def own(self):
        return pltpu.make_async_copy(self.src.at[self.rows], self.dst.at[self.me, self.rows], self.near)

    def out(self, o):
        to = lax.rem(self.me + o, self.n)
        return remote(self.src.at[self.rows], self.dst.at[self.me, self.rows], self.send.at[o], self.recv.at[self.me], self.dp, to)

    def back(self, o):
        frm = lax.rem(self.me + o, self.n)
        part = self.dst.at[frm, self.rows]
        return remote(part, part, self.send.at[o], self.recv.at[frm], self.dp, frm)

    def start_wide(self):
        self.own().start()
        others(self.n, lambda o: self.out(o).start())

    def finish_wide(self):
        self.own().wait()
        others(self.n, lambda o: self.out(o).wait_send())
        others(self.n, lambda o: self.back(o).wait_recv())

    def along_y(self, o):
        part = self.dst.at[:, self.rows]
        to = lax.rem(self.y + o, self.ny)
        return remote(part, part, self.y_send.at[o], self.y_recv.at[self.y], 2 * to + self.core, self.me)

    def along_y_back(self, o):
        frm = lax.rem(self.y + o, self.ny)
        each = self.src.shape[0]
        part = each // self.split
        at = self.core * (each // 2) + frm * part
        ref = self.dst.at[:, pl.ds(pl.multiple_of(at, part), part)]
        return remote(ref, ref, self.y_send.at[o], self.y_recv.at[frm], 2 * frm + self.core, self.me)

    def start_y(self):
        if self.split > 1:
            others(self.ny, lambda o: self.along_y(o).start())

    def finish_y(self):
        if self.split > 1:
            others(self.ny, lambda o: self.along_y(o).wait_send())
            others(self.ny, lambda o: self.along_y_back(o).wait_recv())

    def cross(self):
        part = self.dst.at[:, self.half]
        return remote(part, part, self.c_send, self.c_recv, 2 * self.y + 1 - self.core, self.me)

    def cross_back(self):
        each = self.src.shape[0]
        at = (1 - self.core) * (each // 2)
        part = self.dst.at[:, pl.ds(pl.multiple_of(at, each // 2), each // 2)]
        return remote(part, part, self.c_send, self.c_recv, 2 * self.y + 1 - self.core, self.me)

    def start_core(self):
        if self.split > 1:
            self.cross().start()

    def finish_core(self):
        if self.split > 1:
            self.cross().wait_send()
            self.cross_back().wait_recv()


def split_of(each):
    count = lax.axis_size("dp")
    return count if each % (16 * count) == 0 else 1


def gather_sems():
    n, ny = lax.axis_size("wide"), lax.axis_size("dp") // 2
    dma = pltpu.SemaphoreType.DMA
    return [dma, dma((n,)), dma((n,)), dma((ny,)), dma((ny,)), dma, dma]


def packed_shape(rows, d):
    unit = 16 * lax.axis_size("dp")
    columns = d if rows % unit == 0 else 128
    rows = rows * (d // columns)
    return -(-rows // unit) * unit, columns


def put(block, at, piece):
    rows, d = piece.shape
    columns = block.shape[1]
    for b in range(d // columns):
        begin = at * (d // columns) + rows * b
        block[begin : begin + rows, :] = piece[:, columns * b : columns * b + columns]


def fill(block, rows, d):
    used = rows * (d // block.shape[1])
    if block.shape[0] > used:
        block[used:, :] = jnp.zeros((block.shape[0] - used, block.shape[1]), block.dtype)


def get(block, at, rows, d):
    columns = block.shape[1]
    begin = at * (d // columns)
    return jnp.concatenate(
        [block[begin + rows * b : begin + rows * b + rows, :] for b in range(d // columns)], axis=1
    )


class Scatter:
    def __init__(self, src, refs):
        self.src = src
        (self.half, self.got_core, self.got_y, self.got_wide, self.out, self.near, self.c_sem, self.y_send,
         self.y_recv, self.w_send, self.w_recv, self.yb_send, self.yb_recv, self.cb_sem) = refs
        self.core, self.y, self.me, self.ny, self.n = place()
        self.dp = 2 * self.y + self.core
        self.rows = self.out.shape[0]
        self.each = self.rows // (2 * self.ny)
        self.partner = 2 * self.y + 1 - self.core
        self.part = self.got_core.at[:, 0 : self.each]

    def half_rows(self, core):
        return pl.ds(pl.multiple_of(core * (self.rows // 2), self.rows // 2), self.rows // 2)

    def y_rows(self, y):
        return pl.ds(pl.multiple_of(y * self.each, self.each), self.each)

    def own_rows(self, y):
        at = self.core * (self.rows // 2) + y * self.each
        return pl.ds(pl.multiple_of(at, self.each), self.each)

    def load(self):
        return pltpu.make_async_copy(self.src.at[:, self.half_rows(self.core)], self.half, self.near)

    def cross(self):
        return remote(
            self.src.at[:, self.half_rows(1 - self.core)], self.got_core, self.c_sem.at[0], self.c_sem.at[1], self.partner, self.me
        )

    def start1(self):
        self.cross().start()
        self.load().start()

    def along_y(self, o):
        to = lax.rem(self.y + o, self.ny)
        return remote(
            self.half.at[:, self.y_rows(to)], self.got_y.at[o - 1], self.y_send.at[o], self.y_recv.at[o],
            2 * to + self.core, self.me,
        )

    def finish1_start2(self):
        self.load().wait()
        self.cross().wait()

        def add(w, carry):
            self.half[w] = (self.half[w].astype(F32) + self.got_core[w].astype(F32)).astype(BF16)
            return carry

        lax.fori_loop(0, self.n, add, 0)
        others(self.ny, lambda o: self.along_y(o).start())

    def along_wide(self, o):
        to = lax.rem(self.me + o, self.n)
        return remote(self.part.at[to], self.got_wide.at[o - 1], self.w_send.at[o], self.w_recv.at[o], self.dp, to)

    def finish2_start3(self):
        others(self.ny, lambda o: self.along_y(o).wait())

        def add(w, carry):
            total = self.half[w, self.y_rows(self.y)].astype(F32)
            for o in range(self.ny - 1):
                total = total + self.got_y[o, w].astype(F32)
            self.part[w] = total.astype(BF16)
            return carry

        lax.fori_loop(0, self.n, add, 0)
        others(self.n, lambda o: self.along_wide(o).start())

    def back_y(self, o, back=False):
        other = lax.rem(self.y + o, self.ny)
        rows = self.own_rows(other if back else self.y)
        ref = self.out.at[rows]
        return remote(ref, ref, self.yb_send.at[o], self.yb_recv.at[other if back else self.y], 2 * other + self.core, self.me)

    def finish3_start4(self):
        others(self.n, lambda o: self.along_wide(o).wait())
        total = self.part[self.me].astype(F32)
        total = lax.fori_loop(0, self.n - 1, lambda o, t: t + self.got_wide[o].astype(F32), total)
        self.out[self.own_rows(self.y)] = total.astype(BF16)
        others(self.ny, lambda o: self.back_y(o).start())

    def back_core(self, back=False):
        ref = self.out.at[self.half_rows(1 - self.core if back else self.core)]
        return remote(ref, ref, self.cb_sem.at[0], self.cb_sem.at[1], self.partner, self.me)

    def finish4_start5(self):
        others(self.ny, lambda o: self.back_y(o).wait_send())
        others(self.ny, lambda o: self.back_y(o, True).wait_recv())
        self.back_core().start()

    def finish5(self):
        self.back_core().wait_send()
        self.back_core(True).wait_recv()


def scatter_scratch(shape):
    rows, d = shape
    n, dp = lax.axis_size("wide"), lax.axis_size("dp")
    ny, part = dp // 2, rows // dp
    dma = pltpu.SemaphoreType.DMA
    return [
        pltpu.VMEM((n, rows // 2, d), BF16),
        pltpu.VMEM((n, rows // 2, d), BF16),
        pltpu.VMEM((ny - 1, n, part, d), BF16),
        pltpu.VMEM((n - 1, part, d), BF16),
        pltpu.VMEM((rows, d), BF16),
        dma, dma((2,)), dma((ny,)), dma((ny,)), dma((n,)), dma((n,)), dma((ny,)), dma((ny,)), dma((2,)),
    ]


class VectorSum:
    def __init__(self, refs):
        self.tiles, self.got_core, self.got_y, self.got_wide, self.c_sem, self.y_send, self.y_recv, self.w_send, self.w_recv = refs
        self.core, self.y, self.me, self.ny, self.n = place()
        self.dp = 2 * self.y + self.core

    def cross(self):
        return remote(self.tiles, self.got_core, self.c_sem.at[0], self.c_sem.at[1], 2 * self.y + 1 - self.core, self.me)

    def along_y(self, o):
        to = lax.rem(self.y + o, self.ny)
        return remote(self.tiles, self.got_y.at[o - 1], self.y_send.at[o], self.y_recv.at[o], 2 * to + self.core, self.me)

    def along_wide(self, o):
        to = lax.rem(self.me + o, self.n)
        return remote(self.tiles.at[to], self.got_wide.at[o - 1], self.w_send.at[o], self.w_recv.at[o], self.dp, to)

    def start1(self):
        self.cross().start()

    def finish1_start2(self):
        self.cross().wait()
        self.tiles[...] = self.tiles[...] + self.got_core[...]
        others(self.ny, lambda o: self.along_y(o).start())

    def finish2_start3(self):
        others(self.ny, lambda o: self.along_y(o).wait())
        total = self.tiles[...]
        for o in range(self.ny - 1):
            total = total + self.got_y[o]
        self.tiles[...] = total
        others(self.n, lambda o: self.along_wide(o).start())

    def finish3(self):
        others(self.n, lambda o: self.along_wide(o).wait())
        return lax.fori_loop(0, self.n - 1, lambda o, t: t + self.got_wide[o], self.tiles[self.me])


def vector_scratch():
    n, ny = lax.axis_size("wide"), lax.axis_size("dp") // 2
    dma = pltpu.SemaphoreType.DMA
    return [
        pltpu.VMEM((n, 16, 128), F32),
        pltpu.VMEM((n, 16, 128), F32),
        pltpu.VMEM((ny - 1, n, 16, 128), F32),
        pltpu.VMEM((n - 1, 16, 128), F32),
        dma((2,)), dma((ny,)), dma((ny,)), dma((n,)), dma((n,)),
    ]


def owner_tiles(rows, tiles, each):
    n = tiles.shape[0]
    d = each * n
    per = 4 * each
    row = lax.broadcasted_iota(jnp.int32, (16, 128), 0)
    lane = lax.broadcasted_iota(jnp.int32, (16, 128), 1)
    blocks = [rows[:, 128 * j : 128 * j + 128] for j in range(d // 128)]

    def turned(a, by, axis):
        by = by % a.shape[axis]
        return pltpu.roll(a, by, axis) if by else a

    for w in range(n):
        at = each * w
        tile = jnp.where(row < 5, turned(blocks[at // 128], -(at % 128), 1), 0.0)
        for r in range(4):
            at = per * w + each * r
            from_row, begin = 5 + at // d, at % d
            moved = turned(turned(blocks[begin // 128], -(begin % 128), 1), 5 + r - from_row, 0)
            tile = jnp.where(row == 5 + r, moved, tile)
        tiles[w] = jnp.where(lane < each, tile, 0.0)


HIGH = 4


def low_count():
    return lax.axis_size("wide") // HIGH


def state_rows():
    unit = 16 * low_count()
    return -(-272 // unit) * unit


class Running:
    def __init__(self, own, upward, refs):
        self.own, self.upward = own, upward
        (self.slots, self.group, self.high, self.mine, self.spread, self.result, self.near, self.send1, self.recv1,
         self.send2, self.recv2, self.send3, self.recv3) = refs
        _, _, self.me, _, _ = place()
        self.dp = lax.axis_index("dp")
        self.lo = low_count()
        self.h, self.l = self.me // self.lo, lax.rem(self.me, self.lo)
        self.part = state_rows() // self.lo

    def slice(self, l):
        return pl.ds(pl.multiple_of(l * self.part, self.part), self.part)

    def copy1(self, o, back=False):
        other = lax.rem(self.l + o, self.lo)
        slot = other if back else self.l
        return remote(self.own, self.slots.at[slot], self.send1.at[o], self.recv1.at[slot], self.dp, self.h * self.lo + other)

    def near1(self):
        return pltpu.make_async_copy(self.own, self.slots.at[self.l], self.near.at[0])

    def start1(self):
        self.near1().start()
        others(self.lo, lambda o: self.copy1(o).start())

    def before(self, a, b):
        return a < b if self.upward else a > b

    def finish1_start2(self):
        self.near1().wait()
        others(self.lo, lambda o: self.copy1(o).wait_send())
        others(self.lo, lambda o: self.copy1(o, True).wait_recv())
        every = jnp.zeros(self.own.shape, F32)
        inner = every
        for l in range(self.lo):
            part = self.slots[l].astype(F32)
            every = every + part
            inner = inner + jnp.where(self.before(l, self.l), part, 0.0)
        self.group[...] = every.astype(BF16)
        self.result[...] = inner

        def send(o):
            other = lax.rem(self.h + o, HIGH)

            @pl.when(self.before(self.h, other))
            def _():
                self.copy2(o).start()

        others(HIGH, send)

    def copy2(self, o, back=False):
        other = lax.rem(self.h + o, HIGH)
        slot = other if back else self.h
        return remote(
            self.group.at[:, self.slice(self.l)], self.high.at[slot], self.send2.at[o], self.recv2.at[slot],
            self.dp, other * self.lo + self.l,
        )

    def finish2_start3(self):
        def wait(o):
            other = lax.rem(self.h + o, HIGH)

            @pl.when(self.before(self.h, other))
            def _():
                self.copy2(o).wait_send()

            @pl.when(self.before(other, self.h))
            def _():
                self.copy2(o, True).wait_recv()

        others(HIGH, wait)
        total = jnp.zeros(self.mine.shape, F32)
        for h in range(HIGH):
            total = total + jnp.where(self.before(h, self.h), self.high[h].astype(F32), 0.0)
        self.mine[...] = total.astype(BF16)
        self.near3().start()
        others(self.lo, lambda o: self.copy3(o).start())

    def near3(self):
        return pltpu.make_async_copy(self.mine, self.spread.at[self.l], self.near.at[1])

    def copy3(self, o, back=False):
        other = lax.rem(self.l + o, self.lo)
        slot = other if back else self.l
        return remote(self.mine, self.spread.at[slot], self.send3.at[o], self.recv3.at[slot], self.dp, self.h * self.lo + other)

    def finish3(self):
        self.near3().wait()
        others(self.lo, lambda o: self.copy3(o).wait_send())
        others(self.lo, lambda o: self.copy3(o, True).wait_recv())
        for l in range(self.lo):
            rows = slice(l * self.part, (l + 1) * self.part)
            self.result[:, rows] = self.result[:, rows] + self.spread[l].astype(F32)


def running_scratch(micro):
    lo, rows = low_count(), state_rows()
    dma = pltpu.SemaphoreType.DMA
    return [
        pltpu.VMEM((lo, micro, rows, 128), BF16),
        pltpu.VMEM((micro, rows, 128), BF16),
        pltpu.VMEM((HIGH, micro, rows // lo, 128), BF16),
        pltpu.VMEM((micro, rows // lo, 128), BF16),
        pltpu.VMEM((lo, micro, rows // lo, 128), BF16),
        pltpu.VMEM((micro, rows, 128), F32),
        dma((2,)), dma((lo,)), dma((lo,)), dma((HIGH,)), dma((HIGH,)), dma((lo,)), dma((lo,)),
    ]


def vector_tile(vectors, each):
    row = lax.broadcasted_iota(jnp.int32, (16, 128), 0)

    def padded(piece):
        return jnp.concatenate([piece.astype(F32), jnp.zeros((1, 128 - each), F32)], axis=1)

    pieces = [padded(v[...]) for v in vectors[:5]]
    hidden = vectors[5][...]
    pieces += [padded(hidden[:, each * r : each * r + each]) for r in range(hidden.shape[1] // each)]
    tile = jnp.zeros((16, 128), F32)
    for j, piece in enumerate(pieces):
        tile = jnp.where(row == j, piece, tile)
    return tile.astype(BF16)


def spread_vectors(slots, out, each):
    n = slots.shape[0]
    d = each * n
    per = 4 * each
    row = lax.broadcasted_iota(jnp.int32, (16, 128), 0)
    blocks = [jnp.zeros((16, 128), F32) for _ in range(d // 128)]
    for w in range(n):
        tile = slots[w].astype(F32)
        at = each * w
        moved = pltpu.roll(tile, at % 128, 1) if at % 128 else tile
        blocks[at // 128] = blocks[at // 128] + jnp.where(row < 5, moved, 0.0)
        for r in range(4):
            at = per * w + each * r
            to_row, lane = 5 + at // d, at % d
            only = jnp.where(row == 5 + r, tile, 0.0)
            moved = pltpu.roll(only, lane % 128, 1) if lane % 128 else only
            if to_row != 5 + r:
                moved = pltpu.roll(moved, (to_row - 5 - r) % 16, 0)
            blocks[lane // 128] = blocks[lane // 128] + moved
    for j, block in enumerate(blocks):
        out[:, 128 * j : 128 * j + 128] = block


def first_kernel(
    lens, off, x, *refs
):
    (s_qkv, s_out, s_up, s_down, v0, v1, v2, v3, v4, v5, ones,
     q_out, k_out, v_out, num_out, kc_out, states_out, state_in, w_qkv, w_out, w_up, w_down, vec_out,
     w_ref, q_all, k_all, v_all, acc, zacc, state, norm, local, tile, tiles_ref, tile_near, tile_send, tile_recv,
     save_sem, *rest) = refs
    each = s_qkv.shape[0]
    running_refs, rest = rest[:13], rest[13:]
    jobs = []
    d = x.shape[1]
    for j in range(3):
        jobs.append(Gather(s_qkv.at[:, d * j : d * j + d], w_ref.at[j], rest[7 * j : 7 * j + 7]))
    for j, (src, dst) in enumerate(((s_out, w_out), (s_up, w_up), (s_down, w_down))):
        jobs.append(Gather(src, dst, rest[21 + 7 * j : 28 + 7 * j]))
    running = Running(local, True, running_refs)
    rows = x.shape[0]
    micro = local.shape[0]
    block_rows = num_out.shape[0]
    tiles = block_rows // rows
    steps = micro * tiles
    i = pl.program_id(0)
    core, y, me, ny, n = place()
    dp = 2 * y + core

    def vec_copy(o, back=False):
        other = lax.rem(me + o, n)
        slot = other if back else me
        return remote(tile, tiles_ref.at[slot], tile_send.at[o], tile_recv.at[slot], dp, other)

    def vec_near():
        return pltpu.make_async_copy(tile, tiles_ref.at[me], tile_near)

    def save(j):
        return pltpu.make_async_copy(w_ref.at[j], w_qkv.at[:, :, d * j : d * j + d], save_sem.at[j])

    @pl.when(i == 0)
    def _():
        tile[...] = vector_tile((v0, v1, v2, v3, v4, v5), each)
        greet()
        vec_near().start()
        others(n, lambda o: vec_copy(o).start())
        for job in jobs[:3]:
            job.start_wide()

    @pl.when(i < steps)
    def _():
        xhat, _ = normed(x[...].astype(F32))

        @pl.when(i == 0)
        def _():
            vec_near().wait()
            others(n, lambda o: vec_copy(o).wait_send())
            others(n, lambda o: vec_copy(o, True).wait_recv())
            spread_vectors(tiles_ref, vec_out, each)
            for job in jobs[:3]:
                job.finish_wide()
                job.start_y()
            for job in jobs[3:]:
                job.start_wide()
            for job in jobs[:3]:
                job.finish_y()
                job.start_core()
            jobs[0].finish_core()

        h1 = (xhat * vec_out[0:1, :] + vec_out[1:2, :]).astype(BF16)
        at = pl.ds(pl.multiple_of(i * rows, rows), rows)

        def weights(j):
            return w_ref[j].reshape(d, d)

        q = feature(nn(h1, weights(0))).astype(BF16)
        q_out[...] = q
        q_all[at, :] = q

        @pl.when(i == 0)
        def _():
            jobs[1].finish_core()

        k = feature(nn(h1, weights(1))).astype(BF16)
        k_out[...] = k
        k_all[at, :] = k

        @pl.when(i == 0)
        def _():
            jobs[2].finish_core()
            for j in range(3):
                save(j).start()

        v = nn(h1, weights(2)).astype(BF16)
        v_out[...] = v
        v_all[at, :] = v
        m, t = i // tiles, lax.rem(i, tiles)
        base = off[0]
        final = start_of(lens, m, base + block_rows - 1)
        last = flag(start_of(lens, m, place_rows(base + t * rows, rows)) == final)
        k_last = k * rows_of(last.astype(BF16), d)
        k_turned = k_last.T

        @pl.when(t == 0)
        def _():
            acc[...] = jnp.zeros_like(acc)
            zacc[...] = jnp.zeros_like(zacc)

        for g in range(2):
            acc[g] += nn(k_turned[256 * g : 256 * g + 256, :], v[:, 256 * g : 256 * g + 256])
        zacc[...] += column_sum(k_last.astype(F32))

        @pl.when(t == tiles - 1)
        def _():
            mask = ones[...].astype(F32)
            pack_state([acc[0] * mask, acc[1] * mask], zacc[...], local.at[m])

    @pl.when(i == steps - 1)
    def _():
        running.start1()

    @pl.when(i == steps)
    def _():
        for job in jobs[3:5]:
            job.finish_wide()
            job.start_y()

    @pl.when(i == steps + 1)
    def _():
        running.finish1_start2()
        jobs[5].finish_wide()
        jobs[5].start_y()

    @pl.when(i == steps + 2)
    def _():
        running.finish2_start3()
        for job in jobs[3:5]:
            job.finish_y()
            job.start_core()

    @pl.when(i >= steps)
    def _():
        m = i - steps
        at = pl.ds(pl.multiple_of(m * block_rows, block_rows), block_rows)
        attend(lens, m, off[0], q_all.at[at], k_all.at[at], v_all.at[at], ones, num_out, kc_out, states_out, state, norm)

    @pl.when(i == steps + micro - 1)
    def _():
        jobs[5].finish_y()
        jobs[5].start_core()
        running.finish3()
        state_in[...] = running.result[...]
        for job in jobs[3:]:
            job.finish_core()
        for j in range(3):
            save(j).wait()


def chunk_masks(lens, m, begin, size):
    by_row = start_of(lens, m, place_rows(begin, size))
    lane = begin + lax.broadcasted_iota(jnp.int32, (8, size), 1)
    by_column = start_of(lens, m, lane)[0:1, :]
    final = start_of(lens, m, begin + size - 1)
    return by_row, by_column, final


def pair_mask():
    return flag(lane_half((16, 128))).astype(BF16)[0:1, :]


def split_pair(a, low, high):
    return jnp.concatenate([a * low, a * high], axis=0)


def attend(lens, m, base, q_ref, k_ref, v_ref, ones, num_out, kc_out, states_out, state, norm):
    rows, d = q_ref.shape
    size = CHUNK
    state[...] = jnp.zeros_like(state)
    norm[...] = jnp.zeros_like(norm)
    half = lane_half((1, 128))
    low = flag(half).astype(BF16)
    high = flag(jnp.logical_not(half)).astype(BF16)

    def step(c, carry):
        at = pl.ds(pl.multiple_of(c * size, size), size)
        begin = base + c * size
        q, k, v = q_ref[at, :], k_ref[at, :], v_ref[at, :]
        by_row, by_column, final = chunk_masks(lens, m, begin, size)
        places = lax.broadcasted_iota(jnp.int32, (size, size), 0)
        columns = lax.broadcasted_iota(jnp.int32, (size, size), 1)
        allowed = flag((places >= columns) & (by_row[:, :size] == by_column)).astype(BF16)
        allowed2 = jnp.concatenate([allowed, allowed], axis=1)
        seen = flag(by_row < begin)
        last = flag(by_row == final).astype(BF16)
        keep = jnp.where(final < begin, 1.0, 0.0)
        kc_out[at, :] = (nn(allowed, k) + rows_of(seen, d) * norm[...]).astype(BF16)
        groups = [state[g].astype(BF16) for g in range(2)]
        for g in range(2):
            states_out[c, g] = groups[g]
        q_seen = q * rows_of(seen.astype(BF16), d)
        for p in range(4):
            cut = slice(128 * p, 128 * p + 128)
            s = nt(q[:, cut], split_pair(k[:, cut], low, high)).astype(BF16) * allowed2
            inside = nn(s, split_pair(v[:, cut], low, high))
            g, side = p // 2, 128 * (p % 2)
            before = nn(q_seen[:, 256 * g : 256 * g + 256], groups[g][:, side : side + 128])
            num_out[at, cut] = (inside + before).astype(BF16)
        k_last = k * rows_of(last, d)
        k_turned = k_last.T
        mask = ones[...].astype(F32)
        for g in range(2):
            cut = slice(256 * g, 256 * g + 256)
            state[g] = keep * state[g] + nn(k_turned[cut, :], v[:, cut]) * mask
        norm[...] = keep * norm[...] + column_sum(k_last.astype(F32))
        return carry

    lax.fori_loop(0, rows // size, step, 0)


def middle_kernel(
    lens, off, q_ref, num_ref, kc_ref, x_ref, cot_ref, state_in, ones,
    w_out, vec, w_up, w_down,
    block_out, gm_out, gnum_out, gden_out, use_out, grads, g_vec,
    groups, norm, use, use_norm, acc_out, acc_up, acc_down, total, e_total, h2_ref, h2t_ref, ct_ref,
):
    m, t, tiles = pl.program_id(0), pl.program_id(1), pl.num_programs(1)
    rows, d = x_ref.shape
    first = (m == 0) & (t == 0)
    final = (m == pl.num_programs(0) - 1) & (t == tiles - 1)
    base = off[0]

    @pl.when(first)
    def _():
        acc_out[...] = jnp.zeros_like(acc_out)
        acc_up[...] = jnp.zeros_like(acc_up)
        acc_down[...] = jnp.zeros_like(acc_down)
        g_vec[...] = jnp.zeros_like(g_vec)

    @pl.when(t == 0)
    def _():
        parts, z = unpack_state(state_in[...], ones[...])
        for g in range(2):
            groups[g] = parts[g]
        norm[...] = z
        use[...] = jnp.zeros_like(use)
        use_norm[...] = jnp.zeros_like(use_norm)

    gain, bias, down_bias = vec[2:3, :], vec[3:4, :], vec[4:5, :]
    q = q_ref[...]
    seen = flag(start_of(lens, m, place_rows(base + t * rows, rows)) < base)
    q_seen = q * rows_of(seen.astype(BF16), d)
    num = num_ref[...].astype(F32) + by_group(lambda g, a: nn(a, groups[g]), q_seen)
    kc = kc_ref[...].astype(F32) + rows_of(seen, d) * norm[...]
    den = by_group(lambda g, a: nn(a, ones[...]), (q.astype(F32) * kc).astype(BF16))
    over = 1.0 / den
    mixed = (num * over).astype(BF16)
    middle = x_ref[...].astype(F32) + nn(mixed, w_out[...])
    xhat, scale = normed(middle)
    h2 = (xhat * gain + bias).astype(BF16)
    h2_ref[...] = h2
    h2t_ref[...] = h2.T
    ct_ref[...] = cot_ref[...].T
    total[...] = middle + down_bias
    e_total[...] = jnp.zeros_like(e_total)

    def ffn(f, carry):
        cut = pl.ds(pl.multiple_of(f * FF_TILE, FF_TILE), FF_TILE)
        hidden = nn(h2_ref[...], w_up[:, cut]) + vec[pl.ds(5 + f, 1), :]
        pulled = nt(cot_ref[...], w_down[cut, :])
        square = hidden * hidden
        c0, c1 = 0.7978845608028654, 0.044715
        th = jnp.tanh(hidden * (c0 + (c0 * c1) * square))
        half_up = 0.5 + 0.5 * th
        active = (hidden * half_up).astype(BF16)
        slope = half_up + (0.5 * hidden) * (1.0 - th * th) * (c0 + (3.0 * c0 * c1) * square)
        g_hidden = slope * pulled
        g_low = g_hidden.astype(BF16)
        total[...] += nn(active, w_down[cut, :])
        e_total[...] += nt(g_low, w_up[:, cut])
        acc_down[:, cut] += nn(ct_ref[...], active)
        acc_up[:, cut] += nn(h2t_ref[...], g_low)
        g_vec[pl.ds(5 + f, 1), :] += column_sum(g_hidden)
        return carry

    lax.fori_loop(0, w_up.shape[1] // FF_TILE, ffn, 0)
    block_out[...] = total[...].astype(BF16)
    e = e_total[...]
    cot = cot_ref[...].astype(F32)
    g_middle = cot + norm_back(e, xhat, scale, gain)
    gm_out[...] = g_middle.astype(BF16)
    g_vec[2:3, :] += column_sum(e * xhat)
    g_vec[3:4, :] += column_sum(e)
    g_vec[4:5, :] += column_sum(cot)
    branch = g_middle.astype(BF16)
    acc_out[...] += nn(mixed.T, branch)
    g_mixed = nt(branch, w_out[...])
    gnum = (g_mixed * over).astype(BF16)
    gnum_out[...] = gnum
    gden = -by_group(lambda g, a: nn(a, ones[...]), (g_mixed * num).astype(BF16)) * (over * over)
    gden_out[...] = gden.astype(BF16)
    turned = q_seen.T
    for g in range(2):
        cut = slice(256 * g, 256 * g + 256)
        use[g] += nn(turned[cut, :], gnum[:, cut])
    use_norm[...] += column_sum(q_seen.astype(F32) * gden)

    @pl.when(t == tiles - 1)
    def _():
        mask = ones[...].astype(F32)
        pack_state([use[0] * mask, use[1] * mask], use_norm[...], use_out)

    @pl.when(final)
    def _():
        n = grads.shape[0]
        each = d // n
        down = acc_down[...].astype(BF16).T
        for w in range(n):
            at = slice(each * w, each * w + each)
            block = grads.at[w]
            for j in range(4):
                put(block, each * j, acc_up[at, d * j : d * j + d].astype(BF16))
            put(block, 4 * each, acc_out[at, :].astype(BF16))
            put(block, 5 * each, down[4 * each * w : 4 * each * w + 4 * each, :])
            fill(block, 9 * each, d)


def attend_back(
    lens, m, base, q_ref, k_ref, v_ref, gnum_ref, gden_ref, kc_ref, states, state_in, ones,
    gq_out, dk_out, dv_out, after, after_norm,
):
    rows, d = q_ref.shape
    size = CHUNK
    count = rows // size
    after[...] = jnp.zeros_like(after)
    after_norm[...] = jnp.zeros_like(after_norm)
    half = lane_half((1, 128))
    low = flag(half).astype(BF16)
    high = flag(jnp.logical_not(half)).astype(BF16)
    groups_in, norm_in = unpack_state(state_in[...], ones[...])

    def step(i, carry):
        c = count - 1 - i
        at = pl.ds(pl.multiple_of(c * size, size), size)
        begin = base + c * size
        q, k, v, gnum = q_ref[at, :], k_ref[at, :], v_ref[at, :], gnum_ref[at, :]
        gden = gden_ref[at, :].astype(F32)
        by_row, by_column, final = chunk_masks(lens, m, begin, size)
        places = lax.broadcasted_iota(jnp.int32, (size, size), 0)
        columns = lax.broadcasted_iota(jnp.int32, (size, size), 1)
        same = by_row[:, :size] == by_column
        allowed = flag((places >= columns) & same).astype(BF16)
        allowed2 = jnp.concatenate([allowed, allowed], axis=1)
        turned = flag((places <= columns) & same).astype(BF16)
        turned2 = jnp.concatenate([turned, turned], axis=1)
        seen = rows_of(flag(by_row < begin).astype(BF16), d)
        seen_all = flag(by_row < base)
        last = flag(by_row == final)
        keep = jnp.where(final < begin, 1.0, 0.0)
        last_low = rows_of(last.astype(BF16), d)
        g_after = [after[g].astype(BF16) for g in range(2)]
        gnum_seen = gnum * seen
        gnum_all = gnum * rows_of(seen_all.astype(BF16), d)
        k_last, v_last = k * last_low, v * last_low
        gden_q = gden * q.astype(F32)
        dk_den = nn(turned, gden_q.astype(BF16)) + rows_of(last, d) * after_norm[...]
        dq_den = gden * (kc_ref[at, :].astype(F32) + rows_of(seen_all, d) * norm_in)
        for p in range(4):
            cut = slice(128 * p, 128 * p + 128)
            g, side = p // 2, 128 * (p % 2)
            wide = slice(256 * g, 256 * g + 256)
            edge = slice(side, side + 128)
            qp, kp, vp, gp = q[:, cut], k[:, cut], v[:, cut], gnum[:, cut]
            q2, k2 = split_pair(qp, low, high), split_pair(kp, low, high)
            v2, g2 = split_pair(vp, low, high), split_pair(gp, low, high)
            s_turned = nt(kp, q2).astype(BF16) * turned2
            gs_turned = nt(vp, g2).astype(BF16) * turned2
            gs = nt(gp, v2).astype(BF16) * allowed2
            dq = nn(gs, k2) + nt(gnum_seen[:, wide], states[c, g, edge, :])
            dq = dq + nt(gnum_all[:, wide], groups_in[g][edge, :]) + dq_den[:, cut]
            gq_out[at, cut] = (jnp.minimum(qp.astype(F32), 1.0) * dq).astype(BF16)
            dk = nn(gs_turned, q2) + nt(v_last[:, wide], g_after[g][edge, :]) + dk_den[:, cut]
            dk_out[at, cut] = dk.astype(BF16)
            dv = nn(s_turned, g2) + nn(k_last[:, wide], g_after[g][:, edge])
            dv_out[at, cut] = dv.astype(BF16)
        q_turned = (q * seen).T
        mask = ones[...].astype(F32)
        for g in range(2):
            wide = slice(256 * g, 256 * g + 256)
            after[g] = keep * after[g] + nn(q_turned[wide, :], gnum[:, wide]) * mask
        after_norm[...] = keep * after_norm[...] + column_sum(gden_q * seen.astype(F32))
        return carry

    lax.fori_loop(0, count, step, 0)


def last_kernel(lens, off, *refs):
    (q_ref, k_ref, v_ref, gnum_ref, gden_ref, kc_ref, states, state_in, k_tile, v_tile, x_ref, use, grads, g_vec,
     ones, vec, w,
     gx_out, early_out, later_out, latest_out, vector_out,
     gq_all, dk_all, dv_all, h1t_all, acc, after, after_norm, groups, norm, sums, src_kv, src_q, *rest) = refs
    micro = use.shape[0]
    block_rows, d = q_ref.shape
    rows = x_ref.shape[0]
    tiles = block_rows // rows
    steps = micro * tiles
    n = src_q.shape[0]
    each = d // n
    running = Running(use, False, rest[:13])
    rest = rest[13:]
    early, later, latest = Scatter(grads, rest[:14]), Scatter(src_kv, rest[14:28]), Scatter(src_q, rest[28:42])
    vector = VectorSum(rest[42:])
    i = pl.program_id(0)
    base = off[0]
    p1, p2, p3, end = micro, micro + steps, micro + steps + 1, micro + 2 * steps + 1

    @pl.when(i == 0)
    def _():
        greet()
        running.start1()
        early.start1()
        acc[...] = jnp.zeros_like(acc)
        sums[...] = g_vec[...]

    @pl.when(i == 1)
    def _():
        running.finish1_start2()
        early.finish1_start2()

    @pl.when(i == 2)
    def _():
        running.finish2_start3()

    @pl.when(i == 3)
    def _():
        running.finish3()
        early.finish2_start3()

    @pl.when(i < p1)
    def _():
        at = pl.ds(pl.multiple_of(i * block_rows, block_rows), block_rows)
        attend_back(
            lens, i, base, q_ref, k_ref, v_ref, gnum_ref, gden_ref, kc_ref, states, state_in, ones,
            gq_all.at[at], dk_all.at[at], dv_all.at[at], after, after_norm,
        )

    @pl.when(i == p1 + steps // 2)
    def _():
        early.finish3_start4()

    @pl.when(i == p1 + steps - 2)
    def _():
        early.finish4_start5()

    @pl.when((i >= p1) & (i < p2))
    def _():
        j = i - p1
        m, t = j // tiles, lax.rem(j, tiles)

        @pl.when(t == 0)
        def _():
            parts, z = unpack_state(running.result[m], ones[...])
            for g in range(2):
                groups[g] = parts[g]
            norm[...] = z

        at = pl.ds(pl.multiple_of(j * rows, rows), rows)
        k, v = k_tile[...], v_tile[...]
        final = start_of(lens, m, base + block_rows - 1)
        last = flag(start_of(lens, m, place_rows(base + t * rows, rows)) == final)
        last_low = rows_of(last.astype(BF16), d)
        dk = dk_all[at, :].astype(F32) + rows_of(last, d) * norm[...]
        dk = dk + by_group(lambda g, a: nt(a, groups[g]), v * last_low)
        gk = (jnp.minimum(k.astype(F32), 1.0) * dk).astype(BF16)
        dk_all[at, :] = gk
        gv = dv_all[at, :].astype(F32) + by_group(lambda g, a: nn(a, groups[g]), k * last_low)
        gv = gv.astype(BF16)
        dv_all[at, :] = gv
        xhat, _ = normed(x_ref[...].astype(F32))
        h1t = (xhat * vec[0:1, :] + vec[1:2, :]).astype(BF16).T
        h1t_all[:, at] = h1t
        acc[:, d : 2 * d] += nn(h1t, gk)
        acc[:, 2 * d :] += nn(h1t, gv)

    def arrange(src, parts):
        for w_ in range(n):
            for j, p in enumerate(parts):
                put(src.at[w_], each * j, acc[each * w_ : each * w_ + each, d * p : d * p + d].astype(BF16))
            fill(src.at[w_], each * len(parts), d)

    @pl.when(i == p2 - 1)
    def _():
        arrange(src_kv, (1, 2))
        later.start1()

    @pl.when(i == p2)
    def _():
        early.finish5()
        early_out[...] = early.out[...]

        def add(m, carry):
            at = pl.ds(pl.multiple_of(m * block_rows, block_rows), block_rows)
            acc[:, 0:d] += nn(h1t_all[:, at], gq_all[at, :])
            return carry

        lax.fori_loop(0, micro, add, 0)
        arrange(src_q, (0,))
        later.finish1_start2()
        latest.start1()

    @pl.when(i == p3 + 1)
    def _():
        latest.finish1_start2()

    @pl.when(i == p3 + 3)
    def _():
        later.finish2_start3()

    @pl.when(i == p3 + 5)
    def _():
        latest.finish2_start3()

    @pl.when(i == end - 1)
    def _():
        later.finish3_start4()

    @pl.when(i >= p3)
    def _():
        at = pl.ds(pl.multiple_of((i - p3) * rows, rows), rows)
        e = nt(gq_all[at, :], w[:, 0:d]) + nt(dk_all[at, :], w[:, d : 2 * d]) + nt(dv_all[at, :], w[:, 2 * d :])
        xhat, scale = normed(x_ref[...].astype(F32))
        gx_out[...] = norm_back(e, xhat, scale, vec[0:1, :]).astype(BF16)
        sums[0:1, :] += column_sum(e * xhat)
        sums[1:2, :] += column_sum(e)

    @pl.when(i == end - 1)
    def _():
        owner_tiles(sums[...], vector.tiles, each)
        vector.start1()
        latest.finish3_start4()
        vector.finish1_start2()
        later.finish4_start5()
        latest.finish4_start5()
        vector.finish2_start3()
        later.finish5()
        latest.finish5()
        later_out[...] = later.out[...]
        latest_out[...] = latest.out[...]
        vector_out[...] = vector.finish3()


def result_kernel(
    gm_ref, part_ref, early, later, latest, vector, gx, g_qkv, g_out, g_up, g_down, v0, v1, v2, v3, v4, v5
):
    gx[...] = gm_ref[...].astype(F32) + part_ref[...].astype(F32)

    @pl.when((pl.program_id(0) == 0) & (pl.program_id(1) == 0))
    def _():
        each, d = g_out.shape
        for j in range(4):
            g_up[:, d * j : d * j + d] = get(early, each * j, each, d).astype(F32)
        g_out[...] = get(early, 4 * each, each, d).astype(F32)
        g_down[...] = get(early, 5 * each, 4 * each, d).astype(F32)
        g_qkv[:, 0:d] = get(latest, 0, each, d).astype(F32)
        g_qkv[:, d : 2 * d] = get(later, 0, each, d).astype(F32)
        g_qkv[:, 2 * d :] = get(later, each, each, d).astype(F32)
        for j, v in enumerate((v0, v1, v2, v3, v4)):
            v[...] = vector[j : j + 1, :each]
        for r in range(4):
            v5[:, each * r : each * r + each] = vector[5 + r : 6 + r, :each]


def params(count):
    return pltpu.CompilerParams(
        dimension_semantics=("arbitrary",) * count, vmem_limit_bytes=VMEM
    )


def small():
    return pl.BlockSpec(memory_space=pltpu.SMEM)


def per_device(
    block_in, cotangent, ln1_gain, ln1_bias, qkv_weight, out_weight, ln2_gain, ln2_bias,
    up_weight, up_bias, down_weight, down_bias, seq_lengths,
):
    micro, rows, d = block_in.shape[0], block_in.shape[2], block_in.shape[3]
    ff = up_weight.shape[1]
    wide, index = lax.axis_size("wide"), lax.axis_index("wide")
    lens = seq_lengths.reshape(micro, -1)
    off = (index * rows).astype(jnp.int32).reshape(1)
    x = block_in.reshape(micro, rows, d)
    cot = cotangent.reshape(micro, rows, d)

    each = d // wide
    lane = jnp.arange(256) // 64
    ones = (lane[:, None] == lane[None, :]).astype(BF16)

    tiles = rows // TILE
    token = pl.BlockSpec((None, TILE, d), lambda m, t: (m, t, 0))
    whole = lambda shape: pl.BlockSpec(shape, lambda *_: (0,) * len(shape))
    fixed = lambda shape: pl.BlockSpec(
        shape, lambda *_: (0,) * len(shape), pipeline_mode=pl.Buffered(1)
    )
    packed = pl.BlockSpec((None, state_rows(), 128), lambda m, *_: (m, 0, 0))
    like = lambda dtype: jax.ShapeDtypeStruct((micro, rows, d), dtype)
    early_shape = packed_shape(9 * each, d)

    block = pl.BlockSpec((None, rows, d), lambda m: (m, 0, 0))
    count = rows // CHUNK
    states_spec = pl.BlockSpec((None, count, 2, 256, 256), lambda m: (m, 0, 0, 0, 0))
    steps = micro * tiles
    early = pl.BlockSpec((None, TILE, d), lambda i: (jnp.minimum(i, steps - 1) // tiles, lax.rem(jnp.minimum(i, steps - 1), tiles), 0))
    late = lambda *shape: pl.BlockSpec(
        (None,) + shape, lambda i: (jnp.maximum(i - steps, 0),) + (0,) * len(shape)
    )
    anywhere = pl.BlockSpec(memory_space=pl.ANY)
    spread = lambda a: jax.ShapeDtypeStruct((wide,) + a.shape, BF16)
    dma = pltpu.SemaphoreType.DMA
    vectors = [a.reshape(1, -1) for a in (ln1_gain, ln1_bias, ln2_gain, ln2_bias, down_bias, up_bias)]
    state_shape = (micro, state_rows(), 128)
    (q, k, v, num, kc, states, state_in, w_qkv, w_out, w_up, w_down, vec) = pl.pallas_call(
        first_kernel,
        grid=(steps + micro,),
        in_specs=[small(), small(), early] + [anywhere] * 4 + [whole(a.shape) for a in vectors] + [whole((256, 256))],
        out_specs=[early, early, early, late(rows, d), late(rows, d), late(count, 2, 256, 256), whole(state_shape)]
        + [anywhere] * 4 + [whole((16, d))],
        out_shape=[like(BF16)] * 5 + [
            jax.ShapeDtypeStruct((micro, count, 2, 256, 256), BF16), jax.ShapeDtypeStruct(state_shape, F32),
            spread(qkv_weight), spread(out_weight), spread(up_weight), spread(down_weight),
            jax.ShapeDtypeStruct((16, d), F32),
        ],
        scratch_shapes=[pltpu.VMEM((3, wide, each, d), BF16)]
        + [pltpu.VMEM((micro * rows, d), BF16)] * 3
        + [pltpu.VMEM((2, 256, 256), F32), pltpu.VMEM((1, d), F32)] * 2
        + [
            pltpu.VMEM(state_shape, BF16), pltpu.VMEM((16, 128), BF16), pltpu.VMEM((wide, 16, 128), BF16),
            dma, dma((wide,)), dma((wide,)), dma((3,)),
        ]
        + running_scratch(micro)
        + gather_sems() * 6,
        compiler_params=pltpu.CompilerParams(
            dimension_semantics=("arbitrary",), vmem_limit_bytes=VMEM, collective_id=0, has_side_effects=True
        ),
        name="first",
    )(lens, off, x, qkv_weight, out_weight, up_weight, down_weight, *vectors, ones)
    w_qkv, w_out = w_qkv.reshape(d, 3 * d), w_out.reshape(d, d)
    w_up, w_down = w_up.reshape(d, ff), w_down.reshape(ff, d)

    result, g_middle, gnum, gden, use, grads, g_vec = pl.pallas_call(
        middle_kernel,
        grid=(micro, tiles),
        in_specs=[small(), small()] + [token] * 5 + [packed, whole((256, 256))] + [
            fixed((d, d)), whole((16, d)), fixed((d, ff)), fixed((ff, d)),
        ],
        out_specs=[token, token, token, token, packed, fixed((wide,) + early_shape), whole((16, d))],
        out_shape=[
            like(BF16), like(BF16), like(BF16), like(BF16), jax.ShapeDtypeStruct(state_shape, BF16),
            jax.ShapeDtypeStruct((wide,) + early_shape, BF16), jax.ShapeDtypeStruct((16, d), F32),
        ],
        scratch_shapes=[
            pltpu.VMEM((2, 256, 256), BF16), pltpu.VMEM((1, d), F32),
            pltpu.VMEM((2, 256, 256), F32), pltpu.VMEM((1, d), F32),
            pltpu.VMEM((d, d), F32), pltpu.VMEM((d, ff), F32), pltpu.VMEM((d, ff), F32),
            pltpu.VMEM((TILE, d), F32), pltpu.VMEM((TILE, d), F32), pltpu.VMEM((TILE, d), BF16),
            pltpu.VMEM((d, TILE), BF16), pltpu.VMEM((d, TILE), BF16),
        ],
        compiler_params=params(2),
        name="middle",
    )(lens, off, q, num, kc, x, cot, state_in, ones, w_out, vec, w_up, w_down)

    def first(*shape, buffers=2):
        at = lambda i: (jnp.minimum(i, micro - 1),) + (0,) * len(shape)
        return pl.BlockSpec((None,) + shape, at, pipeline_mode=pl.Buffered(buffers))

    spare = 2 if wide <= 8 else 1

    def walk(*begins):
        def at(i):
            j = 0
            for b in begins:
                j = j + jnp.where(i >= b, jnp.clip(i - b, 0, steps - 1) - j, 0)
            return (j // tiles, lax.rem(j, tiles), 0)

        return pl.BlockSpec((None, TILE, d), at)

    p1, p3 = micro, micro + steps + 1
    kv_shape, q_shape = packed_shape(2 * each, d), packed_shape(each, d)
    vector_shapes = [(1, each)] * 5 + [(1, 4 * each)]
    summed_shapes = [early_shape, kv_shape, q_shape, (16, 128)]
    result_shapes = [(each, 3 * d), (each, d), (each, ff), (4 * each, d)] + vector_shapes
    part, *summed = pl.pallas_call(
        last_kernel,
        grid=(micro + 2 * steps + 1,),
        in_specs=[small(), small()] + [first(rows, d, buffers=spare)] * 6 + [first(count, 2, 256, 256, buffers=1), first(state_rows(), 128)]
        + [walk(p1)] * 2 + [walk(p1, p3)] + [anywhere] * 2
        + [whole((16, d)), whole((256, 256)), whole((16, d)), fixed((d, 3 * d))],
        out_specs=[walk(p3)] + [fixed(s) for s in summed_shapes],
        out_shape=[like(BF16)] + [jax.ShapeDtypeStruct(s, BF16) for s in summed_shapes[:3]]
        + [jax.ShapeDtypeStruct((16, 128), F32)],
        scratch_shapes=[pltpu.VMEM((micro * rows, d), BF16)] * 3
        + [
            pltpu.VMEM((d, micro * rows), BF16), pltpu.VMEM((d, 3 * d), F32),
            pltpu.VMEM((2, 256, 256), F32), pltpu.VMEM((1, d), F32),
            pltpu.VMEM((2, 256, 256), BF16), pltpu.VMEM((1, d), F32), pltpu.VMEM((16, d), F32),
            pltpu.VMEM((wide,) + kv_shape, BF16), pltpu.VMEM((wide,) + q_shape, BF16),
        ]
        + running_scratch(micro)
        + scatter_scratch(early_shape) + scatter_scratch(kv_shape) + scatter_scratch(q_shape)
        + vector_scratch(),
        compiler_params=pltpu.CompilerParams(
            dimension_semantics=("arbitrary",), vmem_limit_bytes=VMEM, collective_id=1, has_side_effects=True
        ),
        name="last",
    )(lens, off, q, k, v, gnum, gden, kc, states, state_in, k, v, x, use, grads, g_vec, ones, vec, w_qkv)
    grad_input, g_qkv, g_out, g_up, g_down, *g_vectors = pl.pallas_call(
        result_kernel,
        grid=(micro, tiles),
        in_specs=[token, token] + [whole(s) for s in summed_shapes],
        out_specs=[token] + [whole(s) for s in result_shapes],
        out_shape=[like(F32)] + [jax.ShapeDtypeStruct(s, F32) for s in result_shapes],
        compiler_params=params(2),
        name="result",
    )(g_middle, part, *summed)
    piece = [a.reshape(-1) for a in g_vectors]
    return (
        result.reshape(block_in.shape),
        grad_input.reshape(block_in.shape),
        piece[0],
        piece[1],
        g_qkv,
        g_out,
        piece[2],
        piece[3],
        g_up,
        piece[5],
        g_down,
        piece[4],
    )


def solution(mesh):
    tokens = P(None, "dp", "wide", None)
    vector, matrix = P("wide"), P("wide", None)
    weights = (vector, vector, matrix, matrix, vector, vector, matrix, vector, matrix, vector)
    return jax.shard_map(
        per_device,
        mesh=mesh,
        in_specs=(tokens, tokens) + weights + (P(None, "dp", None),),
        out_specs=(tokens, tokens) + weights,
        check_vma=False,
    )
```

```python
import functools

import jax
import jax.numpy as jnp
from jax import lax
from jax.experimental import pallas as pl
from jax.experimental.pallas import tpu as pltpu
from jax.sharding import PartitionSpec as P

HEADS = 8
EPSILON = 1e-05
F32 = jnp.float32
BF16 = jnp.bfloat16
CHUNK = 128
TILE = 512
FF_TILE = 512
VMEM = 62 * 1024 * 1024


def nn(a, b):
    return lax.dot_general(a, b, (((1,), (0,)), ((), ())), preferred_element_type=F32)


def nt(a, b):
    return lax.dot_general(a, b, (((1,), (1,)), ((), ())), preferred_element_type=F32)


def rows_of(row, width):
    return jnp.concatenate([row] * (width // 128), axis=1)


def start_of(lens, m, place):
    start, end = jnp.zeros_like(place), 0
    for j in range(lens.shape[1]):
        end = end + lens[m, j]
        start = start + jnp.where(end <= place, lens[m, j], 0)
    return start


def place_rows(first, count):
    return first + lax.broadcasted_iota(jnp.int32, (count, 128), 0)


def flag(condition):
    return jnp.where(condition, 1.0, 0.0)


def normed(x):
    average = jnp.mean(x, axis=-1, keepdims=True)
    centred = x - average
    spread = jnp.mean(centred * centred, axis=-1, keepdims=True)
    scale = lax.rsqrt(spread + EPSILON)
    return centred * scale, scale


def norm_back(e, xhat, scale, gain):
    a = gain * e
    return scale * (
        a - jnp.mean(a, axis=-1, keepdims=True) - xhat * jnp.mean(a * xhat, axis=-1, keepdims=True)
    )


def feature(v):
    return jnp.where(v > 0.0, v + 1.0, jnp.exp(jnp.minimum(v, 0.0)))


def column_sum(a):
    return jnp.sum(a, axis=0, keepdims=True)


def by_group(fn, *arrays):
    return jnp.concatenate(
        [fn(g, *[a[:, 256 * g : 256 * g + 256] for a in arrays]) for g in range(2)], axis=1
    )


def lane_half(shape):
    return lax.broadcasted_iota(jnp.int32, shape, 1) < 64


def pack_state(state, norm, out):
    folded = [s + pltpu.roll(s, 64, 1) for s in state]
    half = lane_half((128, 128))
    for j in range(2):
        out[128 * j : 128 * j + 128, :] = jnp.where(half, folded[j], folded[2 + j]).astype(out.dtype)
    row = lax.broadcasted_iota(jnp.int32, (16, 128), 0)
    tail = jnp.zeros((16, 128), F32)
    for j in range(4):
        tail = jnp.where(row == j, norm[:, 128 * j : 128 * j + 128], tail)
    out[256:272, :] = tail.astype(out.dtype)
    if out.shape[0] > 272:
        out[272:, :] = jnp.zeros((out.shape[0] - 272, 128), out.dtype)


def unpack_pairs(packed, ones):
    half = lane_half((128, 128))
    mask = ones[0:128, 0:128].astype(F32)
    pairs = [None] * 4
    for j in range(2):
        z = packed[128 * j : 128 * j + 128, :]
        turned = pltpu.roll(z, 64, 1)
        pairs[j] = jnp.where(half, z, turned) * mask
        pairs[2 + j] = jnp.where(half, turned, z) * mask
    tail = packed[256:272, :]
    norm = jnp.concatenate([tail[j : j + 1, :] for j in range(4)], axis=1)
    return pairs, norm


def unpack_state(packed, ones):
    pairs, norm = unpack_pairs(packed, ones)
    zero = jnp.zeros((128, 128), BF16)
    groups = []
    for g in range(2):
        above = jnp.concatenate([pairs[2 * g].astype(BF16), zero], axis=1)
        below = jnp.concatenate([zero, pairs[2 * g + 1].astype(BF16)], axis=1)
        groups.append(jnp.concatenate([above, below], axis=0))
    return groups, norm


MESH = pl.DeviceIdType.MESH


def place():
    dp = lax.axis_index("dp")
    return lax.rem(dp, 2), dp // 2, lax.axis_index("wide"), lax.axis_size("dp") // 2, lax.axis_size("wide")


def others(count, fn):
    def body(o, carry):
        fn(o)
        return carry

    lax.fori_loop(1, count, body, 0)


def remote(src, dst, send, recv, dp, wide):
    return pltpu.make_async_remote_copy(
        src_ref=src, dst_ref=dst, send_sem=send, recv_sem=recv, device_id=(dp, wide), device_id_type=MESH
    )


def greet():
    core, y, me, ny, n = place()
    dp = 2 * y + core
    barrier = pltpu.get_barrier_semaphore()

    def signal(d, w):
        pl.semaphore_signal(barrier, inc=1, device_id=(d, w), device_id_type=MESH)

    others(n, lambda o: signal(dp, lax.rem(me + o, n)))
    others(2 * ny, lambda o: signal(lax.rem(dp + o, 2 * ny), me))
    pl.semaphore_wait(barrier, n - 1 + 2 * ny - 1)


class Gather:
    def __init__(self, src, dst, sems):
        self.src, self.dst = src, dst
        self.near, self.send, self.recv, self.y_send, self.y_recv, self.c_send, self.c_recv = sems
        self.core, self.y, self.me, self.ny, self.n = place()
        self.dp = 2 * self.y + self.core
        each = src.shape[0]
        self.split = split_of(each)
        part = each // self.split
        if self.split == 1:
            self.rows, self.half = pl.ds(0, each), None
        else:
            at = self.core * (each // 2) + self.y * part
            self.rows = pl.ds(pl.multiple_of(at, part), part)
            self.half = pl.ds(pl.multiple_of(self.core * (each // 2), each // 2), each // 2)

    def own(self):
        return pltpu.make_async_copy(self.src.at[self.rows], self.dst.at[self.me, self.rows], self.near)

    def out(self, o):
        to = lax.rem(self.me + o, self.n)
        return remote(self.src.at[self.rows], self.dst.at[self.me, self.rows], self.send.at[o], self.recv.at[self.me], self.dp, to)

    def back(self, o):
        frm = lax.rem(self.me + o, self.n)
        part = self.dst.at[frm, self.rows]
        return remote(part, part, self.send.at[o], self.recv.at[frm], self.dp, frm)

    def start_wide(self):
        self.own().start()
        others(self.n, lambda o: self.out(o).start())

    def finish_wide(self):
        self.own().wait()
        others(self.n, lambda o: self.out(o).wait_send())
        others(self.n, lambda o: self.back(o).wait_recv())

    def along_y(self, o):
        part = self.dst.at[:, self.rows]
        to = lax.rem(self.y + o, self.ny)
        return remote(part, part, self.y_send.at[o], self.y_recv.at[self.y], 2 * to + self.core, self.me)

    def along_y_back(self, o):
        frm = lax.rem(self.y + o, self.ny)
        each = self.src.shape[0]
        part = each // self.split
        at = self.core * (each // 2) + frm * part
        ref = self.dst.at[:, pl.ds(pl.multiple_of(at, part), part)]
        return remote(ref, ref, self.y_send.at[o], self.y_recv.at[frm], 2 * frm + self.core, self.me)

    def start_y(self):
        if self.split > 1:
            others(self.ny, lambda o: self.along_y(o).start())

    def finish_y(self):
        if self.split > 1:
            others(self.ny, lambda o: self.along_y(o).wait_send())
            others(self.ny, lambda o: self.along_y_back(o).wait_recv())

    def cross(self):
        part = self.dst.at[:, self.half]
        return remote(part, part, self.c_send, self.c_recv, 2 * self.y + 1 - self.core, self.me)

    def cross_back(self):
        each = self.src.shape[0]
        at = (1 - self.core) * (each // 2)
        part = self.dst.at[:, pl.ds(pl.multiple_of(at, each // 2), each // 2)]
        return remote(part, part, self.c_send, self.c_recv, 2 * self.y + 1 - self.core, self.me)

    def start_core(self):
        if self.split > 1:
            self.cross().start()

    def finish_core(self):
        if self.split > 1:
            self.cross().wait_send()
            self.cross_back().wait_recv()


def split_of(each):
    count = lax.axis_size("dp")
    return count if each % (16 * count) == 0 else 1


def gather_sems():
    n, ny = lax.axis_size("wide"), lax.axis_size("dp") // 2
    dma = pltpu.SemaphoreType.DMA
    return [dma, dma((n,)), dma((n,)), dma((ny,)), dma((ny,)), dma, dma]


def packed_shape(rows, d):
    unit = 16 * lax.axis_size("dp")
    columns = d if rows % unit == 0 else 128
    rows = rows * (d // columns)
    return -(-rows // unit) * unit, columns


def put(block, at, piece):
    rows, d = piece.shape
    columns = block.shape[1]
    for b in range(d // columns):
        begin = at * (d // columns) + rows * b
        block[begin : begin + rows, :] = piece[:, columns * b : columns * b + columns]


def fill(block, rows, d):
    used = rows * (d // block.shape[1])
    if block.shape[0] > used:
        block[used:, :] = jnp.zeros((block.shape[0] - used, block.shape[1]), block.dtype)


def get(block, at, rows, d):
    columns = block.shape[1]
    begin = at * (d // columns)
    return jnp.concatenate(
        [block[begin + rows * b : begin + rows * b + rows, :] for b in range(d // columns)], axis=1
    )


class Scatter:
    def __init__(self, src, refs):
        self.src = src
        (self.half, self.got_core, self.got_y, self.got_wide, self.out, self.near, self.c_sem, self.y_send,
         self.y_recv, self.w_send, self.w_recv, self.b_send, self.b_recv) = refs
        self.core, self.y, self.me, self.ny, self.n = place()
        self.dp = 2 * self.y + self.core
        self.rows = self.out.shape[0]
        self.each = self.rows // (2 * self.ny)
        self.partner = 2 * self.y + 1 - self.core
        self.part = self.got_core.at[:, 0 : self.each]

    def half_rows(self, core):
        return pl.ds(pl.multiple_of(core * (self.rows // 2), self.rows // 2), self.rows // 2)

    def y_rows(self, y):
        return pl.ds(pl.multiple_of(y * self.each, self.each), self.each)

    def own_rows(self, y):
        at = self.core * (self.rows // 2) + y * self.each
        return pl.ds(pl.multiple_of(at, self.each), self.each)

    def load(self):
        return pltpu.make_async_copy(self.src.at[:, self.half_rows(self.core)], self.half, self.near)

    def cross(self):
        return remote(
            self.src.at[:, self.half_rows(1 - self.core)], self.got_core, self.c_sem.at[0], self.c_sem.at[1], self.partner, self.me
        )

    def start1(self):
        self.cross().start()
        self.load().start()

    def along_y(self, o):
        to = lax.rem(self.y + o, self.ny)
        return remote(
            self.half.at[:, self.y_rows(to)], self.got_y.at[o - 1], self.y_send.at[o], self.y_recv.at[o],
            2 * to + self.core, self.me,
        )

    def finish1_start2(self):
        self.load().wait()
        self.cross().wait()

        def add(w, carry):
            self.half[w] = (self.half[w].astype(F32) + self.got_core[w].astype(F32)).astype(BF16)
            return carry

        lax.fori_loop(0, self.n, add, 0)
        others(self.ny, lambda o: self.along_y(o).start())

    def along_wide(self, o):
        to = lax.rem(self.me + o, self.n)
        return remote(self.part.at[to], self.got_wide.at[o - 1], self.w_send.at[o], self.w_recv.at[o], self.dp, to)

    def finish2_start3(self):
        others(self.ny, lambda o: self.along_y(o).wait())

        def add(w, carry):
            total = self.half[w, self.y_rows(self.y)].astype(F32)
            for o in range(self.ny - 1):
                total = total + self.got_y[o, w].astype(F32)
            self.part[w] = total.astype(BF16)
            return carry

        lax.fori_loop(0, self.n, add, 0)
        others(self.n, lambda o: self.along_wide(o).start())

    def back(self, o, wait=False):
        other = lax.rem(self.dp + o, 2 * self.ny)
        slot = other if wait else self.dp
        at = lax.rem(slot, 2) * (self.rows // 2) + (slot // 2) * self.each
        ref = self.out.at[pl.ds(pl.multiple_of(at, self.each), self.each)]
        return remote(ref, ref, self.b_send.at[o], self.b_recv.at[slot], other, self.me)

    def finish3_start4(self):
        others(self.n, lambda o: self.along_wide(o).wait())
        total = self.part[self.me].astype(F32)
        total = lax.fori_loop(0, self.n - 1, lambda o, t: t + self.got_wide[o].astype(F32), total)
        self.out[self.own_rows(self.y)] = total.astype(BF16)
        others(2 * self.ny, lambda o: self.back(o).start())

    def finish4(self):
        others(2 * self.ny, lambda o: self.back(o).wait_send())
        others(2 * self.ny, lambda o: self.back(o, True).wait_recv())


def scatter_scratch(shape):
    rows, d = shape
    n, dp = lax.axis_size("wide"), lax.axis_size("dp")
    ny, part = dp // 2, rows // dp
    dma = pltpu.SemaphoreType.DMA
    return [
        pltpu.VMEM((n, rows // 2, d), BF16),
        pltpu.VMEM((n, rows // 2, d), BF16),
        pltpu.VMEM((ny - 1, n, part, d), BF16),
        pltpu.VMEM((n - 1, part, d), BF16),
        pltpu.VMEM((rows, d), BF16),
        dma, dma((2,)), dma((ny,)), dma((ny,)), dma((n,)), dma((n,)), dma((dp,)), dma((dp,)),
    ]


class VectorSum:
    def __init__(self, refs):
        self.tiles, self.got_core, self.got_y, self.got_wide, self.c_sem, self.y_send, self.y_recv, self.w_send, self.w_recv = refs
        self.core, self.y, self.me, self.ny, self.n = place()
        self.dp = 2 * self.y + self.core

    def cross(self):
        return remote(self.tiles, self.got_core, self.c_sem.at[0], self.c_sem.at[1], 2 * self.y + 1 - self.core, self.me)

    def along_y(self, o):
        to = lax.rem(self.y + o, self.ny)
        return remote(self.tiles, self.got_y.at[o - 1], self.y_send.at[o], self.y_recv.at[o], 2 * to + self.core, self.me)

    def along_wide(self, o):
        to = lax.rem(self.me + o, self.n)
        return remote(self.tiles.at[to], self.got_wide.at[o - 1], self.w_send.at[o], self.w_recv.at[o], self.dp, to)

    def start1(self):
        self.cross().start()

    def finish1_start2(self):
        self.cross().wait()
        self.tiles[...] = self.tiles[...] + self.got_core[...]
        others(self.ny, lambda o: self.along_y(o).start())

    def finish2_start3(self):
        others(self.ny, lambda o: self.along_y(o).wait())
        total = self.tiles[...]
        for o in range(self.ny - 1):
            total = total + self.got_y[o]
        self.tiles[...] = total
        others(self.n, lambda o: self.along_wide(o).start())

    def finish3(self):
        others(self.n, lambda o: self.along_wide(o).wait())
        return lax.fori_loop(0, self.n - 1, lambda o, t: t + self.got_wide[o], self.tiles[self.me])


def vector_scratch():
    n, ny = lax.axis_size("wide"), lax.axis_size("dp") // 2
    dma = pltpu.SemaphoreType.DMA
    return [
        pltpu.VMEM((n, 16, 128), F32),
        pltpu.VMEM((n, 16, 128), F32),
        pltpu.VMEM((ny - 1, n, 16, 128), F32),
        pltpu.VMEM((n - 1, 16, 128), F32),
        dma((2,)), dma((ny,)), dma((ny,)), dma((n,)), dma((n,)),
    ]


def owner_tiles(rows, tiles, each):
    n = tiles.shape[0]
    d = each * n
    per = 4 * each
    row = lax.broadcasted_iota(jnp.int32, (16, 128), 0)
    lane = lax.broadcasted_iota(jnp.int32, (16, 128), 1)
    blocks = [rows[:, 128 * j : 128 * j + 128] for j in range(d // 128)]

    def turned(a, by, axis):
        by = by % a.shape[axis]
        return pltpu.roll(a, by, axis) if by else a

    for w in range(n):
        at = each * w
        tile = jnp.where(row < 5, turned(blocks[at // 128], -(at % 128), 1), 0.0)
        for r in range(4):
            at = per * w + each * r
            from_row, begin = 5 + at // d, at % d
            moved = turned(turned(blocks[begin // 128], -(begin % 128), 1), 5 + r - from_row, 0)
            tile = jnp.where(row == 5 + r, moved, tile)
        tiles[w] = jnp.where(lane < each, tile, 0.0)


HIGH = 4


def low_count():
    return lax.axis_size("wide") // HIGH


def state_rows():
    unit = 16 * low_count()
    return -(-272 // unit) * unit


class Running:
    def __init__(self, own, upward, refs):
        self.own, self.upward = own, upward
        (self.slots, self.group, self.high, self.mine, self.spread, self.result, self.near, self.send1, self.recv1,
         self.send2, self.recv2, self.send3, self.recv3) = refs
        _, _, self.me, _, _ = place()
        self.dp = lax.axis_index("dp")
        self.lo = low_count()
        self.h, self.l = self.me // self.lo, lax.rem(self.me, self.lo)
        self.part = state_rows() // self.lo

    def slice(self, l):
        return pl.ds(pl.multiple_of(l * self.part, self.part), self.part)

    def copy1(self, o, back=False):
        other = lax.rem(self.l + o, self.lo)
        slot = other if back else self.l
        return remote(self.own, self.slots.at[slot], self.send1.at[o], self.recv1.at[slot], self.dp, self.h * self.lo + other)

    def near1(self):
        return pltpu.make_async_copy(self.own, self.slots.at[self.l], self.near.at[0])

    def start1(self):
        self.near1().start()
        others(self.lo, lambda o: self.copy1(o).start())

    def before(self, a, b):
        return a < b if self.upward else a > b

    def finish1_start2(self):
        self.near1().wait()
        others(self.lo, lambda o: self.copy1(o).wait_send())
        others(self.lo, lambda o: self.copy1(o, True).wait_recv())
        every = jnp.zeros(self.own.shape, F32)
        inner = every
        for l in range(self.lo):
            part = self.slots[l].astype(F32)
            every = every + part
            inner = inner + jnp.where(self.before(l, self.l), part, 0.0)
        self.group[...] = every.astype(BF16)
        self.result[...] = inner

        def send(o):
            other = lax.rem(self.h + o, HIGH)

            @pl.when(self.before(self.h, other))
            def _():
                self.copy2(o).start()

        others(HIGH, send)

    def copy2(self, o, back=False):
        other = lax.rem(self.h + o, HIGH)
        slot = other if back else self.h
        return remote(
            self.group.at[:, self.slice(self.l)], self.high.at[slot], self.send2.at[o], self.recv2.at[slot],
            self.dp, other * self.lo + self.l,
        )

    def finish2_start3(self):
        def wait(o):
            other = lax.rem(self.h + o, HIGH)

            @pl.when(self.before(self.h, other))
            def _():
                self.copy2(o).wait_send()

            @pl.when(self.before(other, self.h))
            def _():
                self.copy2(o, True).wait_recv()

        others(HIGH, wait)
        total = jnp.zeros(self.mine.shape, F32)
        for h in range(HIGH):
            total = total + jnp.where(self.before(h, self.h), self.high[h].astype(F32), 0.0)
        self.mine[...] = total.astype(BF16)
        self.near3().start()
        others(self.lo, lambda o: self.copy3(o).start())

    def near3(self):
        return pltpu.make_async_copy(self.mine, self.spread.at[self.l], self.near.at[1])

    def copy3(self, o, back=False):
        other = lax.rem(self.l + o, self.lo)
        slot = other if back else self.l
        return remote(self.mine, self.spread.at[slot], self.send3.at[o], self.recv3.at[slot], self.dp, self.h * self.lo + other)

    def finish3(self):
        self.near3().wait()
        others(self.lo, lambda o: self.copy3(o).wait_send())
        others(self.lo, lambda o: self.copy3(o, True).wait_recv())
        for l in range(self.lo):
            rows = slice(l * self.part, (l + 1) * self.part)
            self.result[:, rows] = self.result[:, rows] + self.spread[l].astype(F32)


def running_scratch(micro):
    lo, rows = low_count(), state_rows()
    dma = pltpu.SemaphoreType.DMA
    return [
        pltpu.VMEM((lo, micro, rows, 128), BF16),
        pltpu.VMEM((micro, rows, 128), BF16),
        pltpu.VMEM((HIGH, micro, rows // lo, 128), BF16),
        pltpu.VMEM((micro, rows // lo, 128), BF16),
        pltpu.VMEM((lo, micro, rows // lo, 128), BF16),
        pltpu.VMEM((micro, rows, 128), F32),
        dma((2,)), dma((lo,)), dma((lo,)), dma((HIGH,)), dma((HIGH,)), dma((lo,)), dma((lo,)),
    ]


def vector_tile(vectors, each):
    row = lax.broadcasted_iota(jnp.int32, (16, 128), 0)

    def padded(piece):
        return jnp.concatenate([piece.astype(F32), jnp.zeros((1, 128 - each), F32)], axis=1)

    pieces = [padded(v[...]) for v in vectors[:5]]
    hidden = vectors[5][...]
    pieces += [padded(hidden[:, each * r : each * r + each]) for r in range(hidden.shape[1] // each)]
    tile = jnp.zeros((16, 128), F32)
    for j, piece in enumerate(pieces):
        tile = jnp.where(row == j, piece, tile)
    return tile.astype(BF16)


def spread_vectors(slots, out, each):
    n = slots.shape[0]
    d = each * n
    per = 4 * each
    row = lax.broadcasted_iota(jnp.int32, (16, 128), 0)
    blocks = [jnp.zeros((16, 128), F32) for _ in range(d // 128)]
    for w in range(n):
        tile = slots[w].astype(F32)
        at = each * w
        moved = pltpu.roll(tile, at % 128, 1) if at % 128 else tile
        blocks[at // 128] = blocks[at // 128] + jnp.where(row < 5, moved, 0.0)
        for r in range(4):
            at = per * w + each * r
            to_row, lane = 5 + at // d, at % d
            only = jnp.where(row == 5 + r, tile, 0.0)
            moved = pltpu.roll(only, lane % 128, 1) if lane % 128 else only
            if to_row != 5 + r:
                moved = pltpu.roll(moved, (to_row - 5 - r) % 16, 0)
            blocks[lane // 128] = blocks[lane // 128] + moved
    for j, block in enumerate(blocks):
        out[:, 128 * j : 128 * j + 128] = block


def first_kernel(lens, off, x, *refs):
    (s_qkv, s_out, s_up, s_down, v0, v1, v2, v3, v4, v5, ones,
     q_out, k_out, v_out, num_out, kc_out, states_out, state_in, w_qkv, w_out, w_up, w_down, vec_out,
     w_ref, h_all, q_all, k_all, v_all, state, norm, local, tile, tiles_ref, tile_near, tile_send, tile_recv,
     save_sem, *rest) = refs
    each = s_qkv.shape[0]
    micro, rows, d = x.shape
    half = micro // 2
    running = []
    for j in range(2):
        running.append(Running(local.at[half * j : half * j + half], True, rest[:13]))
        rest = rest[13:]
    jobs = []
    for j in range(3):
        jobs.append(Gather(s_qkv.at[:, d * j : d * j + d], w_ref.at[j], rest[7 * j : 7 * j + 7]))
    for j, (src, dst) in enumerate(((s_out, w_out), (s_up, w_up), (s_down, w_down))):
        jobs.append(Gather(src, dst, rest[21 + 7 * j : 28 + 7 * j]))
    i = pl.program_id(0)
    core, y, me, ny, n = place()
    dp = 2 * y + core

    def vec_copy(o, back=False):
        other = lax.rem(me + o, n)
        slot = other if back else me
        return remote(tile, tiles_ref.at[slot], tile_send.at[o], tile_recv.at[slot], dp, other)

    def vec_near():
        return pltpu.make_async_copy(tile, tiles_ref.at[me], tile_near)

    def save(j):
        return pltpu.make_async_copy(w_ref.at[j], w_qkv.at[:, :, d * j : d * j + d], save_sem.at[j])

    def weights(j):
        return w_ref[j].reshape(d, d)

    @pl.when(i == 0)
    def _():
        tile[...] = vector_tile((v0, v1, v2, v3, v4, v5), each)
        greet()
        vec_near().start()
        others(n, lambda o: vec_copy(o).start())
        for job in jobs[:3]:
            job.start_wide()
        vec_near().wait()
        others(n, lambda o: vec_copy(o).wait_send())
        others(n, lambda o: vec_copy(o, True).wait_recv())
        spread_vectors(tiles_ref, vec_out, each)

        def norm_micro(m, carry):
            xhat, _ = normed(x[m].astype(F32))
            h_all[m] = (xhat * vec_out[0:1, :] + vec_out[1:2, :]).astype(BF16)
            return carry

        lax.fori_loop(0, micro // 2, norm_micro, 0)
        jobs[0].finish_wide()
        jobs[0].start_y()
        lax.fori_loop(micro // 2, micro, norm_micro, 0)
        for job in jobs[1:3]:
            job.finish_wide()
            job.start_y()
        for job in jobs[3:]:
            job.start_wide()
        jobs[0].finish_y()
        jobs[0].start_core()
        jobs[0].finish_core()

    @pl.when(i == 1)
    def _():
        jobs[1].finish_y()
        jobs[1].start_core()

    @pl.when(i == 2)
    def _():
        jobs[2].finish_y()
        jobs[2].start_core()

    @pl.when(i < micro)
    def _():
        q = feature(nn(h_all[i], weights(0))).astype(BF16)
        q_out[...] = q
        q_all[i] = q

    @pl.when(i == micro)
    def _():
        jobs[1].finish_core()

    @pl.when((i >= micro) & (i < 2 * micro))
    def _():
        m = i - micro
        k = feature(nn(h_all[m], weights(1))).astype(BF16)
        k_out[...] = k
        k_all[m] = k

    @pl.when(i == 2 * micro)
    def _():
        jobs[2].finish_core()
        for j in range(3):
            save(j).start()

    @pl.when((i >= 2 * micro) & (i < 3 * micro))
    def _():
        m = i - 2 * micro
        v = nn(h_all[m], weights(2)).astype(BF16)
        v_out[...] = v
        v_all[m] = v
        base = off[0]
        final = start_of(lens, m, base + rows - 1)
        last = flag(start_of(lens, m, place_rows(base, rows)) == final)
        k_last = k_all[m] * rows_of(last.astype(BF16), d)
        k_turned = k_last.T
        mask = ones[0:128, 0:128].astype(F32)
        parts = [nn(k_turned[128 * p : 128 * p + 128, :], v[:, 128 * p : 128 * p + 128]) * mask for p in range(4)]
        pack_state(parts, column_sum(k_last.astype(F32)), local.at[m])

    @pl.when(i == 2 * micro + half - 1)
    def _():
        running[0].start1()

    @pl.when(i == 2 * micro + half)
    def _():
        for job in jobs[3:5]:
            job.finish_wide()
            job.start_y()

    @pl.when(i == 3 * micro - 1)
    def _():
        running[1].start1()

    @pl.when(i == 3 * micro)
    def _():
        running[0].finish1_start2()

    @pl.when(i == 3 * micro + 1)
    def _():
        running[1].finish1_start2()
        jobs[5].finish_wide()
        jobs[5].start_y()

    @pl.when(i == 3 * micro + 2)
    def _():
        running[0].finish2_start3()
        for job in jobs[3:5]:
            job.finish_y()
            job.start_core()

    @pl.when(i == 3 * micro + 3)
    def _():
        running[1].finish2_start3()

    @pl.when(i >= 3 * micro)
    def _():
        m = i - 3 * micro
        attend(lens, m, off[0], q_all.at[m], k_all.at[m], v_all.at[m], ones, num_out, kc_out, states_out, state, norm)

    @pl.when(i == 4 * micro - 1)
    def _():
        jobs[5].finish_y()
        jobs[5].start_core()
        for j in range(2):
            running[j].finish3()
            state_in[half * j : half * j + half] = running[j].result[...]
        for job in jobs[3:]:
            job.finish_core()
        for j in range(3):
            save(j).wait()


def chunk_masks(lens, m, begin, size):
    by_row = start_of(lens, m, place_rows(begin, size))
    lane = begin + lax.broadcasted_iota(jnp.int32, (8, size), 1)
    by_column = start_of(lens, m, lane)[0:1, :]
    final = start_of(lens, m, begin + size - 1)
    return by_row, by_column, final


def pair_mask():
    return flag(lane_half((16, 128))).astype(BF16)[0:1, :]


def split_pair(a, low, high):
    return jnp.concatenate([a * low, a * high], axis=0)


def attend(lens, m, base, q_ref, k_ref, v_ref, ones, num_out, kc_out, states_out, state, norm):
    rows, d = q_ref.shape
    size = CHUNK
    state[...] = jnp.zeros_like(state)
    norm[...] = jnp.zeros_like(norm)
    half = lane_half((1, 128))
    low = flag(half).astype(BF16)
    high = flag(jnp.logical_not(half)).astype(BF16)

    def step(c, carry):
        at = pl.ds(pl.multiple_of(c * size, size), size)
        begin = base + c * size
        q, k, v = q_ref[at, :], k_ref[at, :], v_ref[at, :]
        by_row, by_column, final = chunk_masks(lens, m, begin, size)
        places = lax.broadcasted_iota(jnp.int32, (size, size), 0)
        columns = lax.broadcasted_iota(jnp.int32, (size, size), 1)
        allowed = flag((places >= columns) & (by_row[:, :size] == by_column)).astype(BF16)
        allowed2 = jnp.concatenate([allowed, allowed], axis=1)
        seen = flag(by_row < begin)
        last = flag(by_row == final).astype(BF16)
        keep = jnp.where(final < begin, 1.0, 0.0)
        kc_out[at, :] = (nn(allowed, k) + rows_of(seen, d) * norm[...]).astype(BF16)
        q_seen = q * rows_of(seen.astype(BF16), d)
        for p in range(4):
            cut = slice(128 * p, 128 * p + 128)
            s = nt(q[:, cut], split_pair(k[:, cut], low, high)).astype(BF16) * allowed2
            inside = nn(s, split_pair(v[:, cut], low, high))
            held = state[p].astype(BF16)
            states_out[c, p] = held
            before = nn(q_seen[:, cut], held)
            num_out[at, cut] = (inside + before).astype(BF16)
        k_last = k * rows_of(last, d)
        k_turned = k_last.T
        mask = ones[0:128, 0:128].astype(F32)
        for p in range(4):
            cut = slice(128 * p, 128 * p + 128)
            state[p] = keep * state[p] + nn(k_turned[cut, :], v[:, cut]) * mask
        norm[...] = keep * norm[...] + column_sum(k_last.astype(F32))
        return carry

    lax.fori_loop(0, rows // size, step, 0, unroll=8)


def middle_kernel(
    lens, off, q_ref, num_ref, kc_ref, x_ref, cot_ref, state_in, ones,
    w_out, vec, w_up, w_down,
    block_out, gm_out, gnum_out, gden_out, use_out, grads, g_vec,
    groups, norm, use, use_norm, acc_out, acc_up, acc_down, total, e_total, h2_ref, h2t_ref, ct_ref,
):
    m, t, tiles = pl.program_id(0), pl.program_id(1), pl.num_programs(1)
    rows, d = x_ref.shape
    first = (m == 0) & (t == 0)
    final = (m == pl.num_programs(0) - 1) & (t == tiles - 1)
    base = off[0]

    @pl.when(first)
    def _():
        acc_out[...] = jnp.zeros_like(acc_out)
        acc_up[...] = jnp.zeros_like(acc_up)
        acc_down[...] = jnp.zeros_like(acc_down)
        g_vec[...] = jnp.zeros_like(g_vec)

    @pl.when(t == 0)
    def _():
        parts, z = unpack_state(state_in[...], ones[...])
        for g in range(2):
            groups[g] = parts[g]
        norm[...] = z
        use[...] = jnp.zeros_like(use)
        use_norm[...] = jnp.zeros_like(use_norm)

    gain, bias, down_bias = vec[2:3, :], vec[3:4, :], vec[4:5, :]
    q = q_ref[...]
    seen = flag(start_of(lens, m, place_rows(base + t * rows, rows)) < base)
    q_seen = q * rows_of(seen.astype(BF16), d)
    num = num_ref[...].astype(F32) + by_group(lambda g, a: nn(a, groups[g]), q_seen)
    kc = kc_ref[...].astype(F32) + rows_of(seen, d) * norm[...]
    den = by_group(lambda g, a: nn(a, ones[...]), (q.astype(F32) * kc).astype(BF16))
    over = 1.0 / den
    mixed = (num * over).astype(BF16)
    middle = x_ref[...].astype(F32) + nn(mixed, w_out[...])
    xhat, scale = normed(middle)
    h2 = (xhat * gain + bias).astype(BF16)
    h2_ref[...] = h2
    h2t_ref[...] = h2.T
    ct_ref[...] = cot_ref[...].T
    total[...] = middle + down_bias
    e_total[...] = jnp.zeros_like(e_total)

    def ffn(f, carry):
        cut = pl.ds(pl.multiple_of(f * FF_TILE, FF_TILE), FF_TILE)
        hidden = nn(h2_ref[...], w_up[:, cut]) + vec[pl.ds(5 + f, 1), :]
        pulled = nt(cot_ref[...], w_down[cut, :])
        square = hidden * hidden
        c0, c1 = 0.7978845608028654, 0.044715
        th = jnp.tanh(hidden * (c0 + (c0 * c1) * square))
        half_up = 0.5 + 0.5 * th
        active = (hidden * half_up).astype(BF16)
        slope = half_up + (0.5 * hidden) * (1.0 - th * th) * (c0 + (3.0 * c0 * c1) * square)
        g_hidden = slope * pulled
        g_low = g_hidden.astype(BF16)
        total[...] += nn(active, w_down[cut, :])
        e_total[...] += nt(g_low, w_up[:, cut])
        acc_down[:, cut] += nn(ct_ref[...], active)
        acc_up[:, cut] += nn(h2t_ref[...], g_low)
        g_vec[pl.ds(5 + f, 1), :] += column_sum(g_hidden)
        return carry

    lax.fori_loop(0, w_up.shape[1] // FF_TILE, ffn, 0, unroll=True)
    block_out[...] = total[...].astype(BF16)
    e = e_total[...]
    cot = cot_ref[...].astype(F32)
    g_middle = cot + norm_back(e, xhat, scale, gain)
    gm_out[...] = g_middle.astype(BF16)
    g_vec[2:3, :] += column_sum(e * xhat)
    g_vec[3:4, :] += column_sum(e)
    g_vec[4:5, :] += column_sum(cot)
    branch = g_middle.astype(BF16)
    acc_out[...] += nn(mixed.T, branch)
    g_mixed = nt(branch, w_out[...])
    gnum = (g_mixed * over).astype(BF16)
    gnum_out[...] = gnum
    gden = -by_group(lambda g, a: nn(a, ones[...]), (g_mixed * num).astype(BF16)) * (over * over)
    gden_out[...] = gden.astype(BF16)
    turned = q_seen.T
    for g in range(2):
        cut = slice(256 * g, 256 * g + 256)
        use[g] += nn(turned[cut, :], gnum[:, cut])
    use_norm[...] += column_sum(q_seen.astype(F32) * gden)

    @pl.when(t == tiles - 1)
    def _():
        mask = ones[0:128, 0:128].astype(F32)
        pack_state([use[p // 2][128 * (p % 2) : 128 * (p % 2) + 128, 128 * (p % 2) : 128 * (p % 2) + 128] * mask for p in range(4)], use_norm[...], use_out)

    @pl.when(final)
    def _():
        n = grads.shape[0]
        each = d // n
        down = acc_down[...].astype(BF16).T
        for w in range(n):
            at = slice(each * w, each * w + each)
            block = grads.at[w]
            for j in range(4):
                put(block, each * j, acc_up[at, d * j : d * j + d].astype(BF16))
            put(block, 4 * each, acc_out[at, :].astype(BF16))
            put(block, 5 * each, down[4 * each * w : 4 * each * w + 4 * each, :])
            fill(block, 9 * each, d)


def attend_back(
    lens, m, base, q_ref, k_ref, v_ref, gnum_ref, gden_ref, kc_ref, states, state_in, ones,
    gq_out, dk_out, dv_out, after, after_norm,
):
    rows, d = q_ref.shape
    size = CHUNK
    count = rows // size
    after[...] = jnp.zeros_like(after)
    after_norm[...] = jnp.zeros_like(after_norm)
    half = lane_half((1, 128))
    low = flag(half).astype(BF16)
    high = flag(jnp.logical_not(half)).astype(BF16)
    pairs_in, norm_in = unpack_pairs(state_in[...], ones[...])

    def step(i, carry):
        c = count - 1 - i
        at = pl.ds(pl.multiple_of(c * size, size), size)
        begin = base + c * size
        q, k, v, gnum = q_ref[at, :], k_ref[at, :], v_ref[at, :], gnum_ref[at, :]
        gden = gden_ref[at, :].astype(F32)
        by_row, by_column, final = chunk_masks(lens, m, begin, size)
        places = lax.broadcasted_iota(jnp.int32, (size, size), 0)
        columns = lax.broadcasted_iota(jnp.int32, (size, size), 1)
        same = by_row[:, :size] == by_column
        allowed = flag((places >= columns) & same).astype(BF16)
        allowed2 = jnp.concatenate([allowed, allowed], axis=1)
        turned = flag((places <= columns) & same).astype(BF16)
        turned2 = jnp.concatenate([turned, turned], axis=1)
        seen = rows_of(flag(by_row < begin).astype(BF16), d)
        seen_all = flag(by_row < base)
        last = flag(by_row == final)
        keep = jnp.where(final < begin, 1.0, 0.0)
        last_low = rows_of(last.astype(BF16), d)
        carried = jnp.where((c == 0) | (start_of(lens, m, begin - 1) < base), 1.0, 0.0)
        gnum_seen = gnum * seen
        k_last, v_last = k * last_low, v * last_low
        gden_q = gden * q.astype(F32)
        dk_den = nn(turned, gden_q.astype(BF16)) + rows_of(last, d) * after_norm[...]
        dq_den = gden * (kc_ref[at, :].astype(F32) + rows_of(seen_all, d) * norm_in)
        for p in range(4):
            cut = slice(128 * p, 128 * p + 128)
            held = (states[c, p].astype(F32) + carried * pairs_in[p]).astype(BF16)
            g_after = after[p].astype(BF16)
            qp, kp, vp, gp = q[:, cut], k[:, cut], v[:, cut], gnum[:, cut]
            q2, k2 = split_pair(qp, low, high), split_pair(kp, low, high)
            v2, g2 = split_pair(vp, low, high), split_pair(gp, low, high)
            s_turned = nt(kp, q2).astype(BF16) * turned2
            gs_turned = nt(vp, g2).astype(BF16) * turned2
            gs = nt(gp, v2).astype(BF16) * allowed2
            dq = nn(gs, k2) + nt(gnum_seen[:, cut], held) + dq_den[:, cut]
            gq_out[at, cut] = (jnp.minimum(qp.astype(F32), 1.0) * dq).astype(BF16)
            dk = nn(gs_turned, q2) + nt(v_last[:, cut], g_after) + dk_den[:, cut]
            dk_out[at, cut] = dk.astype(BF16)
            dv = nn(s_turned, g2) + nn(k_last[:, cut], g_after)
            dv_out[at, cut] = dv.astype(BF16)
        q_turned = (q * seen).T
        mask = ones[0:128, 0:128].astype(F32)
        for p in range(4):
            cut = slice(128 * p, 128 * p + 128)
            after[p] = keep * after[p] + nn(q_turned[cut, :], gnum[:, cut]) * mask
        after_norm[...] = keep * after_norm[...] + column_sum(gden_q * seen.astype(F32))
        return carry

    lax.fori_loop(0, count, step, 0, unroll=4)


def last_kernel(lens, off, *refs):
    (q_ref, k_ref, v_ref, gnum_ref, gden_ref, kc_ref, states, state_in, x_ref, use, grads, g_vec, ones, vec, w,
     gx_out, early_out, later_out, latest_out, final_out, vector_out,
     gq_all, dk_all, dv_all, h1t_all, acc, after, after_norm, sums, shares, src_k, src_v, src_q, *rest) = refs
    micro = use.shape[0]
    rows, d = q_ref.shape
    n = src_q.shape[0]
    each = d // n
    running = Running(use, False, rest[:13])
    rest = rest[13:]
    jobs = [Scatter(src, rest[13 * j : 13 * j + 13]) for j, src in enumerate((grads, src_k, src_v, src_q))]
    early, of_k, of_v, of_q = jobs
    vector = VectorSum(rest[52:])
    i = pl.program_id(0)
    base = off[0]
    p1, p2, p3, p4, end = micro, 2 * micro, 3 * micro, 3 * micro + 1, 4 * micro + 1

    def at_step(step, *actions):
        @pl.when(i == step)
        def _():
            for action in actions:
                action()

    @pl.when(i == 0)
    def _():
        greet()
        running.start1()
        early.start1()
        acc[...] = jnp.zeros_like(acc)
        shares[...] = jnp.zeros_like(shares)

    at_step(1, running.finish1_start2, early.finish1_start2)
    at_step(3, running.finish2_start3, early.finish2_start3)
    at_step(p1, running.finish3)
    at_step(p1 + 3, early.finish3_start4)
    at_step(p2 + 1, early.finish4, of_k.finish1_start2)
    at_step(p2 + 3, of_k.finish2_start3)
    at_step(p4, of_k.finish3_start4)
    at_step(p4 + 1, of_v.finish2_start3, vector.finish1_start2)
    at_step(p4 + 2, of_k.finish4, of_q.finish2_start3)
    at_step(p4 + 3, of_v.finish3_start4, vector.finish2_start3)

    @pl.when(i < p1)
    def _():
        at = pl.ds(pl.multiple_of(i * rows, rows), rows)
        attend_back(
            lens, i, base, q_ref, k_ref, v_ref, gnum_ref, gden_ref, kc_ref, states, state_in, ones,
            gq_all.at[at], dk_all.at[at], dv_all.at[at], after, after_norm,
        )

    def block(m):
        final = start_of(lens, m, base + rows - 1)
        last = flag(start_of(lens, m, place_rows(base, rows)) == final)
        groups, norm = unpack_state(running.result[m], ones[...])
        return last, rows_of(last.astype(BF16), d), groups, norm

    @pl.when((i >= p1) & (i < p2))
    def _():
        m = i - p1
        at = pl.ds(pl.multiple_of(m * rows, rows), rows)
        last, last_low, groups, norm = block(m)
        dk = dk_all[at, :].astype(F32) + rows_of(last, d) * norm
        dk = dk + by_group(lambda g, a: nt(a, groups[g]), v_ref[...] * last_low)
        gk = (jnp.minimum(k_ref[...].astype(F32), 1.0) * dk).astype(BF16)
        dk_all[at, :] = gk
        xhat, _ = normed(x_ref[...].astype(F32))
        h1t = (xhat * vec[0:1, :] + vec[1:2, :]).astype(BF16).T
        h1t_all[:, at] = h1t
        acc[:, d : 2 * d] += nn(h1t, gk)
        shares[:, d : 2 * d] += column_sum(gk.astype(F32))

    def arrange(src, part):
        for w_ in range(n):
            put(src.at[w_], 0, acc[each * w_ : each * w_ + each, d * part : d * part + d].astype(BF16))
            fill(src.at[w_], each, d)

    @pl.when(i == p2 - 1)
    def _():
        arrange(src_k, 1)
        of_k.start1()

    @pl.when((i >= p2) & (i < p3))
    def _():
        m = i - p2
        at = pl.ds(pl.multiple_of(m * rows, rows), rows)
        _, last_low, groups, _ = block(m)
        gv = dv_all[at, :].astype(F32) + by_group(lambda g, a: nn(a, groups[g]), k_ref[...] * last_low)
        gv = gv.astype(BF16)
        dv_all[at, :] = gv
        acc[:, 2 * d :] += nn(h1t_all[:, at], gv)
        shares[:, 2 * d :] += column_sum(gv.astype(F32))

    @pl.when(i == p3 - 1)
    def _():
        arrange(src_v, 2)
        of_v.start1()

    @pl.when(i == p3)
    def _():
        early_out[...] = early.out[...]

        def add(m, carry):
            at = pl.ds(pl.multiple_of(m * rows, rows), rows)
            gq = gq_all[at, :]
            acc[:, 0:d] += nn(h1t_all[:, at], gq)
            shares[:, 0:d] += column_sum(gq.astype(F32))
            return carry

        lax.fori_loop(0, micro // 2, add, 0)
        of_v.finish1_start2()
        lax.fori_loop(micro // 2, micro, add, 0)
        arrange(src_q, 0)
        of_q.start1()
        both = jnp.zeros((d, 128), F32)
        only = jnp.zeros((d, 128), F32)
        for j in range(3 * d // 128):
            cut = slice(128 * j, 128 * j + 128)
            weight = w[:, cut].astype(F32)
            both = both + weight * acc[:, cut]
            only = only + weight * shares[:, cut]
        both, only = column_sum(both.T), column_sum(only.T)
        sums[...] = g_vec[...]
        sums[0:1, :] = (both - vec[1:2, :] * only) / vec[0:1, :]
        sums[1:2, :] = only
        owner_tiles(sums[...], vector.tiles, each)
        vector.start1()
        of_q.finish1_start2()

    @pl.when(i >= p4)
    def _():
        at = pl.ds(pl.multiple_of((i - p4) * rows, rows), rows)
        e = nt(gq_all[at, :], w[:, 0:d]) + nt(dk_all[at, :], w[:, d : 2 * d]) + nt(dv_all[at, :], w[:, 2 * d :])
        xhat, scale = normed(x_ref[...].astype(F32))
        gx_out[...] = norm_back(e, xhat, scale, vec[0:1, :]).astype(BF16)

    @pl.when(i == end - 1)
    def _():
        of_q.finish3_start4()
        later_out[...] = of_k.out[...]
        vector_out[...] = vector.finish3()
        of_v.finish4()
        latest_out[...] = of_v.out[...]
        of_q.finish4()
        final_out[...] = of_q.out[...]


def result_kernel(
    gm_ref, part_ref, early, of_k, of_v, of_q, vector, gx, g_qkv, g_out, g_up, g_down, v0, v1, v2, v3, v4, v5
):
    gx[...] = gm_ref[...].astype(F32) + part_ref[...].astype(F32)

    @pl.when(pl.program_id(0) == 0)
    def _():
        each, d = g_out.shape
        for j in range(4):
            g_up[:, d * j : d * j + d] = get(early, each * j, each, d).astype(F32)
        g_out[...] = get(early, 4 * each, each, d).astype(F32)
        g_down[...] = get(early, 5 * each, 4 * each, d).astype(F32)
        for j, part in enumerate((of_q, of_k, of_v)):
            g_qkv[:, d * j : d * j + d] = get(part, 0, each, d).astype(F32)
        for j, v in enumerate((v0, v1, v2, v3, v4)):
            v[...] = vector[j : j + 1, :each]
        for r in range(4):
            v5[:, each * r : each * r + each] = vector[5 + r : 6 + r, :each]


def params(count):
    return pltpu.CompilerParams(
        dimension_semantics=("arbitrary",) * count, vmem_limit_bytes=VMEM
    )


def small():
    return pl.BlockSpec(memory_space=pltpu.SMEM)


def per_device(
    block_in, cotangent, ln1_gain, ln1_bias, qkv_weight, out_weight, ln2_gain, ln2_bias,
    up_weight, up_bias, down_weight, down_bias, seq_lengths,
):
    micro, rows, d = block_in.shape[0], block_in.shape[2], block_in.shape[3]
    ff = up_weight.shape[1]
    wide, index = lax.axis_size("wide"), lax.axis_index("wide")
    lens = seq_lengths.reshape(micro, -1)
    off = (index * rows).astype(jnp.int32).reshape(1)
    x = block_in.reshape(micro, rows, d)
    cot = cotangent.reshape(micro, rows, d)

    each = d // wide
    lane = jnp.arange(256) // 64
    ones = (lane[:, None] == lane[None, :]).astype(BF16)

    tiles = rows // TILE
    token = pl.BlockSpec((None, TILE, d), lambda m, t: (m, t, 0))
    whole = lambda shape: pl.BlockSpec(shape, lambda *_: (0,) * len(shape))
    fixed = lambda shape: pl.BlockSpec(
        shape, lambda *_: (0,) * len(shape), pipeline_mode=pl.Buffered(1)
    )
    packed = pl.BlockSpec((None, state_rows(), 128), lambda m, *_: (m, 0, 0))
    like = lambda dtype: jax.ShapeDtypeStruct((micro, rows, d), dtype)
    early_shape = packed_shape(9 * each, d)

    block = pl.BlockSpec((None, rows, d), lambda m: (m, 0, 0))
    count = rows // CHUNK
    states_spec = pl.BlockSpec((None, count, 2, 256, 256), lambda m: (m, 0, 0, 0, 0))
    during = lambda begin, *shape: pl.BlockSpec(
        (None,) + shape, lambda i: (jnp.clip(i - begin, 0, micro - 1),) + (0,) * len(shape)
    )
    anywhere = pl.BlockSpec(memory_space=pl.ANY)
    spread = lambda a: jax.ShapeDtypeStruct((wide,) + a.shape, BF16)
    dma = pltpu.SemaphoreType.DMA
    vectors = [a.reshape(1, -1) for a in (ln1_gain, ln1_bias, ln2_gain, ln2_bias, down_bias, up_bias)]
    state_shape = (micro, state_rows(), 128)
    (q, k, v, num, kc, states, state_in, w_qkv, w_out, w_up, w_down, vec) = pl.pallas_call(
        first_kernel,
        grid=(4 * micro,),
        in_specs=[small(), small(), fixed((micro, rows, d))] + [anywhere] * 4 + [whole(a.shape) for a in vectors] + [whole((256, 256))],
        out_specs=[during(micro * j, rows, d) for j in range(3)] + [during(3 * micro, rows, d)] * 2
        + [during(3 * micro, count, 4, 128, 128), whole(state_shape)]
        + [anywhere] * 4 + [whole((16, d))],
        out_shape=[like(BF16)] * 5 + [
            jax.ShapeDtypeStruct((micro, count, 4, 128, 128), BF16), jax.ShapeDtypeStruct(state_shape, F32),
            spread(qkv_weight), spread(out_weight), spread(up_weight), spread(down_weight),
            jax.ShapeDtypeStruct((16, d), F32),
        ],
        scratch_shapes=[pltpu.VMEM((3, wide, each, d), BF16)]
        + [pltpu.VMEM((micro, rows, d), BF16)] * 4
        + [
            pltpu.VMEM((4, 128, 128), F32), pltpu.VMEM((1, d), F32), pltpu.VMEM(state_shape, BF16), pltpu.VMEM((16, 128), BF16), pltpu.VMEM((wide, 16, 128), BF16),
            dma, dma((wide,)), dma((wide,)), dma((3,)),
        ]
        + running_scratch(micro // 2) * 2
        + gather_sems() * 6,
        compiler_params=pltpu.CompilerParams(
            dimension_semantics=("arbitrary",), vmem_limit_bytes=VMEM, collective_id=0, has_side_effects=True
        ),
        name="first",
    )(lens, off, x, qkv_weight, out_weight, up_weight, down_weight, *vectors, ones)
    w_qkv, w_out = w_qkv.reshape(d, 3 * d), w_out.reshape(d, d)
    w_up, w_down = w_up.reshape(d, ff), w_down.reshape(ff, d)

    result, g_middle, gnum, gden, use, grads, g_vec = pl.pallas_call(
        middle_kernel,
        grid=(micro, tiles),
        in_specs=[small(), small()] + [token] * 5 + [packed, whole((256, 256))] + [
            fixed((d, d)), whole((16, d)), fixed((d, ff)), fixed((ff, d)),
        ],
        out_specs=[token, token, token, token, packed, fixed((wide,) + early_shape), whole((16, d))],
        out_shape=[
            like(BF16), like(BF16), like(BF16), like(BF16), jax.ShapeDtypeStruct(state_shape, BF16),
            jax.ShapeDtypeStruct((wide,) + early_shape, BF16), jax.ShapeDtypeStruct((16, d), F32),
        ],
        scratch_shapes=[
            pltpu.VMEM((2, 256, 256), BF16), pltpu.VMEM((1, d), F32),
            pltpu.VMEM((2, 256, 256), F32), pltpu.VMEM((1, d), F32),
            pltpu.VMEM((d, d), F32), pltpu.VMEM((d, ff), F32), pltpu.VMEM((d, ff), F32),
            pltpu.VMEM((TILE, d), F32), pltpu.VMEM((TILE, d), F32), pltpu.VMEM((TILE, d), BF16),
            pltpu.VMEM((d, TILE), BF16), pltpu.VMEM((d, TILE), BF16),
        ],
        compiler_params=params(2),
        name="middle",
    )(lens, off, q, num, kc, x, cot, state_in, ones, w_out, vec, w_up, w_down)

    def first(*shape, buffers=2):
        at = lambda i: (jnp.minimum(i, micro - 1),) + (0,) * len(shape)
        return pl.BlockSpec((None,) + shape, at, pipeline_mode=pl.Buffered(buffers))

    spare = 2 if wide <= 8 else 1

    def walk(*begins, buffers=2):
        def at(i):
            j = 0
            for b in begins:
                j = j + jnp.where(i >= b, jnp.clip(i - b, 0, micro - 1) - j, 0)
            return (j, 0, 0)

        return pl.BlockSpec((None, rows, d), at, pipeline_mode=pl.Buffered(buffers))

    p1, p2, p4 = micro, 2 * micro, 3 * micro + 1
    part_shape = packed_shape(each, d)
    vector_shapes = [(1, each)] * 5 + [(1, 4 * each)]
    summed_shapes = [early_shape, part_shape, part_shape, part_shape, (16, 128)]
    result_shapes = [(each, 3 * d), (each, d), (each, ff), (4 * each, d)] + vector_shapes
    part, *summed = pl.pallas_call(
        last_kernel,
        grid=(4 * micro + 1,),
        in_specs=[small(), small(), first(rows, d, buffers=spare), walk(0, p1, p2, buffers=spare), walk(0, p1, buffers=spare)]
        + [first(rows, d, buffers=spare)] * 3 + [first(count, 4, 128, 128, buffers=spare), first(state_rows(), 128)]
        + [walk(p1, p4)] + [anywhere] * 2
        + [whole((16, d)), whole((256, 256)), whole((16, d)), fixed((d, 3 * d))],
        out_specs=[walk(p4)] + [fixed(s) for s in summed_shapes],
        out_shape=[like(BF16)] + [jax.ShapeDtypeStruct(s, BF16) for s in summed_shapes[:4]]
        + [jax.ShapeDtypeStruct((16, 128), F32)],
        scratch_shapes=[pltpu.VMEM((micro * rows, d), BF16)] * 3
        + [
            pltpu.VMEM((d, micro * rows), BF16), pltpu.VMEM((d, 3 * d), F32),
            pltpu.VMEM((4, 128, 128), F32), pltpu.VMEM((1, d), F32),
            pltpu.VMEM((16, d), F32), pltpu.VMEM((1, 3 * d), F32),
        ]
        + [pltpu.VMEM((wide,) + part_shape, BF16)] * 3
        + running_scratch(micro)
        + scatter_scratch(early_shape) + scatter_scratch(part_shape) * 3
        + vector_scratch(),
        compiler_params=pltpu.CompilerParams(
            dimension_semantics=("arbitrary",), vmem_limit_bytes=VMEM, collective_id=1, has_side_effects=True
        ),
        name="last",
    )(lens, off, q, k, v, gnum, gden, kc, states, state_in, x, use, grads, g_vec, ones, vec, w_qkv)
    grad_input, g_qkv, g_out, g_up, g_down, *g_vectors = pl.pallas_call(
        result_kernel,
        grid=(micro,),
        in_specs=[block, block] + [whole(s) for s in summed_shapes],
        out_specs=[block] + [whole(s) for s in result_shapes],
        out_shape=[like(F32)] + [jax.ShapeDtypeStruct(s, F32) for s in result_shapes],
        compiler_params=params(1),
        name="result",
    )(g_middle, part, *summed)
    piece = [a.reshape(-1) for a in g_vectors]
    return (
        result.reshape(block_in.shape),
        grad_input.reshape(block_in.shape),
        piece[0],
        piece[1],
        g_qkv,
        g_out,
        piece[2],
        piece[3],
        g_up,
        piece[5],
        g_down,
        piece[4],
    )


def solution(mesh):
    tokens = P(None, "dp", "wide", None)
    vector, matrix = P("wide"), P("wide", None)
    weights = (vector, vector, matrix, matrix, vector, vector, matrix, vector, matrix, vector)
    return jax.shard_map(
        per_device,
        mesh=mesh,
        in_specs=(tokens, tokens) + weights + (P(None, "dp", None),),
        out_specs=(tokens, tokens) + weights,
        check_vma=False,
    )
```

```python
import functools

import jax
import jax.numpy as jnp
from jax import lax
from jax.experimental import pallas as pl
from jax.experimental.pallas import tpu as pltpu
from jax.sharding import PartitionSpec as P

HEADS = 8
EPSILON = 1e-05
F32 = jnp.float32
BF16 = jnp.bfloat16
CHUNK = 128
TILE = 512
FF_TILE = 512
VMEM = 62 * 1024 * 1024


def nn(a, b):
    return lax.dot_general(a, b, (((1,), (0,)), ((), ())), preferred_element_type=F32)


def nt(a, b):
    return lax.dot_general(a, b, (((1,), (1,)), ((), ())), preferred_element_type=F32)


def rows_of(row, width):
    return jnp.concatenate([row] * (width // 128), axis=1)


def start_of(lens, m, place):
    start, end = jnp.zeros_like(place), 0
    for j in range(lens.shape[1]):
        end = end + lens[m, j]
        start = start + jnp.where(end <= place, lens[m, j], 0)
    return start


def place_rows(first, count):
    return first + lax.broadcasted_iota(jnp.int32, (count, 128), 0)


def flag(condition):
    return jnp.where(condition, 1.0, 0.0)


def normed(x):
    average = jnp.mean(x, axis=-1, keepdims=True)
    centred = x - average
    spread = jnp.mean(centred * centred, axis=-1, keepdims=True)
    scale = lax.rsqrt(spread + EPSILON)
    return centred * scale, scale


def norm_back(e, xhat, scale, gain):
    a = gain * e
    return scale * (
        a - jnp.mean(a, axis=-1, keepdims=True) - xhat * jnp.mean(a * xhat, axis=-1, keepdims=True)
    )


def feature(v):
    return jnp.where(v > 0.0, v + 1.0, jnp.exp(jnp.minimum(v, 0.0)))


def column_sum(a):
    return jnp.sum(a, axis=0, keepdims=True)


def by_group(fn, *arrays):
    return jnp.concatenate(
        [fn(g, *[a[:, 256 * g : 256 * g + 256] for a in arrays]) for g in range(2)], axis=1
    )


def lane_half(shape):
    return lax.broadcasted_iota(jnp.int32, shape, 1) < 64


def pack_state(state, norm, out):
    folded = [s + pltpu.roll(s, 64, 1) for s in state]
    half = lane_half((128, 128))
    for j in range(2):
        out[128 * j : 128 * j + 128, :] = jnp.where(half, folded[j], folded[2 + j]).astype(out.dtype)
    row = lax.broadcasted_iota(jnp.int32, (16, 128), 0)
    tail = jnp.zeros((16, 128), F32)
    for j in range(4):
        tail = jnp.where(row == j, norm[:, 128 * j : 128 * j + 128], tail)
    out[256:272, :] = tail.astype(out.dtype)
    if out.shape[0] > 272:
        out[272:, :] = jnp.zeros((out.shape[0] - 272, 128), out.dtype)


def unpack_pairs(packed, ones):
    half = lane_half((128, 128))
    mask = ones[0:128, 0:128].astype(F32)
    pairs = [None] * 4
    for j in range(2):
        z = packed[128 * j : 128 * j + 128, :]
        turned = pltpu.roll(z, 64, 1)
        pairs[j] = jnp.where(half, z, turned) * mask
        pairs[2 + j] = jnp.where(half, turned, z) * mask
    tail = packed[256:272, :]
    norm = jnp.concatenate([tail[j : j + 1, :] for j in range(4)], axis=1)
    return pairs, norm


def unpack_state(packed, ones):
    pairs, norm = unpack_pairs(packed, ones)
    zero = jnp.zeros((128, 128), BF16)
    groups = []
    for g in range(2):
        above = jnp.concatenate([pairs[2 * g].astype(BF16), zero], axis=1)
        below = jnp.concatenate([zero, pairs[2 * g + 1].astype(BF16)], axis=1)
        groups.append(jnp.concatenate([above, below], axis=0))
    return groups, norm


MESH = pl.DeviceIdType.MESH


def place():
    dp = lax.axis_index("dp")
    return lax.rem(dp, 2), dp // 2, lax.axis_index("wide"), lax.axis_size("dp") // 2, lax.axis_size("wide")


def others(count, fn):
    def body(o, carry):
        fn(o)
        return carry

    lax.fori_loop(1, count, body, 0)


def remote(src, dst, send, recv, dp, wide):
    return pltpu.make_async_remote_copy(
        src_ref=src, dst_ref=dst, send_sem=send, recv_sem=recv, device_id=(dp, wide), device_id_type=MESH
    )


def signal_all():
    core, y, me, ny, n = place()
    dp = 2 * y + core
    barrier = pltpu.get_barrier_semaphore()

    def signal(d, w):
        pl.semaphore_signal(barrier, inc=1, device_id=(d, w), device_id_type=MESH)

    others(n, lambda o: signal(dp, lax.rem(me + o, n)))
    others(2 * ny, lambda o: signal(lax.rem(dp + o, 2 * ny), me))


def wait_all():
    _, _, _, ny, n = place()
    pl.semaphore_wait(pltpu.get_barrier_semaphore(), n - 1 + 2 * ny - 1)


class Gather:
    def __init__(self, src, dst, sems):
        self.src, self.dst = src, dst
        self.near, self.send, self.recv, self.y_send, self.y_recv, self.c_send, self.c_recv = sems
        self.core, self.y, self.me, self.ny, self.n = place()
        self.dp = 2 * self.y + self.core
        each = src.shape[0]
        self.split = split_of(each)
        part = each // self.split
        if self.split == 1:
            self.rows, self.half = pl.ds(0, each), None
        else:
            at = self.core * (each // 2) + self.y * part
            self.rows = pl.ds(pl.multiple_of(at, part), part)
            self.half = pl.ds(pl.multiple_of(self.core * (each // 2), each // 2), each // 2)

    def own(self):
        return pltpu.make_async_copy(self.src.at[self.rows], self.dst.at[self.me, self.rows], self.near)

    def out(self, o):
        to = lax.rem(self.me + o, self.n)
        return remote(self.src.at[self.rows], self.dst.at[self.me, self.rows], self.send.at[o], self.recv.at[self.me], self.dp, to)

    def back(self, o):
        frm = lax.rem(self.me + o, self.n)
        part = self.dst.at[frm, self.rows]
        return remote(part, part, self.send.at[o], self.recv.at[frm], self.dp, frm)

    def start_wide(self):
        self.own().start()
        others(self.n, lambda o: self.out(o).start())

    def finish_wide(self):
        self.own().wait()
        others(self.n, lambda o: self.out(o).wait_send())
        others(self.n, lambda o: self.back(o).wait_recv())

    def along_y(self, o):
        part = self.dst.at[:, self.rows]
        to = lax.rem(self.y + o, self.ny)
        return remote(part, part, self.y_send.at[o], self.y_recv.at[self.y], 2 * to + self.core, self.me)

    def along_y_back(self, o):
        frm = lax.rem(self.y + o, self.ny)
        each = self.src.shape[0]
        part = each // self.split
        at = self.core * (each // 2) + frm * part
        ref = self.dst.at[:, pl.ds(pl.multiple_of(at, part), part)]
        return remote(ref, ref, self.y_send.at[o], self.y_recv.at[frm], 2 * frm + self.core, self.me)

    def start_y(self):
        if self.split > 1:
            others(self.ny, lambda o: self.along_y(o).start())

    def finish_y(self):
        if self.split > 1:
            others(self.ny, lambda o: self.along_y(o).wait_send())
            others(self.ny, lambda o: self.along_y_back(o).wait_recv())

    def cross(self):
        part = self.dst.at[:, self.half]
        return remote(part, part, self.c_send, self.c_recv, 2 * self.y + 1 - self.core, self.me)

    def cross_back(self):
        each = self.src.shape[0]
        at = (1 - self.core) * (each // 2)
        part = self.dst.at[:, pl.ds(pl.multiple_of(at, each // 2), each // 2)]
        return remote(part, part, self.c_send, self.c_recv, 2 * self.y + 1 - self.core, self.me)

    def start_core(self):
        if self.split > 1:
            self.cross().start()

    def finish_core(self):
        if self.split > 1:
            self.cross().wait_send()
            self.cross_back().wait_recv()


def split_of(each):
    count = lax.axis_size("dp")
    return count if each % (16 * count) == 0 else 1


def gather_sems():
    n, ny = lax.axis_size("wide"), lax.axis_size("dp") // 2
    dma = pltpu.SemaphoreType.DMA
    return [dma, dma((n,)), dma((n,)), dma((ny,)), dma((ny,)), dma, dma]


def packed_shape(rows, d):
    unit = 16 * lax.axis_size("dp")
    columns = d if rows % unit == 0 else 128
    rows = rows * (d // columns)
    return -(-rows // unit) * unit, columns


def put(block, at, piece):
    rows, d = piece.shape
    columns = block.shape[1]
    for b in range(d // columns):
        begin = at * (d // columns) + rows * b
        block[begin : begin + rows, :] = piece[:, columns * b : columns * b + columns]


def fill(block, rows, d):
    used = rows * (d // block.shape[1])
    if block.shape[0] > used:
        block[used:, :] = jnp.zeros((block.shape[0] - used, block.shape[1]), block.dtype)


def get(block, at, rows, d):
    columns = block.shape[1]
    begin = at * (d // columns)
    return jnp.concatenate(
        [block[begin + rows * b : begin + rows * b + rows, :] for b in range(d // columns)], axis=1
    )


class Scatter:
    def __init__(self, src, refs):
        self.src = src
        (self.half, self.got_core, self.got_y, self.got_wide, self.out, self.near, self.c_sem, self.y_send,
         self.y_recv, self.w_send, self.w_recv, self.b_send, self.b_recv) = refs
        self.core, self.y, self.me, self.ny, self.n = place()
        self.dp = 2 * self.y + self.core
        self.rows = self.out.shape[0]
        self.each = self.rows // (2 * self.ny)
        self.partner = 2 * self.y + 1 - self.core
        self.part = self.got_core.at[:, 0 : self.each]

    def half_rows(self, core):
        return pl.ds(pl.multiple_of(core * (self.rows // 2), self.rows // 2), self.rows // 2)

    def y_rows(self, y):
        return pl.ds(pl.multiple_of(y * self.each, self.each), self.each)

    def own_rows(self, y):
        at = self.core * (self.rows // 2) + y * self.each
        return pl.ds(pl.multiple_of(at, self.each), self.each)

    def load(self):
        return pltpu.make_async_copy(self.src.at[:, self.half_rows(self.core)], self.half, self.near)

    def cross(self):
        return remote(
            self.src.at[:, self.half_rows(1 - self.core)], self.got_core, self.c_sem.at[0], self.c_sem.at[1], self.partner, self.me
        )

    def start1(self):
        self.cross().start()
        self.load().start()

    def along_y(self, o):
        to = lax.rem(self.y + o, self.ny)
        return remote(
            self.half.at[:, self.y_rows(to)], self.got_y.at[o - 1], self.y_send.at[o], self.y_recv.at[o],
            2 * to + self.core, self.me,
        )

    def finish1_start2(self):
        self.load().wait()
        self.cross().wait()

        def add(w, carry):
            self.half[w] = (self.half[w].astype(F32) + self.got_core[w].astype(F32)).astype(BF16)
            return carry

        lax.fori_loop(0, self.n, add, 0)
        others(self.ny, lambda o: self.along_y(o).start())

    def along_wide(self, o):
        to = lax.rem(self.me + o, self.n)
        return remote(self.part.at[to], self.got_wide.at[o - 1], self.w_send.at[o], self.w_recv.at[o], self.dp, to)

    def finish2_start3(self):
        others(self.ny, lambda o: self.along_y(o).wait())

        def add(w, carry):
            total = self.half[w, self.y_rows(self.y)].astype(F32)
            for o in range(self.ny - 1):
                total = total + self.got_y[o, w].astype(F32)
            self.part[w] = total.astype(BF16)
            return carry

        lax.fori_loop(0, self.n, add, 0)
        others(self.n, lambda o: self.along_wide(o).start())

    def back(self, o, wait=False):
        other = lax.rem(self.dp + o, 2 * self.ny)
        slot = other if wait else self.dp
        at = lax.rem(slot, 2) * (self.rows // 2) + (slot // 2) * self.each
        ref = self.out.at[pl.ds(pl.multiple_of(at, self.each), self.each)]
        return remote(ref, ref, self.b_send.at[o], self.b_recv.at[slot], other, self.me)

    def finish3_start4(self):
        others(self.n, lambda o: self.along_wide(o).wait())
        total = self.part[self.me].astype(F32)
        total = lax.fori_loop(0, self.n - 1, lambda o, t: t + self.got_wide[o].astype(F32), total)
        self.out[self.own_rows(self.y)] = total.astype(BF16)
        others(2 * self.ny, lambda o: self.back(o).start())

    def finish4(self):
        others(2 * self.ny, lambda o: self.back(o).wait_send())
        others(2 * self.ny, lambda o: self.back(o, True).wait_recv())


def scatter_scratch(shape):
    rows, d = shape
    n, dp = lax.axis_size("wide"), lax.axis_size("dp")
    ny, part = dp // 2, rows // dp
    dma = pltpu.SemaphoreType.DMA
    return [
        pltpu.VMEM((n, rows // 2, d), BF16),
        pltpu.VMEM((n, rows // 2, d), BF16),
        pltpu.VMEM((ny - 1, n, part, d), BF16),
        pltpu.VMEM((n - 1, part, d), BF16),
        pltpu.VMEM((rows, d), BF16),
        dma, dma((2,)), dma((ny,)), dma((ny,)), dma((n,)), dma((n,)), dma((dp,)), dma((dp,)),
    ]


class VectorSum:
    def __init__(self, refs):
        self.tiles, self.got_core, self.got_y, self.got_wide, self.c_sem, self.y_send, self.y_recv, self.w_send, self.w_recv = refs
        self.core, self.y, self.me, self.ny, self.n = place()
        self.dp = 2 * self.y + self.core

    def cross(self):
        return remote(self.tiles, self.got_core, self.c_sem.at[0], self.c_sem.at[1], 2 * self.y + 1 - self.core, self.me)

    def along_y(self, o):
        to = lax.rem(self.y + o, self.ny)
        return remote(self.tiles, self.got_y.at[o - 1], self.y_send.at[o], self.y_recv.at[o], 2 * to + self.core, self.me)

    def along_wide(self, o):
        to = lax.rem(self.me + o, self.n)
        return remote(self.tiles.at[to], self.got_wide.at[o - 1], self.w_send.at[o], self.w_recv.at[o], self.dp, to)

    def start1(self):
        self.cross().start()

    def finish1_start2(self):
        self.cross().wait()
        self.tiles[...] = self.tiles[...] + self.got_core[...]
        others(self.ny, lambda o: self.along_y(o).start())

    def finish2_start3(self):
        others(self.ny, lambda o: self.along_y(o).wait())
        total = self.tiles[...]
        for o in range(self.ny - 1):
            total = total + self.got_y[o]
        self.tiles[...] = total
        others(self.n, lambda o: self.along_wide(o).start())

    def finish3(self):
        others(self.n, lambda o: self.along_wide(o).wait())
        return lax.fori_loop(0, self.n - 1, lambda o, t: t + self.got_wide[o], self.tiles[self.me])


def vector_scratch():
    n, ny = lax.axis_size("wide"), lax.axis_size("dp") // 2
    dma = pltpu.SemaphoreType.DMA
    return [
        pltpu.VMEM((n, 16, 128), F32),
        pltpu.VMEM((n, 16, 128), F32),
        pltpu.VMEM((ny - 1, n, 16, 128), F32),
        pltpu.VMEM((n - 1, 16, 128), F32),
        dma((2,)), dma((ny,)), dma((ny,)), dma((n,)), dma((n,)),
    ]


def owner_tiles(rows, tiles, each):
    n = tiles.shape[0]
    d = each * n
    per = 4 * each
    row = lax.broadcasted_iota(jnp.int32, (16, 128), 0)
    lane = lax.broadcasted_iota(jnp.int32, (16, 128), 1)
    blocks = [rows[:, 128 * j : 128 * j + 128] for j in range(d // 128)]

    def turned(a, by, axis):
        by = by % a.shape[axis]
        return pltpu.roll(a, by, axis) if by else a

    for w in range(n):
        at = each * w
        tile = jnp.where(row < 5, turned(blocks[at // 128], -(at % 128), 1), 0.0)
        for r in range(4):
            at = per * w + each * r
            from_row, begin = 5 + at // d, at % d
            moved = turned(turned(blocks[begin // 128], -(begin % 128), 1), 5 + r - from_row, 0)
            tile = jnp.where(row == 5 + r, moved, tile)
        tiles[w] = jnp.where(lane < each, tile, 0.0)


HIGH = 4


def low_count():
    return lax.axis_size("wide") // HIGH


def state_rows():
    unit = 16 * low_count()
    return -(-272 // unit) * unit


class Running:
    def __init__(self, own, upward, refs):
        self.own, self.upward = own, upward
        (self.slots, self.group, self.high, self.mine, self.spread, self.result, self.near, self.send1, self.recv1,
         self.send2, self.recv2, self.send3, self.recv3) = refs
        _, _, self.me, _, _ = place()
        self.dp = lax.axis_index("dp")
        self.lo = low_count()
        self.h, self.l = self.me // self.lo, lax.rem(self.me, self.lo)
        self.part = state_rows() // self.lo

    def slice(self, l):
        return pl.ds(pl.multiple_of(l * self.part, self.part), self.part)

    def copy1(self, o, back=False):
        other = lax.rem(self.l + o, self.lo)
        slot = other if back else self.l
        return remote(self.own, self.slots.at[slot], self.send1.at[o], self.recv1.at[slot], self.dp, self.h * self.lo + other)

    def near1(self):
        return pltpu.make_async_copy(self.own, self.slots.at[self.l], self.near.at[0])

    def start1(self):
        self.near1().start()
        others(self.lo, lambda o: self.copy1(o).start())

    def before(self, a, b):
        return a < b if self.upward else a > b

    def finish1_start2(self):
        self.near1().wait()
        others(self.lo, lambda o: self.copy1(o).wait_send())
        others(self.lo, lambda o: self.copy1(o, True).wait_recv())
        every = jnp.zeros(self.own.shape, F32)
        inner = every
        for l in range(self.lo):
            part = self.slots[l].astype(F32)
            every = every + part
            inner = inner + jnp.where(self.before(l, self.l), part, 0.0)
        self.group[...] = every.astype(BF16)
        self.result[...] = inner

        def send(o):
            other = lax.rem(self.h + o, HIGH)

            @pl.when(self.before(self.h, other))
            def _():
                self.copy2(o).start()

        others(HIGH, send)

    def copy2(self, o, back=False):
        other = lax.rem(self.h + o, HIGH)
        slot = other if back else self.h
        return remote(
            self.group.at[:, self.slice(self.l)], self.high.at[slot], self.send2.at[o], self.recv2.at[slot],
            self.dp, other * self.lo + self.l,
        )

    def finish2_start3(self):
        def wait(o):
            other = lax.rem(self.h + o, HIGH)

            @pl.when(self.before(self.h, other))
            def _():
                self.copy2(o).wait_send()

            @pl.when(self.before(other, self.h))
            def _():
                self.copy2(o, True).wait_recv()

        others(HIGH, wait)
        total = jnp.zeros(self.mine.shape, F32)
        for h in range(HIGH):
            total = total + jnp.where(self.before(h, self.h), self.high[h].astype(F32), 0.0)
        self.mine[...] = total.astype(BF16)
        self.near3().start()
        others(self.lo, lambda o: self.copy3(o).start())

    def near3(self):
        return pltpu.make_async_copy(self.mine, self.spread.at[self.l], self.near.at[1])

    def copy3(self, o, back=False):
        other = lax.rem(self.l + o, self.lo)
        slot = other if back else self.l
        return remote(self.mine, self.spread.at[slot], self.send3.at[o], self.recv3.at[slot], self.dp, self.h * self.lo + other)

    def finish3(self):
        self.near3().wait()
        others(self.lo, lambda o: self.copy3(o).wait_send())
        others(self.lo, lambda o: self.copy3(o, True).wait_recv())
        for l in range(self.lo):
            rows = slice(l * self.part, (l + 1) * self.part)
            self.result[:, rows] = self.result[:, rows] + self.spread[l].astype(F32)


def running_scratch(micro):
    lo, rows = low_count(), state_rows()
    dma = pltpu.SemaphoreType.DMA
    return [
        pltpu.VMEM((lo, micro, rows, 128), BF16),
        pltpu.VMEM((micro, rows, 128), BF16),
        pltpu.VMEM((HIGH, micro, rows // lo, 128), BF16),
        pltpu.VMEM((micro, rows // lo, 128), BF16),
        pltpu.VMEM((lo, micro, rows // lo, 128), BF16),
        pltpu.VMEM((micro, rows, 128), F32),
        dma((2,)), dma((lo,)), dma((lo,)), dma((HIGH,)), dma((HIGH,)), dma((lo,)), dma((lo,)),
    ]


def vector_tile(vectors, each):
    row = lax.broadcasted_iota(jnp.int32, (16, 128), 0)

    def padded(piece):
        return jnp.concatenate([piece.astype(F32), jnp.zeros((1, 128 - each), F32)], axis=1)

    pieces = [padded(v[...]) for v in vectors[:5]]
    hidden = vectors[5][...]
    pieces += [padded(hidden[:, each * r : each * r + each]) for r in range(hidden.shape[1] // each)]
    tile = jnp.zeros((16, 128), F32)
    for j, piece in enumerate(pieces):
        tile = jnp.where(row == j, piece, tile)
    return tile.astype(BF16)


def spread_vectors(slots, out, each):
    n = slots.shape[0]
    d = each * n
    per = 4 * each
    row = lax.broadcasted_iota(jnp.int32, (16, 128), 0)
    blocks = [jnp.zeros((16, 128), F32) for _ in range(d // 128)]
    for w in range(n):
        tile = slots[w].astype(F32)
        at = each * w
        moved = pltpu.roll(tile, at % 128, 1) if at % 128 else tile
        blocks[at // 128] = blocks[at // 128] + jnp.where(row < 5, moved, 0.0)
        for r in range(4):
            at = per * w + each * r
            to_row, lane = 5 + at // d, at % d
            only = jnp.where(row == 5 + r, tile, 0.0)
            moved = pltpu.roll(only, lane % 128, 1) if lane % 128 else only
            if to_row != 5 + r:
                moved = pltpu.roll(moved, (to_row - 5 - r) % 16, 0)
            blocks[lane // 128] = blocks[lane // 128] + moved
    for j, block in enumerate(blocks):
        out[:, 128 * j : 128 * j + 128] = block


def first_kernel(lens, off, x, *refs):
    (s_qkv, s_out, s_up, s_down, v0, v1, v2, v3, v4, v5, ones,
     q_out, k_out, v_out, num_out, kc_out, states_out, state_in, w_qkv, w_out, w_up, w_down, vec_out,
     w_ref, h_all, q_all, k_all, v_all, state, norm, local, tile, tiles_ref, tile_near, tile_send, tile_recv,
     save_sem, *rest) = refs
    each = s_qkv.shape[0]
    micro, rows, d = x.shape
    half = micro // 2
    running = []
    for j in range(2):
        running.append(Running(local.at[half * j : half * j + half], True, rest[:13]))
        rest = rest[13:]
    jobs = []
    for j in range(3):
        jobs.append(Gather(s_qkv.at[:, d * j : d * j + d], w_ref.at[j], rest[7 * j : 7 * j + 7]))
    pieces = [(s_out, w_out)]
    for src, dst in ((s_up, w_up), (s_down, w_down)):
        columns = src.shape[1] // 2
        pieces += [(src.at[:, c : c + columns], dst.at[:, :, c : c + columns]) for c in (0, columns)]
    for j, (src, dst) in enumerate(pieces):
        jobs.append(Gather(src, dst, rest[21 + 7 * j : 28 + 7 * j]))
    i = pl.program_id(0)
    core, y, me, ny, n = place()
    dp = 2 * y + core

    def vec_copy(o, back=False):
        other = lax.rem(me + o, n)
        slot = other if back else me
        return remote(tile, tiles_ref.at[slot], tile_send.at[o], tile_recv.at[slot], dp, other)

    def vec_near():
        return pltpu.make_async_copy(tile, tiles_ref.at[me], tile_near)

    def save(j):
        return pltpu.make_async_copy(w_ref.at[j], w_qkv.at[:, :, d * j : d * j + d], save_sem.at[j])

    def weights(j):
        return w_ref[j].reshape(d, d)

    @pl.when(i == 0)
    def _():
        signal_all()
        tile[...] = vector_tile((v0, v1, v2, v3, v4, v5), each)
        wait_all()
        vec_near().start()
        others(n, lambda o: vec_copy(o).start())
        for job in jobs[:3]:
            job.start_wide()
        vec_near().wait()
        others(n, lambda o: vec_copy(o).wait_send())
        others(n, lambda o: vec_copy(o, True).wait_recv())
        spread_vectors(tiles_ref, vec_out, each)

        def norm_micro(m, carry):
            xhat, _ = normed(x[m].astype(F32))
            h_all[m] = (xhat * vec_out[0:1, :] + vec_out[1:2, :]).astype(BF16)
            return carry

        lax.fori_loop(0, micro // 2, norm_micro, 0)
        jobs[0].finish_wide()
        jobs[0].start_y()
        lax.fori_loop(micro // 2, micro, norm_micro, 0)
        for job in jobs[1:3]:
            job.finish_wide()
            job.start_y()
        for job in jobs[3:]:
            job.start_wide()
        jobs[0].finish_y()
        jobs[0].start_core()
        jobs[0].finish_core()

    @pl.when(i == 1)
    def _():
        jobs[1].finish_y()
        jobs[1].start_core()

    @pl.when(i == 2)
    def _():
        jobs[2].finish_y()
        jobs[2].start_core()

    @pl.when(i < micro)
    def _():
        q = feature(nn(h_all[i], weights(0))).astype(BF16)
        q_out[...] = q
        q_all[i] = q

    @pl.when(i == micro)
    def _():
        jobs[1].finish_core()

    @pl.when((i >= micro) & (i < 2 * micro))
    def _():
        m = i - micro
        k = feature(nn(h_all[m], weights(1))).astype(BF16)
        k_out[...] = k
        k_all[m] = k

    @pl.when(i == 2 * micro)
    def _():
        jobs[2].finish_core()
        for j in range(3):
            save(j).start()

    @pl.when((i >= 2 * micro) & (i < 3 * micro))
    def _():
        m = i - 2 * micro
        v = nn(h_all[m], weights(2)).astype(BF16)
        v_out[...] = v
        v_all[m] = v
        base = off[0]
        final = start_of(lens, m, base + rows - 1)
        last = flag(start_of(lens, m, place_rows(base, rows)) == final)
        k_last = k_all[m] * rows_of(last.astype(BF16), d)
        k_turned = k_last.T
        mask = ones[0:128, 0:128].astype(F32)
        parts = [nn(k_turned[128 * p : 128 * p + 128, :], v[:, 128 * p : 128 * p + 128]) * mask for p in range(4)]
        pack_state(parts, column_sum(k_last.astype(F32)), local.at[m])

    @pl.when(i == 2 * micro + half - 1)
    def _():
        running[0].start1()

    @pl.when(i == 3 * micro - 1)
    def _():
        running[1].start1()

    def pass_on(step, *parts):
        @pl.when(i == step)
        def _():
            for job in parts:
                job.finish_wide()
                job.start_y()

    def cross_over(step, *parts):
        @pl.when(i == step)
        def _():
            for job in parts:
                job.finish_y()
                job.start_core()

    pass_on(micro + 1, jobs[3], jobs[4])
    pass_on(2 * micro + 1, jobs[5])
    pass_on(3 * micro, jobs[6])

    @pl.when(i == 3 * micro)
    def _():
        running[0].finish1_start2()

    cross_over(3 * micro, jobs[3], jobs[4])
    pass_on(3 * micro + 1, jobs[7])

    @pl.when(i == 3 * micro + 1)
    def _():
        running[1].finish1_start2()

    cross_over(3 * micro + 2, jobs[5], jobs[6])

    @pl.when(i == 3 * micro + 2)
    def _():
        running[0].finish2_start3()

    @pl.when(i == 3 * micro + 3)
    def _():
        running[1].finish2_start3()

    cross_over(3 * micro + 3, jobs[7])

    @pl.when(i >= 3 * micro)
    def _():
        m = i - 3 * micro
        attend(lens, m, off[0], q_all.at[m], k_all.at[m], v_all.at[m], ones, num_out, kc_out, states_out, state, norm)

    @pl.when(i == 4 * micro - 1)
    def _():
        for j in range(2):
            running[j].finish3()
            state_in[half * j : half * j + half] = running[j].result[...]
        for job in jobs[3:]:
            job.finish_core()
        for j in range(3):
            save(j).wait()


def chunk_masks(lens, m, begin, size):
    by_row = start_of(lens, m, place_rows(begin, size))
    lane = begin + lax.broadcasted_iota(jnp.int32, (8, size), 1)
    by_column = start_of(lens, m, lane)[0:1, :]
    final = start_of(lens, m, begin + size - 1)
    return by_row, by_column, final


def pair_mask():
    return flag(lane_half((16, 128))).astype(BF16)[0:1, :]


def split_pair(a, low, high):
    return jnp.concatenate([a * low, a * high], axis=0)


def attend(lens, m, base, q_ref, k_ref, v_ref, ones, num_out, kc_out, states_out, state, norm):
    rows, d = q_ref.shape
    size = CHUNK
    state[...] = jnp.zeros_like(state)
    norm[...] = jnp.zeros_like(norm)
    half = lane_half((1, 128))
    low = flag(half).astype(BF16)
    high = flag(jnp.logical_not(half)).astype(BF16)

    def step(c, carry):
        at = pl.ds(pl.multiple_of(c * size, size), size)
        begin = base + c * size
        q, k, v = q_ref[at, :], k_ref[at, :], v_ref[at, :]
        by_row, by_column, final = chunk_masks(lens, m, begin, size)
        places = lax.broadcasted_iota(jnp.int32, (size, size), 0)
        columns = lax.broadcasted_iota(jnp.int32, (size, size), 1)
        allowed = flag((places >= columns) & (by_row[:, :size] == by_column)).astype(BF16)
        allowed2 = jnp.concatenate([allowed, allowed], axis=1)
        seen = flag(by_row < begin)
        last = flag(by_row == final).astype(BF16)
        keep = jnp.where(final < begin, 1.0, 0.0)
        kc_out[at, :] = (nn(allowed, k) + rows_of(seen, d) * norm[...]).astype(BF16)
        q_seen = q * rows_of(seen.astype(BF16), d)
        for p in range(4):
            cut = slice(128 * p, 128 * p + 128)
            s = nt(q[:, cut], split_pair(k[:, cut], low, high)).astype(BF16) * allowed2
            inside = nn(s, split_pair(v[:, cut], low, high))
            held = state[p].astype(BF16)
            states_out[c, p] = held
            before = nn(q_seen[:, cut], held)
            num_out[at, cut] = (inside + before).astype(BF16)
        k_last = k * rows_of(last, d)
        k_turned = k_last.T
        mask = ones[0:128, 0:128].astype(F32)
        for p in range(4):
            cut = slice(128 * p, 128 * p + 128)
            state[p] = keep * state[p] + nn(k_turned[cut, :], v[:, cut]) * mask
        norm[...] = keep * norm[...] + column_sum(k_last.astype(F32))
        return carry

    lax.fori_loop(0, rows // size, step, 0, unroll=8)


def middle_kernel(
    lens, off, q_ref, num_ref, kc_ref, x_ref, cot_ref, state_in, ones,
    w_out, vec, w_up, w_down,
    block_out, gm_out, gnum_out, gden_out, use_out, grads_up, grads_down, g_vec,
    groups, norm, use, use_norm, acc_out, acc_up, acc_down, total, e_total, h2_ref, h2t_ref, ct_ref,
):
    m, t, tiles = pl.program_id(0), pl.program_id(1), pl.num_programs(1)
    rows, d = x_ref.shape
    first = (m == 0) & (t == 0)
    final = (m == pl.num_programs(0) - 1) & (t == tiles - 1)
    base = off[0]

    @pl.when(first)
    def _():
        acc_out[...] = jnp.zeros_like(acc_out)
        acc_up[...] = jnp.zeros_like(acc_up)
        acc_down[...] = jnp.zeros_like(acc_down)
        g_vec[...] = jnp.zeros_like(g_vec)

    @pl.when(t == 0)
    def _():
        parts, z = unpack_state(state_in[...], ones[...])
        for g in range(2):
            groups[g] = parts[g]
        norm[...] = z
        use[...] = jnp.zeros_like(use)
        use_norm[...] = jnp.zeros_like(use_norm)

    gain, bias, down_bias = vec[2:3, :], vec[3:4, :], vec[4:5, :]
    q = q_ref[...]
    seen = flag(start_of(lens, m, place_rows(base + t * rows, rows)) < base)
    q_seen = q * rows_of(seen.astype(BF16), d)
    num = num_ref[...].astype(F32) + by_group(lambda g, a: nn(a, groups[g]), q_seen)
    kc = kc_ref[...].astype(F32) + rows_of(seen, d) * norm[...]
    den = by_group(lambda g, a: nn(a, ones[...]), (q.astype(F32) * kc).astype(BF16))
    over = 1.0 / den
    mixed = (num * over).astype(BF16)
    middle = x_ref[...].astype(F32) + nn(mixed, w_out[...])
    xhat, scale = normed(middle)
    h2 = (xhat * gain + bias).astype(BF16)
    h2_ref[...] = h2
    h2t_ref[...] = h2.T
    ct_ref[...] = cot_ref[...].T
    total[...] = middle + down_bias
    e_total[...] = jnp.zeros_like(e_total)

    def ffn(f, carry):
        cut = pl.ds(pl.multiple_of(f * FF_TILE, FF_TILE), FF_TILE)
        hidden = nn(h2_ref[...], w_up[:, cut]) + vec[pl.ds(5 + f, 1), :]
        pulled = nt(cot_ref[...], w_down[cut, :])
        square = hidden * hidden
        c0, c1 = 0.7978845608028654, 0.044715
        th = jnp.tanh(hidden * (c0 + (c0 * c1) * square))
        half_up = 0.5 + 0.5 * th
        active = (hidden * half_up).astype(BF16)
        slope = half_up + (0.5 * hidden) * (1.0 - th * th) * (c0 + (3.0 * c0 * c1) * square)
        g_hidden = slope * pulled
        g_low = g_hidden.astype(BF16)
        total[...] += nn(active, w_down[cut, :])
        e_total[...] += nt(g_low, w_up[:, cut])
        acc_down[:, cut] += nn(ct_ref[...], active)
        acc_up[:, cut] += nn(h2t_ref[...], g_low)
        g_vec[pl.ds(5 + f, 1), :] += column_sum(g_hidden)
        return carry

    lax.fori_loop(0, w_up.shape[1] // FF_TILE, ffn, 0, unroll=True)
    block_out[...] = total[...].astype(BF16)
    e = e_total[...]
    cot = cot_ref[...].astype(F32)
    g_middle = cot + norm_back(e, xhat, scale, gain)
    gm_out[...] = g_middle.astype(BF16)
    g_vec[2:3, :] += column_sum(e * xhat)
    g_vec[3:4, :] += column_sum(e)
    g_vec[4:5, :] += column_sum(cot)
    branch = g_middle.astype(BF16)
    acc_out[...] += nn(mixed.T, branch)
    g_mixed = nt(branch, w_out[...])
    gnum = (g_mixed * over).astype(BF16)
    gnum_out[...] = gnum
    gden = -by_group(lambda g, a: nn(a, ones[...]), (g_mixed * num).astype(BF16)) * (over * over)
    gden_out[...] = gden.astype(BF16)
    turned = q_seen.T
    for g in range(2):
        cut = slice(256 * g, 256 * g + 256)
        use[g] += nn(turned[cut, :], gnum[:, cut])
    use_norm[...] += column_sum(q_seen.astype(F32) * gden)

    @pl.when(t == tiles - 1)
    def _():
        mask = ones[0:128, 0:128].astype(F32)
        pack_state([use[p // 2][128 * (p % 2) : 128 * (p % 2) + 128, 128 * (p % 2) : 128 * (p % 2) + 128] * mask for p in range(4)], use_norm[...], use_out)

    @pl.when(final)
    def _():
        n = grads_up.shape[0]
        each = d // n
        down = acc_down[...].astype(BF16).T
        for w in range(n):
            at = slice(each * w, each * w + each)
            for j in range(4):
                put(grads_up.at[w], each * j, acc_up[at, d * j : d * j + d].astype(BF16))
            put(grads_up.at[w], 4 * each, acc_out[at, :].astype(BF16))
            fill(grads_up.at[w], 5 * each, d)
            put(grads_down.at[w], 0, down[4 * each * w : 4 * each * w + 4 * each, :])
            fill(grads_down.at[w], 4 * each, d)


def attend_back(
    lens, m, base, lead, q_ref, k_ref, v_ref, gnum_ref, gden_ref, kc_ref, states, state_in, ones,
    gq_out, dk_out, dv_out, after, after_norm,
):
    rows, d = q_ref.shape
    size = CHUNK
    count = rows // size
    half = lane_half((1, 128))
    low = flag(half).astype(BF16)
    high = flag(jnp.logical_not(half)).astype(BF16)
    pairs_in, norm_in = unpack_pairs(state_in[...], ones[...])

    def step(i, carry):
        c = count - 1 - i
        at = pl.ds(pl.multiple_of(c * size, size), size)
        begin = lead + c * size
        q, k, v, gnum = q_ref[at, :], k_ref[at, :], v_ref[at, :], gnum_ref[at, :]
        gden = gden_ref[at, :].astype(F32)
        by_row, by_column, final = chunk_masks(lens, m, begin, size)
        places = lax.broadcasted_iota(jnp.int32, (size, size), 0)
        columns = lax.broadcasted_iota(jnp.int32, (size, size), 1)
        same = by_row[:, :size] == by_column
        allowed = flag((places >= columns) & same).astype(BF16)
        allowed2 = jnp.concatenate([allowed, allowed], axis=1)
        turned = flag((places <= columns) & same).astype(BF16)
        turned2 = jnp.concatenate([turned, turned], axis=1)
        seen = rows_of(flag(by_row < begin).astype(BF16), d)
        seen_all = flag(by_row < base)
        last = flag(by_row == final)
        keep = jnp.where(final < begin, 1.0, 0.0)
        last_low = rows_of(last.astype(BF16), d)
        carried = jnp.where((begin == base) | (start_of(lens, m, begin - 1) < base), 1.0, 0.0)
        gnum_seen = gnum * seen
        k_last, v_last = k * last_low, v * last_low
        gden_q = gden * q.astype(F32)
        dk_den = nn(turned, gden_q.astype(BF16)) + rows_of(last, d) * after_norm[...]
        dq_den = gden * (kc_ref[at, :].astype(F32) + rows_of(seen_all, d) * norm_in)
        for p in range(4):
            cut = slice(128 * p, 128 * p + 128)
            held = (states[c, p].astype(F32) + carried * pairs_in[p]).astype(BF16)
            g_after = after[p].astype(BF16)
            qp, kp, vp, gp = q[:, cut], k[:, cut], v[:, cut], gnum[:, cut]
            q2, k2 = split_pair(qp, low, high), split_pair(kp, low, high)
            v2, g2 = split_pair(vp, low, high), split_pair(gp, low, high)
            s_turned = nt(kp, q2).astype(BF16) * turned2
            gs_turned = nt(vp, g2).astype(BF16) * turned2
            gs = nt(gp, v2).astype(BF16) * allowed2
            dq = nn(gs, k2) + nt(gnum_seen[:, cut], held) + dq_den[:, cut]
            gq_out[at, cut] = (jnp.minimum(qp.astype(F32), 1.0) * dq).astype(BF16)
            dk = nn(gs_turned, q2) + nt(v_last[:, cut], g_after) + dk_den[:, cut]
            dk_out[at, cut] = dk.astype(BF16)
            dv = nn(s_turned, g2) + nn(k_last[:, cut], g_after)
            dv_out[at, cut] = dv.astype(BF16)
        q_turned = (q * seen).T
        mask = ones[0:128, 0:128].astype(F32)
        for p in range(4):
            cut = slice(128 * p, 128 * p + 128)
            after[p] = keep * after[p] + nn(q_turned[cut, :], gnum[:, cut]) * mask
        after_norm[...] = keep * after_norm[...] + column_sum(gden_q * seen.astype(F32))
        return carry

    lax.fori_loop(0, count, step, 0, unroll=4)


def last_kernel(lens, off, *refs):
    (q_ref, k_half, v_half, gnum_ref, gden_ref, kc_ref, states, state_in, k_ref, v_ref, x_ref,
     use, grads_up, grads_down, g_vec, ones, vec, w,
     gx_out, up_out, down_out, k_out, v_out, q_out, vector_out,
     gq_all, dk_all, dv_all, h1t_all, acc, after, after_norm, sums, shares, src_k, src_v, src_q, *rest) = refs
    micro = use.shape[0]
    rows, d = k_ref.shape
    part_rows = q_ref.shape[0]
    halves = rows // part_rows
    n = src_q.shape[0]
    each = d // n
    running = Running(use, False, rest[:13])
    rest = rest[13:]
    jobs = [
        Scatter(src, rest[13 * j : 13 * j + 13]) for j, src in enumerate((grads_up, grads_down, src_k, src_v, src_q))
    ]
    of_up, of_down, of_k, of_v, of_q = jobs
    vector = VectorSum(rest[65:])
    i = pl.program_id(0)
    base = off[0]
    p1 = halves * micro
    p2, p3 = p1 + micro, p1 + 2 * micro
    p4, end = p3 + 1, p3 + 1 + micro

    def at_step(step, *actions):
        @pl.when(i == step)
        def _():
            for action in actions:
                action()

    @pl.when(i == 0)
    def _():
        signal_all()
        wait_all()
        of_up.start1()
        of_down.start1()
        running.start1()
        acc[...] = jnp.zeros_like(acc)
        shares[...] = jnp.zeros_like(shares)

    at_step(1, of_up.finish1_start2, of_down.finish1_start2)
    at_step(2, running.finish1_start2)
    at_step(p1 - 2, of_up.finish2_start3)
    at_step(p1 - 1, running.finish2_start3)
    at_step(p1, running.finish3, of_down.finish2_start3)
    at_step(p1 + 3, of_up.finish3_start4)
    at_step(p2 + 1, of_up.finish4, of_k.finish1_start2)
    at_step(p4, of_down.finish3_start4)
    at_step(p4 + 1, of_k.finish3_start4, of_v.finish2_start3, vector.finish1_start2)
    at_step(p4 + 2, of_down.finish4, of_q.finish2_start3)
    at_step(p4 + 3, of_k.finish4, vector.finish2_start3)

    @pl.when(i < p1)
    def _():
        m, t = i // halves, halves - 1 - lax.rem(i, halves)

        @pl.when(t == halves - 1)
        def _():
            after[...] = jnp.zeros_like(after)
            after_norm[...] = jnp.zeros_like(after_norm)

        lead = t * part_rows
        at = pl.ds(pl.multiple_of(m * rows + lead, part_rows), part_rows)
        attend_back(
            lens, m, base, base + lead, q_ref, k_half, v_half, gnum_ref, gden_ref, kc_ref, states, state_in, ones,
            gq_all.at[at], dk_all.at[at], dv_all.at[at], after, after_norm,
        )

    def block(m):
        final = start_of(lens, m, base + rows - 1)
        last = flag(start_of(lens, m, place_rows(base, rows)) == final)
        groups, norm = unpack_state(running.result[m], ones[...])
        return last, rows_of(last.astype(BF16), d), groups, norm

    @pl.when((i >= p1) & (i < p2))
    def _():
        m = i - p1
        at = pl.ds(pl.multiple_of(m * rows, rows), rows)
        last, last_low, groups, norm = block(m)
        dk = dk_all[at, :].astype(F32) + rows_of(last, d) * norm
        dk = dk + by_group(lambda g, a: nt(a, groups[g]), v_ref[...] * last_low)
        gk = (jnp.minimum(k_ref[...].astype(F32), 1.0) * dk).astype(BF16)
        dk_all[at, :] = gk
        xhat, _ = normed(x_ref[...].astype(F32))
        h1t = (xhat * vec[0:1, :] + vec[1:2, :]).astype(BF16).T
        h1t_all[:, at] = h1t
        acc[:, d : 2 * d] += nn(h1t, gk)
        shares[:, d : 2 * d] += column_sum(gk.astype(F32))

    def arrange(src, part):
        for w_ in range(n):
            put(src.at[w_], 0, acc[each * w_ : each * w_ + each, d * part : d * part + d].astype(BF16))
            fill(src.at[w_], each, d)

    @pl.when(i == p2 - 1)
    def _():
        arrange(src_k, 1)
        of_k.start1()

    @pl.when((i >= p2) & (i < p3))
    def _():
        m = i - p2
        at = pl.ds(pl.multiple_of(m * rows, rows), rows)
        _, last_low, groups, _ = block(m)
        gv = dv_all[at, :].astype(F32) + by_group(lambda g, a: nn(a, groups[g]), k_ref[...] * last_low)
        gv = gv.astype(BF16)
        dv_all[at, :] = gv
        acc[:, 2 * d :] += nn(h1t_all[:, at], gv)
        shares[:, 2 * d :] += column_sum(gv.astype(F32))

    @pl.when(i == p3 - 1)
    def _():
        arrange(src_v, 2)
        of_v.start1()

    @pl.when(i == p3)
    def _():
        up_out[...] = of_up.out[...]

        def add(m, carry):
            at = pl.ds(pl.multiple_of(m * rows, rows), rows)
            gq = gq_all[at, :]
            acc[:, 0:d] += nn(h1t_all[:, at], gq)
            shares[:, 0:d] += column_sum(gq.astype(F32))
            return carry

        lax.fori_loop(0, micro // 2, add, 0)
        of_k.finish2_start3()
        of_v.finish1_start2()
        lax.fori_loop(micro // 2, micro, add, 0)
        arrange(src_q, 0)
        of_q.start1()
        both = jnp.zeros((d, 128), F32)
        only = jnp.zeros((d, 128), F32)
        for j in range(3 * d // 128):
            cut = slice(128 * j, 128 * j + 128)
            weight = w[:, cut].astype(F32)
            both = both + weight * acc[:, cut]
            only = only + weight * shares[:, cut]
        both, only = column_sum(both.T), column_sum(only.T)
        sums[...] = g_vec[...]
        sums[0:1, :] = (both - vec[1:2, :] * only) / vec[0:1, :]
        sums[1:2, :] = only
        owner_tiles(sums[...], vector.tiles, each)
        vector.start1()
        of_q.finish1_start2()

    @pl.when(i >= p4)
    def _():
        at = pl.ds(pl.multiple_of((i - p4) * rows, rows), rows)
        e = nt(gq_all[at, :], w[:, 0:d]) + nt(dk_all[at, :], w[:, d : 2 * d]) + nt(dv_all[at, :], w[:, 2 * d :])
        xhat, scale = normed(x_ref[...].astype(F32))
        gx_out[...] = norm_back(e, xhat, scale, vec[0:1, :]).astype(BF16)

    @pl.when(i == end - 1)
    def _():
        of_v.finish3_start4()
        of_q.finish3_start4()
        down_out[...] = of_down.out[...]
        k_out[...] = of_k.out[...]
        vector_out[...] = vector.finish3()
        of_v.finish4()
        v_out[...] = of_v.out[...]
        of_q.finish4()
        q_out[...] = of_q.out[...]


def result_kernel(
    gm_ref, part_ref, of_up, of_down, of_k, of_v, of_q, vector, gx, g_qkv, g_out, g_up, g_down, v0, v1, v2, v3, v4, v5
):
    gx[...] = gm_ref[...].astype(F32) + part_ref[...].astype(F32)

    @pl.when(pl.program_id(0) == 0)
    def _():
        each, d = g_out.shape
        for j in range(4):
            g_up[:, d * j : d * j + d] = get(of_up, each * j, each, d).astype(F32)
        g_out[...] = get(of_up, 4 * each, each, d).astype(F32)
        g_down[...] = get(of_down, 0, 4 * each, d).astype(F32)
        for j, part in enumerate((of_q, of_k, of_v)):
            g_qkv[:, d * j : d * j + d] = get(part, 0, each, d).astype(F32)
        for j, v in enumerate((v0, v1, v2, v3, v4)):
            v[...] = vector[j : j + 1, :each]
        for r in range(4):
            v5[:, each * r : each * r + each] = vector[5 + r : 6 + r, :each]


def params(count):
    return pltpu.CompilerParams(
        dimension_semantics=("arbitrary",) * count, vmem_limit_bytes=VMEM
    )


def small():
    return pl.BlockSpec(memory_space=pltpu.SMEM)


def per_device(
    block_in, cotangent, ln1_gain, ln1_bias, qkv_weight, out_weight, ln2_gain, ln2_bias,
    up_weight, up_bias, down_weight, down_bias, seq_lengths,
):
    micro, rows, d = block_in.shape[0], block_in.shape[2], block_in.shape[3]
    ff = up_weight.shape[1]
    wide, index = lax.axis_size("wide"), lax.axis_index("wide")
    lens = seq_lengths.reshape(micro, -1)
    off = (index * rows).astype(jnp.int32).reshape(1)
    x = block_in.reshape(micro, rows, d)
    cot = cotangent.reshape(micro, rows, d)

    each = d // wide
    lane = jnp.arange(256) // 64
    ones = (lane[:, None] == lane[None, :]).astype(BF16)

    tiles = rows // TILE
    token = pl.BlockSpec((None, TILE, d), lambda m, t: (m, t, 0))
    whole = lambda shape: pl.BlockSpec(shape, lambda *_: (0,) * len(shape))
    fixed = lambda shape: pl.BlockSpec(
        shape, lambda *_: (0,) * len(shape), pipeline_mode=pl.Buffered(1)
    )
    packed = pl.BlockSpec((None, state_rows(), 128), lambda m, *_: (m, 0, 0))
    like = lambda dtype: jax.ShapeDtypeStruct((micro, rows, d), dtype)
    up_shape, down_shape = packed_shape(5 * each, d), packed_shape(4 * each, d)

    block = pl.BlockSpec((None, rows, d), lambda m: (m, 0, 0))
    count = rows // CHUNK
    states_spec = pl.BlockSpec((None, count, 2, 256, 256), lambda m: (m, 0, 0, 0, 0))
    during = lambda begin, *shape: pl.BlockSpec(
        (None,) + shape, lambda i: (jnp.clip(i - begin, 0, micro - 1),) + (0,) * len(shape)
    )
    anywhere = pl.BlockSpec(memory_space=pl.ANY)
    spread = lambda a: jax.ShapeDtypeStruct((wide,) + a.shape, BF16)
    dma = pltpu.SemaphoreType.DMA
    vectors = [a.reshape(1, -1) for a in (ln1_gain, ln1_bias, ln2_gain, ln2_bias, down_bias, up_bias)]
    state_shape = (micro, state_rows(), 128)
    (q, k, v, num, kc, states, state_in, w_qkv, w_out, w_up, w_down, vec) = pl.pallas_call(
        first_kernel,
        grid=(4 * micro,),
        in_specs=[small(), small(), fixed((micro, rows, d))] + [anywhere] * 4 + [whole(a.shape) for a in vectors] + [whole((256, 256))],
        out_specs=[during(micro * j, rows, d) for j in range(3)] + [during(3 * micro, rows, d)] * 2
        + [during(3 * micro, count, 4, 128, 128), whole(state_shape)]
        + [anywhere] * 4 + [whole((16, d))],
        out_shape=[like(BF16)] * 5 + [
            jax.ShapeDtypeStruct((micro, count, 4, 128, 128), BF16), jax.ShapeDtypeStruct(state_shape, F32),
            spread(qkv_weight), spread(out_weight), spread(up_weight), spread(down_weight),
            jax.ShapeDtypeStruct((16, d), F32),
        ],
        scratch_shapes=[pltpu.VMEM((3, wide, each, d), BF16)]
        + [pltpu.VMEM((micro, rows, d), BF16)] * 4
        + [
            pltpu.VMEM((4, 128, 128), F32), pltpu.VMEM((1, d), F32), pltpu.VMEM(state_shape, BF16), pltpu.VMEM((16, 128), BF16), pltpu.VMEM((wide, 16, 128), BF16),
            dma, dma((wide,)), dma((wide,)), dma((3,)),
        ]
        + running_scratch(micro // 2) * 2
        + gather_sems() * 8,
        compiler_params=pltpu.CompilerParams(
            dimension_semantics=("arbitrary",), vmem_limit_bytes=VMEM, collective_id=0, has_side_effects=True
        ),
        name="first",
    )(lens, off, x, qkv_weight, out_weight, up_weight, down_weight, *vectors, ones)
    w_qkv, w_out = w_qkv.reshape(d, 3 * d), w_out.reshape(d, d)
    w_up, w_down = w_up.reshape(d, ff), w_down.reshape(ff, d)

    result, g_middle, gnum, gden, use, grads_up, grads_down, g_vec = pl.pallas_call(
        middle_kernel,
        grid=(micro, tiles),
        in_specs=[small(), small()] + [token] * 5 + [packed, whole((256, 256))] + [
            fixed((d, d)), whole((16, d)), fixed((d, ff)), fixed((ff, d)),
        ],
        out_specs=[token, token, token, token, packed, fixed((wide,) + up_shape), fixed((wide,) + down_shape), whole((16, d))],
        out_shape=[
            like(BF16), like(BF16), like(BF16), like(BF16), jax.ShapeDtypeStruct(state_shape, BF16),
            jax.ShapeDtypeStruct((wide,) + up_shape, BF16), jax.ShapeDtypeStruct((wide,) + down_shape, BF16),
            jax.ShapeDtypeStruct((16, d), F32),
        ],
        scratch_shapes=[
            pltpu.VMEM((2, 256, 256), BF16), pltpu.VMEM((1, d), F32),
            pltpu.VMEM((2, 256, 256), F32), pltpu.VMEM((1, d), F32),
            pltpu.VMEM((d, d), F32), pltpu.VMEM((d, ff), F32), pltpu.VMEM((d, ff), F32),
            pltpu.VMEM((TILE, d), F32), pltpu.VMEM((TILE, d), F32), pltpu.VMEM((TILE, d), BF16),
            pltpu.VMEM((d, TILE), BF16), pltpu.VMEM((d, TILE), BF16),
        ],
        compiler_params=params(2),
        name="middle",
    )(lens, off, q, num, kc, x, cot, state_in, ones, w_out, vec, w_up, w_down)

    spare = 2 if wide <= 8 else 1
    halves = rows // TILE
    p1 = halves * micro
    p2, p4 = p1 + micro, p1 + 2 * micro + 1

    def backward(*shape):
        def at(i):
            i = jnp.minimum(i, p1 - 1)
            return (i // halves, halves - 1 - lax.rem(i, halves)) + (0,) * (len(shape) - 1)

        return pl.BlockSpec((None,) + shape, at)

    def walk(*begins, buffers=2):
        def at(i):
            j = 0
            for b in begins:
                j = j + jnp.where(i >= b, jnp.clip(i - b, 0, micro - 1) - j, 0)
            return (j, 0, 0)

        return pl.BlockSpec((None, rows, d), at, pipeline_mode=pl.Buffered(buffers))

    part_shape = packed_shape(each, d)
    vector_shapes = [(1, each)] * 5 + [(1, 4 * each)]
    summed_shapes = [up_shape, down_shape, part_shape, part_shape, part_shape, (16, 128)]
    result_shapes = [(each, 3 * d), (each, d), (each, ff), (4 * each, d)] + vector_shapes
    part, *summed = pl.pallas_call(
        last_kernel,
        grid=(p4 + micro,),
        in_specs=[small(), small()] + [backward(TILE, d)] * 6 + [backward(count // halves, 4, 128, 128)]
        + [pl.BlockSpec((None, state_rows(), 128), lambda i: (jnp.minimum(i // halves, micro - 1), 0, 0))]
        + [walk(p1, p2, buffers=spare), walk(p1, buffers=spare), walk(p1, p4, buffers=spare)] + [anywhere] * 3
        + [whole((16, d)), whole((256, 256)), whole((16, d)), fixed((d, 3 * d))],
        out_specs=[walk(p4)] + [fixed(s) for s in summed_shapes],
        out_shape=[like(BF16)] + [jax.ShapeDtypeStruct(s, BF16) for s in summed_shapes[:5]]
        + [jax.ShapeDtypeStruct((16, 128), F32)],
        scratch_shapes=[pltpu.VMEM((micro * rows, d), BF16)] * 3
        + [
            pltpu.VMEM((d, micro * rows), BF16), pltpu.VMEM((d, 3 * d), F32),
            pltpu.VMEM((4, 128, 128), F32), pltpu.VMEM((1, d), F32),
            pltpu.VMEM((16, d), F32), pltpu.VMEM((1, 3 * d), F32),
        ]
        + [pltpu.VMEM((wide,) + part_shape, BF16)] * 3
        + running_scratch(micro)
        + scatter_scratch(up_shape) + scatter_scratch(down_shape) + scatter_scratch(part_shape) * 3
        + vector_scratch(),
        compiler_params=pltpu.CompilerParams(
            dimension_semantics=("arbitrary",), vmem_limit_bytes=VMEM, collective_id=1, has_side_effects=True
        ),
        name="last",
    )(lens, off, q, k, v, gnum, gden, kc, states, state_in, k, v, x, use, grads_up, grads_down, g_vec, ones, vec, w_qkv)
    grad_input, g_qkv, g_out, g_up, g_down, *g_vectors = pl.pallas_call(
        result_kernel,
        grid=(micro,),
        in_specs=[block, block] + [whole(s) for s in summed_shapes],
        out_specs=[block] + [whole(s) for s in result_shapes],
        out_shape=[like(F32)] + [jax.ShapeDtypeStruct(s, F32) for s in result_shapes],
        compiler_params=params(1),
        name="result",
    )(g_middle, part, *summed)
    piece = [a.reshape(-1) for a in g_vectors]
    return (
        result.reshape(block_in.shape),
        grad_input.reshape(block_in.shape),
        piece[0],
        piece[1],
        g_qkv,
        g_out,
        piece[2],
        piece[3],
        g_up,
        piece[5],
        g_down,
        piece[4],
    )


def solution(mesh):
    tokens = P(None, "dp", "wide", None)
    vector, matrix = P("wide"), P("wide", None)
    weights = (vector, vector, matrix, matrix, vector, vector, matrix, vector, matrix, vector)
    return jax.shard_map(
        per_device,
        mesh=mesh,
        in_specs=(tokens, tokens) + weights + (P(None, "dp", None),),
        out_specs=(tokens, tokens) + weights,
        check_vma=False,
    )
```

```python
import functools

import jax
import jax.numpy as jnp
from jax import lax
from jax.experimental import pallas as pl
from jax.experimental.pallas import tpu as pltpu
from jax.sharding import PartitionSpec as P

HEADS = 8
EPSILON = 1e-05
F32 = jnp.float32
BF16 = jnp.bfloat16
CHUNK = 128
TILE = 512
FF_TILE = 512
VMEM = 62 * 1024 * 1024


def nn(a, b):
    return lax.dot_general(a, b, (((1,), (0,)), ((), ())), preferred_element_type=F32)


def nt(a, b):
    return lax.dot_general(a, b, (((1,), (1,)), ((), ())), preferred_element_type=F32)


def rows_of(row, width):
    return jnp.concatenate([row] * (width // 128), axis=1)


def start_of(lens, m, place):
    start, end = jnp.zeros_like(place), 0
    for j in range(lens.shape[1]):
        end = end + lens[m, j]
        start = start + jnp.where(end <= place, lens[m, j], 0)
    return start


def place_rows(first, count):
    return first + lax.broadcasted_iota(jnp.int32, (count, 128), 0)


def flag(condition):
    return jnp.where(condition, 1.0, 0.0)


def normed(x):
    average = jnp.mean(x, axis=-1, keepdims=True)
    centred = x - average
    spread = jnp.mean(centred * centred, axis=-1, keepdims=True)
    scale = lax.rsqrt(spread + EPSILON)
    return centred * scale, scale


def norm_back(e, xhat, scale, gain):
    a = gain * e
    return scale * (
        a - jnp.mean(a, axis=-1, keepdims=True) - xhat * jnp.mean(a * xhat, axis=-1, keepdims=True)
    )


def feature(v):
    return jnp.where(v > 0.0, v + 1.0, jnp.exp(jnp.minimum(v, 0.0)))


def column_sum(a):
    return jnp.sum(a, axis=0, keepdims=True)


def by_group(fn, *arrays):
    return jnp.concatenate(
        [fn(g, *[a[:, 256 * g : 256 * g + 256] for a in arrays]) for g in range(2)], axis=1
    )


def lane_half(shape):
    return lax.broadcasted_iota(jnp.int32, shape, 1) < 64


def pack_state(state, norm, out):
    folded = [s + pltpu.roll(s, 64, 1) for s in state]
    half = lane_half((128, 128))
    for j in range(2):
        out[128 * j : 128 * j + 128, :] = jnp.where(half, folded[j], folded[2 + j]).astype(out.dtype)
    row = lax.broadcasted_iota(jnp.int32, (16, 128), 0)
    tail = jnp.zeros((16, 128), F32)
    for j in range(4):
        tail = jnp.where(row == j, norm[:, 128 * j : 128 * j + 128], tail)
    out[256:272, :] = tail.astype(out.dtype)
    if out.shape[0] > 272:
        out[272:, :] = jnp.zeros((out.shape[0] - 272, 128), out.dtype)


def unpack_pairs(packed, ones):
    half = lane_half((128, 128))
    mask = ones[0:128, 0:128].astype(F32)
    pairs = [None] * 4
    for j in range(2):
        z = packed[128 * j : 128 * j + 128, :]
        turned = pltpu.roll(z, 64, 1)
        pairs[j] = jnp.where(half, z, turned) * mask
        pairs[2 + j] = jnp.where(half, turned, z) * mask
    tail = packed[256:272, :]
    norm = jnp.concatenate([tail[j : j + 1, :] for j in range(4)], axis=1)
    return pairs, norm


def unpack_state(packed, ones):
    pairs, norm = unpack_pairs(packed, ones)
    zero = jnp.zeros((128, 128), BF16)
    groups = []
    for g in range(2):
        above = jnp.concatenate([pairs[2 * g].astype(BF16), zero], axis=1)
        below = jnp.concatenate([zero, pairs[2 * g + 1].astype(BF16)], axis=1)
        groups.append(jnp.concatenate([above, below], axis=0))
    return groups, norm


MESH = pl.DeviceIdType.MESH


def place():
    dp = lax.axis_index("dp")
    return lax.rem(dp, 2), dp // 2, lax.axis_index("wide"), lax.axis_size("dp") // 2, lax.axis_size("wide")


def others(count, fn):
    def body(o, carry):
        fn(o)
        return carry

    lax.fori_loop(1, count, body, 0)


def remote(src, dst, send, recv, dp, wide):
    return pltpu.make_async_remote_copy(
        src_ref=src, dst_ref=dst, send_sem=send, recv_sem=recv, device_id=(dp, wide), device_id_type=MESH
    )


def signal_all():
    core, y, me, ny, n = place()
    dp = 2 * y + core
    barrier = pltpu.get_barrier_semaphore()

    def signal(d, w):
        pl.semaphore_signal(barrier, inc=1, device_id=(d, w), device_id_type=MESH)

    others(n, lambda o: signal(dp, lax.rem(me + o, n)))
    others(2 * ny, lambda o: signal(lax.rem(dp + o, 2 * ny), me))


def wait_all():
    _, _, _, ny, n = place()
    pl.semaphore_wait(pltpu.get_barrier_semaphore(), n - 1 + 2 * ny - 1)


class Gather:
    def __init__(self, src, dst, sems):
        self.src, self.dst = src, dst
        self.near, self.send, self.recv, self.y_send, self.y_recv, self.c_send, self.c_recv = sems
        self.core, self.y, self.me, self.ny, self.n = place()
        self.dp = 2 * self.y + self.core
        each = src.shape[0]
        self.split = split_of(each)
        part = each // self.split
        if self.split == 1:
            self.rows, self.half = pl.ds(0, each), None
        else:
            at = self.core * (each // 2) + self.y * part
            self.rows = pl.ds(pl.multiple_of(at, part), part)
            self.half = pl.ds(pl.multiple_of(self.core * (each // 2), each // 2), each // 2)

    def own(self):
        return pltpu.make_async_copy(self.src.at[self.rows], self.dst.at[self.me, self.rows], self.near)

    def out(self, o):
        to = lax.rem(self.me + o, self.n)
        return remote(self.src.at[self.rows], self.dst.at[self.me, self.rows], self.send.at[o], self.recv.at[self.me], self.dp, to)

    def back(self, o):
        frm = lax.rem(self.me + o, self.n)
        part = self.dst.at[frm, self.rows]
        return remote(part, part, self.send.at[o], self.recv.at[frm], self.dp, frm)

    def start_wide(self):
        self.own().start()
        others(self.n, lambda o: self.out(o).start())

    def finish_wide(self):
        self.own().wait()
        others(self.n, lambda o: self.out(o).wait_send())
        others(self.n, lambda o: self.back(o).wait_recv())

    def along_y(self, o):
        part = self.dst.at[:, self.rows]
        to = lax.rem(self.y + o, self.ny)
        return remote(part, part, self.y_send.at[o], self.y_recv.at[self.y], 2 * to + self.core, self.me)

    def along_y_back(self, o):
        frm = lax.rem(self.y + o, self.ny)
        each = self.src.shape[0]
        part = each // self.split
        at = self.core * (each // 2) + frm * part
        ref = self.dst.at[:, pl.ds(pl.multiple_of(at, part), part)]
        return remote(ref, ref, self.y_send.at[o], self.y_recv.at[frm], 2 * frm + self.core, self.me)

    def start_y(self):
        if self.split > 1:
            others(self.ny, lambda o: self.along_y(o).start())

    def finish_y(self):
        if self.split > 1:
            others(self.ny, lambda o: self.along_y(o).wait_send())
            others(self.ny, lambda o: self.along_y_back(o).wait_recv())

    def cross(self):
        part = self.dst.at[:, self.half]
        return remote(part, part, self.c_send, self.c_recv, 2 * self.y + 1 - self.core, self.me)

    def cross_back(self):
        each = self.src.shape[0]
        at = (1 - self.core) * (each // 2)
        part = self.dst.at[:, pl.ds(pl.multiple_of(at, each // 2), each // 2)]
        return remote(part, part, self.c_send, self.c_recv, 2 * self.y + 1 - self.core, self.me)

    def start_core(self):
        if self.split > 1:
            self.cross().start()

    def finish_core(self):
        if self.split > 1:
            self.cross().wait_send()
            self.cross_back().wait_recv()


def split_of(each):
    count = lax.axis_size("dp")
    return count if each % (16 * count) == 0 else 1


def gather_sems():
    n, ny = lax.axis_size("wide"), lax.axis_size("dp") // 2
    dma = pltpu.SemaphoreType.DMA
    return [dma, dma((n,)), dma((n,)), dma((ny,)), dma((ny,)), dma, dma]


def packed_shape(rows, d):
    unit = 16 * lax.axis_size("dp")
    columns = d if rows % unit == 0 else 128
    rows = rows * (d // columns)
    return -(-rows // unit) * unit, columns


def put(block, at, piece):
    rows, d = piece.shape
    columns = block.shape[1]
    for b in range(d // columns):
        begin = at * (d // columns) + rows * b
        block[begin : begin + rows, :] = piece[:, columns * b : columns * b + columns]


def fill(block, rows, d):
    used = rows * (d // block.shape[1])
    if block.shape[0] > used:
        block[used:, :] = jnp.zeros((block.shape[0] - used, block.shape[1]), block.dtype)


def get(block, at, rows, d):
    columns = block.shape[1]
    begin = at * (d // columns)
    return jnp.concatenate(
        [block[begin + rows * b : begin + rows * b + rows, :] for b in range(d // columns)], axis=1
    )


class Scatter:
    def __init__(self, src, refs):
        self.src = src
        (self.half, self.got_core, self.got_y, self.got_wide, self.out, self.near, self.c_sem, self.y_send,
         self.y_recv, self.w_send, self.w_recv, self.b_send, self.b_recv) = refs
        self.core, self.y, self.me, self.ny, self.n = place()
        self.dp = 2 * self.y + self.core
        self.rows = self.out.shape[0]
        self.each = self.rows // (2 * self.ny)
        self.partner = 2 * self.y + 1 - self.core
        self.part = self.got_core.at[:, 0 : self.each]

    def half_rows(self, core):
        return pl.ds(pl.multiple_of(core * (self.rows // 2), self.rows // 2), self.rows // 2)

    def y_rows(self, y):
        return pl.ds(pl.multiple_of(y * self.each, self.each), self.each)

    def own_rows(self, y):
        at = self.core * (self.rows // 2) + y * self.each
        return pl.ds(pl.multiple_of(at, self.each), self.each)

    def load(self):
        return pltpu.make_async_copy(self.src.at[:, self.half_rows(self.core)], self.half, self.near)

    def cross(self):
        return remote(
            self.src.at[:, self.half_rows(1 - self.core)], self.got_core, self.c_sem.at[0], self.c_sem.at[1], self.partner, self.me
        )

    def start1(self):
        self.cross().start()
        self.load().start()

    def along_y(self, o):
        to = lax.rem(self.y + o, self.ny)
        return remote(
            self.half.at[:, self.y_rows(to)], self.got_y.at[o - 1], self.y_send.at[o], self.y_recv.at[o],
            2 * to + self.core, self.me,
        )

    def finish1_start2(self):
        self.load().wait()
        self.cross().wait()

        def add(w, carry):
            self.half[w] = (self.half[w].astype(F32) + self.got_core[w].astype(F32)).astype(BF16)
            return carry

        lax.fori_loop(0, self.n, add, 0)
        others(self.ny, lambda o: self.along_y(o).start())

    def along_wide(self, o):
        to = lax.rem(self.me + o, self.n)
        return remote(self.part.at[to], self.got_wide.at[o - 1], self.w_send.at[o], self.w_recv.at[o], self.dp, to)

    def finish2_start3(self):
        others(self.ny, lambda o: self.along_y(o).wait())

        def add(w, carry):
            total = self.half[w, self.y_rows(self.y)].astype(F32)
            for o in range(self.ny - 1):
                total = total + self.got_y[o, w].astype(F32)
            self.part[w] = total.astype(BF16)
            return carry

        lax.fori_loop(0, self.n, add, 0)
        others(self.n, lambda o: self.along_wide(o).start())

    def back(self, o, wait=False):
        other = lax.rem(self.dp + o, 2 * self.ny)
        slot = other if wait else self.dp
        at = lax.rem(slot, 2) * (self.rows // 2) + (slot // 2) * self.each
        ref = self.out.at[pl.ds(pl.multiple_of(at, self.each), self.each)]
        return remote(ref, ref, self.b_send.at[o], self.b_recv.at[slot], other, self.me)

    def finish3_start4(self):
        others(self.n, lambda o: self.along_wide(o).wait())
        total = self.part[self.me].astype(F32)
        total = lax.fori_loop(0, self.n - 1, lambda o, t: t + self.got_wide[o].astype(F32), total)
        self.out[self.own_rows(self.y)] = total.astype(BF16)
        others(2 * self.ny, lambda o: self.back(o).start())

    def finish4(self):
        others(2 * self.ny, lambda o: self.back(o).wait_send())
        others(2 * self.ny, lambda o: self.back(o, True).wait_recv())


def scatter_scratch(shape):
    rows, d = shape
    n, dp = lax.axis_size("wide"), lax.axis_size("dp")
    ny, part = dp // 2, rows // dp
    dma = pltpu.SemaphoreType.DMA
    return [
        pltpu.VMEM((n, rows // 2, d), BF16),
        pltpu.VMEM((n, rows // 2, d), BF16),
        pltpu.VMEM((ny - 1, n, part, d), BF16),
        pltpu.VMEM((n - 1, part, d), BF16),
        pltpu.VMEM((rows, d), BF16),
        dma, dma((2,)), dma((ny,)), dma((ny,)), dma((n,)), dma((n,)), dma((dp,)), dma((dp,)),
    ]


class VectorSum:
    def __init__(self, refs):
        self.tiles, self.got_core, self.got_y, self.got_wide, self.c_sem, self.y_send, self.y_recv, self.w_send, self.w_recv = refs
        self.core, self.y, self.me, self.ny, self.n = place()
        self.dp = 2 * self.y + self.core

    def cross(self):
        return remote(self.tiles, self.got_core, self.c_sem.at[0], self.c_sem.at[1], 2 * self.y + 1 - self.core, self.me)

    def along_y(self, o):
        to = lax.rem(self.y + o, self.ny)
        return remote(self.tiles, self.got_y.at[o - 1], self.y_send.at[o], self.y_recv.at[o], 2 * to + self.core, self.me)

    def along_wide(self, o):
        to = lax.rem(self.me + o, self.n)
        return remote(self.tiles.at[to], self.got_wide.at[o - 1], self.w_send.at[o], self.w_recv.at[o], self.dp, to)

    def start1(self):
        self.cross().start()

    def finish1_start2(self):
        self.cross().wait()
        self.tiles[...] = self.tiles[...] + self.got_core[...]
        others(self.ny, lambda o: self.along_y(o).start())

    def finish2_start3(self):
        others(self.ny, lambda o: self.along_y(o).wait())
        total = self.tiles[...]
        for o in range(self.ny - 1):
            total = total + self.got_y[o]
        self.tiles[...] = total
        others(self.n, lambda o: self.along_wide(o).start())

    def finish3(self):
        others(self.n, lambda o: self.along_wide(o).wait())
        return lax.fori_loop(0, self.n - 1, lambda o, t: t + self.got_wide[o], self.tiles[self.me])


def vector_scratch():
    n, ny = lax.axis_size("wide"), lax.axis_size("dp") // 2
    dma = pltpu.SemaphoreType.DMA
    return [
        pltpu.VMEM((n, 16, 128), F32),
        pltpu.VMEM((n, 16, 128), F32),
        pltpu.VMEM((ny - 1, n, 16, 128), F32),
        pltpu.VMEM((n - 1, 16, 128), F32),
        dma((2,)), dma((ny,)), dma((ny,)), dma((n,)), dma((n,)),
    ]


def owner_tiles(rows, tiles, each):
    n = tiles.shape[0]
    d = each * n
    per = 4 * each
    row = lax.broadcasted_iota(jnp.int32, (16, 128), 0)
    lane = lax.broadcasted_iota(jnp.int32, (16, 128), 1)
    blocks = [rows[:, 128 * j : 128 * j + 128] for j in range(d // 128)]

    def turned(a, by, axis):
        by = by % a.shape[axis]
        return pltpu.roll(a, by, axis) if by else a

    for w in range(n):
        at = each * w
        tile = jnp.where(row < 5, turned(blocks[at // 128], -(at % 128), 1), 0.0)
        for r in range(4):
            at = per * w + each * r
            from_row, begin = 5 + at // d, at % d
            moved = turned(turned(blocks[begin // 128], -(begin % 128), 1), 5 + r - from_row, 0)
            tile = jnp.where(row == 5 + r, moved, tile)
        tiles[w] = jnp.where(lane < each, tile, 0.0)


HIGH = 4


def low_count():
    return lax.axis_size("wide") // HIGH


def state_rows():
    unit = 16 * low_count()
    return -(-272 // unit) * unit


class Running:
    def __init__(self, own, upward, refs):
        self.own, self.upward = own, upward
        (self.slots, self.group, self.high, self.mine, self.spread, self.result, self.near, self.send1, self.recv1,
         self.send2, self.recv2, self.send3, self.recv3) = refs
        _, _, self.me, _, _ = place()
        self.dp = lax.axis_index("dp")
        self.lo = low_count()
        self.h, self.l = self.me // self.lo, lax.rem(self.me, self.lo)
        self.part = state_rows() // self.lo

    def slice(self, l):
        return pl.ds(pl.multiple_of(l * self.part, self.part), self.part)

    def copy1(self, o, back=False):
        other = lax.rem(self.l + o, self.lo)
        slot = other if back else self.l
        return remote(self.own, self.slots.at[slot], self.send1.at[o], self.recv1.at[slot], self.dp, self.h * self.lo + other)

    def near1(self):
        return pltpu.make_async_copy(self.own, self.slots.at[self.l], self.near.at[0])

    def start1(self):
        self.near1().start()
        others(self.lo, lambda o: self.copy1(o).start())

    def before(self, a, b):
        return a < b if self.upward else a > b

    def finish1_start2(self):
        self.near1().wait()
        others(self.lo, lambda o: self.copy1(o).wait_send())
        others(self.lo, lambda o: self.copy1(o, True).wait_recv())
        every = jnp.zeros(self.own.shape, F32)
        inner = every
        for l in range(self.lo):
            part = self.slots[l].astype(F32)
            every = every + part
            inner = inner + jnp.where(self.before(l, self.l), part, 0.0)
        self.group[...] = every.astype(BF16)
        self.result[...] = inner

        def send(o):
            other = lax.rem(self.h + o, HIGH)

            @pl.when(self.before(self.h, other))
            def _():
                self.copy2(o).start()

        others(HIGH, send)

    def copy2(self, o, back=False):
        other = lax.rem(self.h + o, HIGH)
        slot = other if back else self.h
        return remote(
            self.group.at[:, self.slice(self.l)], self.high.at[slot], self.send2.at[o], self.recv2.at[slot],
            self.dp, other * self.lo + self.l,
        )

    def finish2_start3(self):
        def wait(o):
            other = lax.rem(self.h + o, HIGH)

            @pl.when(self.before(self.h, other))
            def _():
                self.copy2(o).wait_send()

            @pl.when(self.before(other, self.h))
            def _():
                self.copy2(o, True).wait_recv()

        others(HIGH, wait)
        total = jnp.zeros(self.mine.shape, F32)
        for h in range(HIGH):
            total = total + jnp.where(self.before(h, self.h), self.high[h].astype(F32), 0.0)
        self.mine[...] = total.astype(BF16)
        self.near3().start()
        others(self.lo, lambda o: self.copy3(o).start())

    def near3(self):
        return pltpu.make_async_copy(self.mine, self.spread.at[self.l], self.near.at[1])

    def copy3(self, o, back=False):
        other = lax.rem(self.l + o, self.lo)
        slot = other if back else self.l
        return remote(self.mine, self.spread.at[slot], self.send3.at[o], self.recv3.at[slot], self.dp, self.h * self.lo + other)

    def finish3(self):
        self.near3().wait()
        others(self.lo, lambda o: self.copy3(o).wait_send())
        others(self.lo, lambda o: self.copy3(o, True).wait_recv())
        for l in range(self.lo):
            rows = slice(l * self.part, (l + 1) * self.part)
            self.result[:, rows] = self.result[:, rows] + self.spread[l].astype(F32)


def running_scratch(micro):
    lo, rows = low_count(), state_rows()
    dma = pltpu.SemaphoreType.DMA
    return [
        pltpu.VMEM((lo, micro, rows, 128), BF16),
        pltpu.VMEM((micro, rows, 128), BF16),
        pltpu.VMEM((HIGH, micro, rows // lo, 128), BF16),
        pltpu.VMEM((micro, rows // lo, 128), BF16),
        pltpu.VMEM((lo, micro, rows // lo, 128), BF16),
        pltpu.VMEM((micro, rows, 128), F32),
        dma((2,)), dma((lo,)), dma((lo,)), dma((HIGH,)), dma((HIGH,)), dma((lo,)), dma((lo,)),
    ]


def vector_tile(vectors, each):
    row = lax.broadcasted_iota(jnp.int32, (16, 128), 0)

    def padded(piece):
        return jnp.concatenate([piece.astype(F32), jnp.zeros((1, 128 - each), F32)], axis=1)

    pieces = [padded(v[...]) for v in vectors[:5]]
    hidden = vectors[5][...]
    pieces += [padded(hidden[:, each * r : each * r + each]) for r in range(hidden.shape[1] // each)]
    tile = jnp.zeros((16, 128), F32)
    for j, piece in enumerate(pieces):
        tile = jnp.where(row == j, piece, tile)
    return tile.astype(BF16)


def spread_vectors(slots, out, each):
    n = slots.shape[0]
    d = each * n
    per = 4 * each
    row = lax.broadcasted_iota(jnp.int32, (16, 128), 0)
    blocks = [jnp.zeros((16, 128), F32) for _ in range(d // 128)]
    for w in range(n):
        tile = slots[w].astype(F32)
        at = each * w
        moved = pltpu.roll(tile, at % 128, 1) if at % 128 else tile
        blocks[at // 128] = blocks[at // 128] + jnp.where(row < 5, moved, 0.0)
        for r in range(4):
            at = per * w + each * r
            to_row, lane = 5 + at // d, at % d
            only = jnp.where(row == 5 + r, tile, 0.0)
            moved = pltpu.roll(only, lane % 128, 1) if lane % 128 else only
            if to_row != 5 + r:
                moved = pltpu.roll(moved, (to_row - 5 - r) % 16, 0)
            blocks[lane // 128] = blocks[lane // 128] + moved
    for j, block in enumerate(blocks):
        out[:, 128 * j : 128 * j + 128] = block


def first_kernel(lens, off, x, *refs):
    (s_qkv, s_out, s_up, s_down, v0, v1, v2, v3, v4, v5, ones,
     q_out, k_out, v_out, num_out, kc_out, states_out, state_in, w_qkv, w_out, w_up, w_down, vec_out,
     w_ref, h_all, q_all, k_all, v_all, state, norm, local, tile, tiles_ref, tile_near, tile_send, tile_recv,
     save_sem, *rest) = refs
    each = s_qkv.shape[0]
    micro, rows, d = x.shape
    half = micro // 2
    running = []
    for j in range(2):
        running.append(Running(local.at[half * j : half * j + half], True, rest[:13]))
        rest = rest[13:]
    jobs = []
    for j in range(3):
        jobs.append(Gather(s_qkv.at[:, d * j : d * j + d], w_ref.at[j], rest[7 * j : 7 * j + 7]))
    pieces = [(s_out, w_out)]
    for src, dst in ((s_up, w_up), (s_down, w_down)):
        columns = src.shape[1] // 2
        pieces += [(src.at[:, c : c + columns], dst.at[:, :, c : c + columns]) for c in (0, columns)]
    for j, (src, dst) in enumerate(pieces):
        jobs.append(Gather(src, dst, rest[21 + 7 * j : 28 + 7 * j]))
    i = pl.program_id(0)
    core, y, me, ny, n = place()
    dp = 2 * y + core

    def vec_copy(o, back=False):
        other = lax.rem(me + o, n)
        slot = other if back else me
        return remote(tile, tiles_ref.at[slot], tile_send.at[o], tile_recv.at[slot], dp, other)

    def vec_near():
        return pltpu.make_async_copy(tile, tiles_ref.at[me], tile_near)

    def save(j):
        return pltpu.make_async_copy(w_ref.at[j], w_qkv.at[:, :, d * j : d * j + d], save_sem.at[j])

    def weights(j):
        return w_ref[j].reshape(d, d)

    @pl.when(i == 0)
    def _():
        signal_all()
        tile[...] = vector_tile((v0, v1, v2, v3, v4, v5), each)
        wait_all()
        vec_near().start()
        others(n, lambda o: vec_copy(o).start())
        for job in jobs[:3]:
            job.start_wide()
        vec_near().wait()
        others(n, lambda o: vec_copy(o).wait_send())
        others(n, lambda o: vec_copy(o, True).wait_recv())
        spread_vectors(tiles_ref, vec_out, each)

        def norm_micro(m, carry):
            xhat, _ = normed(x[m].astype(F32))
            h_all[m] = (xhat * vec_out[0:1, :] + vec_out[1:2, :]).astype(BF16)
            return carry

        lax.fori_loop(0, micro // 2, norm_micro, 0)
        jobs[0].finish_wide()
        jobs[0].start_y()
        lax.fori_loop(micro // 2, micro, norm_micro, 0)
        for job in jobs[1:3]:
            job.finish_wide()
            job.start_y()
        for job in jobs[3:]:
            job.start_wide()
        jobs[0].finish_y()
        jobs[0].start_core()
        jobs[0].finish_core()

    @pl.when(i == 1)
    def _():
        jobs[1].finish_y()
        jobs[1].start_core()

    @pl.when(i == 2)
    def _():
        jobs[2].finish_y()
        jobs[2].start_core()

    @pl.when(i < micro)
    def _():
        q = feature(nn(h_all[i], weights(0))).astype(BF16)
        q_out[...] = q
        q_all[i] = q

    @pl.when(i == micro)
    def _():
        jobs[1].finish_core()

    @pl.when((i >= micro) & (i < 2 * micro))
    def _():
        m = i - micro
        k = feature(nn(h_all[m], weights(1))).astype(BF16)
        k_out[...] = k
        k_all[m] = k

    @pl.when(i == 2 * micro)
    def _():
        jobs[2].finish_core()
        for j in range(3):
            save(j).start()

    @pl.when((i >= 2 * micro) & (i < 3 * micro))
    def _():
        m = i - 2 * micro
        v = nn(h_all[m], weights(2)).astype(BF16)
        v_out[...] = v
        v_all[m] = v
        base = off[0]
        final = start_of(lens, m, base + rows - 1)
        last = flag(start_of(lens, m, place_rows(base, rows)) == final)
        k_last = k_all[m] * rows_of(last.astype(BF16), d)
        k_turned = k_last.T
        mask = ones[0:128, 0:128].astype(F32)
        parts = [nn(k_turned[128 * p : 128 * p + 128, :], v[:, 128 * p : 128 * p + 128]) * mask for p in range(4)]
        pack_state(parts, column_sum(k_last.astype(F32)), local.at[m])

    @pl.when(i == 2 * micro + half - 1)
    def _():
        running[0].start1()

    @pl.when(i == 3 * micro - 1)
    def _():
        running[1].start1()

    def pass_on(step, *parts):
        @pl.when(i == step)
        def _():
            for job in parts:
                job.finish_wide()
                job.start_y()

    def cross_over(step, *parts):
        @pl.when(i == step)
        def _():
            for job in parts:
                job.finish_y()
                job.start_core()

    pass_on(micro + 1, jobs[3], jobs[4])
    pass_on(2 * micro + 1, jobs[5])
    pass_on(3 * micro, jobs[6])

    @pl.when(i == 3 * micro)
    def _():
        running[0].finish1_start2()

    cross_over(3 * micro, jobs[3], jobs[4])
    pass_on(3 * micro + 1, jobs[7])

    @pl.when(i == 3 * micro + 1)
    def _():
        running[1].finish1_start2()

    cross_over(3 * micro + 2, jobs[5], jobs[6])

    @pl.when(i == 3 * micro + 2)
    def _():
        running[0].finish2_start3()

    @pl.when(i == 3 * micro + 3)
    def _():
        running[1].finish2_start3()

    cross_over(3 * micro + 3, jobs[7])

    @pl.when(i >= 3 * micro)
    def _():
        m = i - 3 * micro
        attend(lens, m, off[0], q_all.at[m], k_all.at[m], v_all.at[m], ones, num_out, kc_out, states_out, state, norm)

    @pl.when(i == 4 * micro - 1)
    def _():
        for j in range(2):
            running[j].finish3()
            state_in[half * j : half * j + half] = running[j].result[...]
        for job in jobs[3:]:
            job.finish_core()
        for j in range(3):
            save(j).wait()


def chunk_masks(lens, m, begin, size):
    by_row = start_of(lens, m, place_rows(begin, size))
    lane = begin + lax.broadcasted_iota(jnp.int32, (8, size), 1)
    by_column = start_of(lens, m, lane)[0:1, :]
    final = start_of(lens, m, begin + size - 1)
    return by_row, by_column, final


def split_pair(a, low, high):
    return jnp.concatenate([a * low, a * high], axis=0)


def attend(lens, m, base, q_ref, k_ref, v_ref, ones, num_out, kc_out, states_out, state, norm):
    rows, d = q_ref.shape
    size = CHUNK
    state[...] = jnp.zeros_like(state)
    norm[...] = jnp.zeros_like(norm)
    half = lane_half((1, 128))
    low = flag(half).astype(BF16)
    high = flag(jnp.logical_not(half)).astype(BF16)

    def step(c, carry):
        at = pl.ds(pl.multiple_of(c * size, size), size)
        begin = base + c * size
        q, k, v = q_ref[at, :], k_ref[at, :], v_ref[at, :]
        by_row, by_column, final = chunk_masks(lens, m, begin, size)
        places = lax.broadcasted_iota(jnp.int32, (size, size), 0)
        columns = lax.broadcasted_iota(jnp.int32, (size, size), 1)
        allowed = flag((places >= columns) & (by_row[:, :size] == by_column)).astype(BF16)
        allowed2 = jnp.concatenate([allowed, allowed], axis=1)
        seen = flag(by_row < begin)
        last = flag(by_row == final).astype(BF16)
        keep = jnp.where(final < begin, 1.0, 0.0)
        kc_out[at, :] = (nn(allowed, k) + rows_of(seen, d) * norm[...]).astype(BF16)
        q_seen = q * rows_of(seen.astype(BF16), d)
        for p in range(4):
            cut = slice(128 * p, 128 * p + 128)
            s = nt(q[:, cut], split_pair(k[:, cut], low, high)).astype(BF16) * allowed2
            inside = nn(s, split_pair(v[:, cut], low, high))
            held = state[p].astype(BF16)
            states_out[c, p] = held
            before = nn(q_seen[:, cut], held)
            num_out[at, cut] = (inside + before).astype(BF16)
        k_last = k * rows_of(last, d)
        k_turned = k_last.T
        mask = ones[0:128, 0:128].astype(F32)
        for p in range(4):
            cut = slice(128 * p, 128 * p + 128)
            state[p] = keep * state[p] + nn(k_turned[cut, :], v[:, cut]) * mask
        norm[...] = keep * norm[...] + column_sum(k_last.astype(F32))
        return carry

    lax.fori_loop(0, rows // size, step, 0, unroll=8)


def middle_kernel(
    lens, off, q_ref, num_ref, kc_ref, x_ref, cot_ref, state_in, ones,
    w_out, vec, w_up, w_down,
    block_out, gm_out, gnum_out, gden_out, use_out, grads_up, grads_down, g_vec,
    groups, norm, use, use_norm, acc_out, acc_up, acc_down, total, e_total, h2_ref, h2t_ref, ct_ref,
):
    m, t, tiles = pl.program_id(0), pl.program_id(1), pl.num_programs(1)
    rows, d = x_ref.shape
    first = (m == 0) & (t == 0)
    final = (m == pl.num_programs(0) - 1) & (t == tiles - 1)
    base = off[0]

    @pl.when(first)
    def _():
        acc_out[...] = jnp.zeros_like(acc_out)
        acc_up[...] = jnp.zeros_like(acc_up)
        acc_down[...] = jnp.zeros_like(acc_down)
        g_vec[...] = jnp.zeros_like(g_vec)
        h2t_ref[d:, :] = jnp.ones((16, rows), BF16)

    @pl.when(t == 0)
    def _():
        parts, z = unpack_state(state_in[...], ones[...])
        for g in range(2):
            groups[g] = parts[g]
        norm[...] = z
        use[...] = jnp.zeros_like(use)
        use_norm[...] = jnp.zeros_like(use_norm)

    gain, bias, down_bias = vec[2:3, :], vec[3:4, :], vec[4:5, :]
    q = q_ref[...]
    seen = flag(start_of(lens, m, place_rows(base + t * rows, rows)) < base)
    q_seen = q * rows_of(seen.astype(BF16), d)
    num = num_ref[...].astype(F32) + by_group(lambda g, a: nn(a, groups[g]), q_seen)
    kc = kc_ref[...].astype(F32) + rows_of(seen, d) * norm[...]
    den = by_group(lambda g, a: nn(a, ones[...]), (q.astype(F32) * kc).astype(BF16))
    over = 1.0 / den
    mixed = (num * over).astype(BF16)
    middle = x_ref[...].astype(F32) + nn(mixed, w_out[...])
    xhat, scale = normed(middle)
    h2 = (xhat * gain + bias).astype(BF16)
    h2_ref[...] = h2
    h2t_ref[0:d, :] = h2.T
    ct_ref[...] = cot_ref[...].T
    total[...] = middle + down_bias
    e_total[...] = jnp.zeros_like(e_total)

    def ffn(f, carry):
        cut = pl.ds(pl.multiple_of(f * FF_TILE, FF_TILE), FF_TILE)
        hidden = nn(h2_ref[...], w_up[:, cut]) + vec[pl.ds(5 + f, 1), :]
        pulled = nt(cot_ref[...], w_down[cut, :])
        square = hidden * hidden
        c0, c1 = 0.7978845608028654, 0.044715
        th = jnp.tanh(hidden * (c0 + (c0 * c1) * square))
        half_up = 0.5 + 0.5 * th
        active = (hidden * half_up).astype(BF16)
        slope = half_up + hidden * (1.0 - th * th) * (0.5 * c0 + (1.5 * c0 * c1) * square)
        g_low = (slope * pulled).astype(BF16)
        total[...] += nn(active, w_down[cut, :])
        e_total[...] += nt(g_low, w_up[:, cut])
        acc_down[:, cut] += nn(ct_ref[...], active)
        acc_up[:, cut] += nn(h2t_ref[...], g_low)
        return carry

    lax.fori_loop(0, w_up.shape[1] // FF_TILE, ffn, 0, unroll=True)
    block_out[...] = total[...].astype(BF16)
    e = e_total[...]
    cot = cot_ref[...].astype(F32)
    g_middle = cot + norm_back(e, xhat, scale, gain)
    gm_out[...] = g_middle.astype(BF16)
    g_vec[2:3, :] += column_sum(e * xhat)
    g_vec[3:4, :] += column_sum(e)
    g_vec[4:5, :] += column_sum(cot)
    branch = g_middle.astype(BF16)
    acc_out[...] += nn(mixed.T, branch)
    g_mixed = nt(branch, w_out[...])
    gnum = (g_mixed * over).astype(BF16)
    gnum_out[...] = gnum
    gden = -by_group(lambda g, a: nn(a, ones[...]), (g_mixed * num).astype(BF16)) * (over * over)
    gden_out[...] = gden.astype(BF16)
    turned = q_seen.T
    for g in range(2):
        cut = slice(256 * g, 256 * g + 256)
        use[g] += nn(turned[cut, :], gnum[:, cut])
    use_norm[...] += column_sum(q_seen.astype(F32) * gden)

    @pl.when(t == tiles - 1)
    def _():
        mask = ones[0:128, 0:128].astype(F32)
        pack_state([use[p // 2][128 * (p % 2) : 128 * (p % 2) + 128, 128 * (p % 2) : 128 * (p % 2) + 128] * mask for p in range(4)], use_norm[...], use_out)

    @pl.when(final)
    def _():
        for j in range(4):
            g_vec[5 + j : 6 + j, :] = acc_up[d : d + 1, d * j : d * j + d]
        n = grads_up.shape[0]
        each = d // n
        down = acc_down[...].astype(BF16).T
        for w in range(n):
            at = slice(each * w, each * w + each)
            for j in range(4):
                put(grads_up.at[w], each * j, acc_up[at, d * j : d * j + d].astype(BF16))
            put(grads_up.at[w], 4 * each, acc_out[at, :].astype(BF16))
            fill(grads_up.at[w], 5 * each, d)
            put(grads_down.at[w], 0, down[4 * each * w : 4 * each * w + 4 * each, :])
            fill(grads_down.at[w], 4 * each, d)


def attend_back(
    lens, m, base, lead, q_ref, k_ref, v_ref, gnum_ref, gden_ref, kc_ref, states, state_in, ones,
    gq_out, dk_out, dv_out, after, after_norm,
):
    rows, d = q_ref.shape
    size = CHUNK
    count = rows // size
    half = lane_half((1, 128))
    low = flag(half).astype(BF16)
    high = flag(jnp.logical_not(half)).astype(BF16)
    pairs_in, norm_in = unpack_pairs(state_in[...], ones[...])

    def step(i, carry):
        c = count - 1 - i
        at = pl.ds(pl.multiple_of(c * size, size), size)
        begin = lead + c * size
        q, k, v, gnum = q_ref[at, :], k_ref[at, :], v_ref[at, :], gnum_ref[at, :]
        gden = gden_ref[at, :].astype(F32)
        by_row, by_column, final = chunk_masks(lens, m, begin, size)
        places = lax.broadcasted_iota(jnp.int32, (size, size), 0)
        columns = lax.broadcasted_iota(jnp.int32, (size, size), 1)
        same = by_row[:, :size] == by_column
        allowed = flag((places >= columns) & same).astype(BF16)
        allowed2 = jnp.concatenate([allowed, allowed], axis=1)
        turned = flag((places <= columns) & same).astype(BF16)
        turned2 = jnp.concatenate([turned, turned], axis=1)
        seen = rows_of(flag(by_row < begin).astype(BF16), d)
        seen_all = flag(by_row < base)
        last = flag(by_row == final)
        keep = jnp.where(final < begin, 1.0, 0.0)
        last_low = rows_of(last.astype(BF16), d)
        carried = jnp.where((begin == base) | (start_of(lens, m, begin - 1) < base), 1.0, 0.0)
        gnum_seen = gnum * seen
        k_last, v_last = k * last_low, v * last_low
        gden_q = gden * q.astype(F32)
        dk_den = nn(turned, gden_q.astype(BF16)) + rows_of(last, d) * after_norm[...]
        dq_den = gden * (kc_ref[at, :].astype(F32) + rows_of(seen_all, d) * norm_in)
        for p in range(4):
            cut = slice(128 * p, 128 * p + 128)
            held = (states[c, p].astype(F32) + carried * pairs_in[p]).astype(BF16)
            g_after = after[p].astype(BF16)
            qp, kp, vp, gp = q[:, cut], k[:, cut], v[:, cut], gnum[:, cut]
            q2, k2 = split_pair(qp, low, high), split_pair(kp, low, high)
            v2, g2 = split_pair(vp, low, high), split_pair(gp, low, high)
            s_turned = nt(kp, q2).astype(BF16) * turned2
            gs_turned = nt(vp, g2).astype(BF16) * turned2
            gs = nt(gp, v2).astype(BF16) * allowed2
            dq = nn(gs, k2) + nt(gnum_seen[:, cut], held) + dq_den[:, cut]
            gq_out[at, cut] = (jnp.minimum(qp.astype(F32), 1.0) * dq).astype(BF16)
            dk = nn(gs_turned, q2) + nt(v_last[:, cut], g_after) + dk_den[:, cut]
            dk_out[at, cut] = dk.astype(BF16)
            dv = nn(s_turned, g2) + nn(k_last[:, cut], g_after)
            dv_out[at, cut] = dv.astype(BF16)
        q_turned = (q * seen).T
        mask = ones[0:128, 0:128].astype(F32)
        for p in range(4):
            cut = slice(128 * p, 128 * p + 128)
            after[p] = keep * after[p] + nn(q_turned[cut, :], gnum[:, cut]) * mask
        after_norm[...] = keep * after_norm[...] + column_sum(gden_q * seen.astype(F32))
        return carry

    lax.fori_loop(0, count, step, 0, unroll=4)


def last_kernel(lens, off, *refs):
    (q_ref, k_half, v_half, gnum_ref, gden_ref, kc_ref, states, state_in, k_ref, v_ref, x_ref,
     use, grads_up, grads_down, g_vec, ones, vec, w,
     gx_out, up_out, down_out, k_out, v_out, q_out, vector_out,
     gq_all, dk_all, dv_all, h1t_all, acc, after, after_norm, sums, shares, src_k, src_v, src_q, *rest) = refs
    micro = use.shape[0]
    rows, d = k_ref.shape
    part_rows = q_ref.shape[0]
    halves = rows // part_rows
    n = src_q.shape[0]
    each = d // n
    running = Running(use, False, rest[:13])
    rest = rest[13:]
    jobs = [
        Scatter(src, rest[13 * j : 13 * j + 13]) for j, src in enumerate((grads_up, grads_down, src_k, src_v, src_q))
    ]
    of_up, of_down, of_k, of_v, of_q = jobs
    vector = VectorSum(rest[65:])
    i = pl.program_id(0)
    base = off[0]
    p1 = halves * micro
    p2, p3 = p1 + micro, p1 + 2 * micro
    p4, end = p3 + 1, p3 + 1 + micro

    def at_step(step, *actions):
        @pl.when(i == step)
        def _():
            for action in actions:
                action()

    @pl.when(i == 0)
    def _():
        signal_all()
        acc[...] = jnp.zeros_like(acc)
        shares[...] = jnp.zeros_like(shares)

    at_step(1, wait_all, of_up.start1, of_down.start1, running.start1)
    at_step(2, of_up.finish1_start2, of_down.finish1_start2)
    at_step(3, running.finish1_start2)
    at_step(p1 - 2, of_up.finish2_start3)
    at_step(p1 - 1, running.finish2_start3)
    at_step(p1, running.finish3, of_down.finish2_start3)
    at_step(p1 + 3, of_up.finish3_start4)
    at_step(p2 + 1, of_up.finish4, of_k.finish1_start2)
    at_step(p4, of_down.finish3_start4)
    at_step(p4 + 1, of_k.finish3_start4, of_v.finish2_start3, vector.finish1_start2)
    at_step(p4 + 2, of_down.finish4, of_q.finish2_start3)
    at_step(p4 + 3, of_k.finish4, vector.finish2_start3)

    @pl.when(i < p1)
    def _():
        m, t = i // halves, halves - 1 - lax.rem(i, halves)

        @pl.when(t == halves - 1)
        def _():
            after[...] = jnp.zeros_like(after)
            after_norm[...] = jnp.zeros_like(after_norm)

        lead = t * part_rows
        at = pl.ds(pl.multiple_of(m * rows + lead, part_rows), part_rows)
        attend_back(
            lens, m, base, base + lead, q_ref, k_half, v_half, gnum_ref, gden_ref, kc_ref, states, state_in, ones,
            gq_all.at[at], dk_all.at[at], dv_all.at[at], after, after_norm,
        )

    def block(m):
        final = start_of(lens, m, base + rows - 1)
        last = flag(start_of(lens, m, place_rows(base, rows)) == final)
        groups, norm = unpack_state(running.result[m], ones[...])
        return last, rows_of(last.astype(BF16), d), groups, norm

    @pl.when((i >= p1) & (i < p2))
    def _():
        m = i - p1
        at = pl.ds(pl.multiple_of(m * rows, rows), rows)
        last, last_low, groups, norm = block(m)
        dk = dk_all[at, :].astype(F32) + rows_of(last, d) * norm
        dk = dk + by_group(lambda g, a: nt(a, groups[g]), v_ref[...] * last_low)
        gk = (jnp.minimum(k_ref[...].astype(F32), 1.0) * dk).astype(BF16)
        dk_all[at, :] = gk
        xhat, _ = normed(x_ref[...].astype(F32))
        h1t = (xhat * vec[0:1, :] + vec[1:2, :]).astype(BF16).T
        h1t_all[:, at] = h1t
        acc[:, d : 2 * d] += nn(h1t, gk)
        shares[:, d : 2 * d] += column_sum(gk.astype(F32))

    def arrange(src, part):
        for w_ in range(n):
            put(src.at[w_], 0, acc[each * w_ : each * w_ + each, d * part : d * part + d].astype(BF16))
            fill(src.at[w_], each, d)

    @pl.when(i == p2 - 1)
    def _():
        arrange(src_k, 1)
        of_k.start1()

    @pl.when((i >= p2) & (i < p3))
    def _():
        m = i - p2
        at = pl.ds(pl.multiple_of(m * rows, rows), rows)
        _, last_low, groups, _ = block(m)
        gv = dv_all[at, :].astype(F32) + by_group(lambda g, a: nn(a, groups[g]), k_ref[...] * last_low)
        gv = gv.astype(BF16)
        dv_all[at, :] = gv
        acc[:, 2 * d :] += nn(h1t_all[:, at], gv)
        shares[:, 2 * d :] += column_sum(gv.astype(F32))

    @pl.when(i == p3 - 1)
    def _():
        arrange(src_v, 2)
        of_v.start1()

    @pl.when(i == p3)
    def _():
        up_out[...] = of_up.out[...]

        def add(m, carry):
            at = pl.ds(pl.multiple_of(m * rows, rows), rows)
            gq = gq_all[at, :]
            acc[:, 0:d] += nn(h1t_all[:, at], gq)
            shares[:, 0:d] += column_sum(gq.astype(F32))
            return carry

        lax.fori_loop(0, micro // 2, add, 0)
        of_k.finish2_start3()
        of_v.finish1_start2()
        lax.fori_loop(micro // 2, micro, add, 0)
        arrange(src_q, 0)
        of_q.start1()
        both = jnp.zeros((d, 128), F32)
        only = jnp.zeros((d, 128), F32)
        for j in range(3 * d // 128):
            cut = slice(128 * j, 128 * j + 128)
            weight = w[:, cut].astype(F32)
            both = both + weight * acc[:, cut]
            only = only + weight * shares[:, cut]
        both, only = column_sum(both.T), column_sum(only.T)
        sums[...] = g_vec[...]
        sums[0:1, :] = (both - vec[1:2, :] * only) / vec[0:1, :]
        sums[1:2, :] = only
        owner_tiles(sums[...], vector.tiles, each)
        vector.start1()
        of_q.finish1_start2()

    @pl.when(i >= p4)
    def _():
        at = pl.ds(pl.multiple_of((i - p4) * rows, rows), rows)
        e = nt(gq_all[at, :], w[:, 0:d]) + nt(dk_all[at, :], w[:, d : 2 * d]) + nt(dv_all[at, :], w[:, 2 * d :])
        xhat, scale = normed(x_ref[...].astype(F32))
        gx_out[...] = norm_back(e, xhat, scale, vec[0:1, :]).astype(BF16)

    @pl.when(i == end - 1)
    def _():
        of_v.finish3_start4()
        of_q.finish3_start4()
        down_out[...] = of_down.out[...]
        k_out[...] = of_k.out[...]
        vector_out[...] = vector.finish3()
        of_v.finish4()
        v_out[...] = of_v.out[...]
        of_q.finish4()
        q_out[...] = of_q.out[...]


def result_kernel(
    gm_ref, part_ref, of_up, of_down, of_k, of_v, of_q, vector, gx, g_qkv, g_out, g_up, g_down, v0, v1, v2, v3, v4, v5
):
    gx[...] = gm_ref[...].astype(F32) + part_ref[...].astype(F32)

    @pl.when(pl.program_id(0) == 0)
    def _():
        each, d = g_out.shape
        for j in range(4):
            g_up[:, d * j : d * j + d] = get(of_up, each * j, each, d).astype(F32)
        g_out[...] = get(of_up, 4 * each, each, d).astype(F32)
        g_down[...] = get(of_down, 0, 4 * each, d).astype(F32)
        for j, part in enumerate((of_q, of_k, of_v)):
            g_qkv[:, d * j : d * j + d] = get(part, 0, each, d).astype(F32)
        for j, v in enumerate((v0, v1, v2, v3, v4)):
            v[...] = vector[j : j + 1, :each]
        for r in range(4):
            v5[:, each * r : each * r + each] = vector[5 + r : 6 + r, :each]


def params(count):
    return pltpu.CompilerParams(
        dimension_semantics=("arbitrary",) * count, vmem_limit_bytes=VMEM
    )


def small():
    return pl.BlockSpec(memory_space=pltpu.SMEM)


def per_device(
    block_in, cotangent, ln1_gain, ln1_bias, qkv_weight, out_weight, ln2_gain, ln2_bias,
    up_weight, up_bias, down_weight, down_bias, seq_lengths,
):
    micro, rows, d = block_in.shape[0], block_in.shape[2], block_in.shape[3]
    ff = up_weight.shape[1]
    wide, index = lax.axis_size("wide"), lax.axis_index("wide")
    lens = seq_lengths.reshape(micro, -1)
    off = (index * rows).astype(jnp.int32).reshape(1)
    x = block_in.reshape(micro, rows, d)
    cot = cotangent.reshape(micro, rows, d)

    each = d // wide
    lane = jnp.arange(256) // 64
    ones = (lane[:, None] == lane[None, :]).astype(BF16)

    tiles = rows // TILE
    token = pl.BlockSpec((None, TILE, d), lambda m, t: (m, t, 0))
    whole = lambda shape: pl.BlockSpec(shape, lambda *_: (0,) * len(shape))
    fixed = lambda shape: pl.BlockSpec(
        shape, lambda *_: (0,) * len(shape), pipeline_mode=pl.Buffered(1)
    )
    packed = pl.BlockSpec((None, state_rows(), 128), lambda m, *_: (m, 0, 0))
    like = lambda dtype: jax.ShapeDtypeStruct((micro, rows, d), dtype)
    up_shape, down_shape = packed_shape(5 * each, d), packed_shape(4 * each, d)

    block = pl.BlockSpec((None, rows, d), lambda m: (m, 0, 0))
    count = rows // CHUNK
    states_spec = pl.BlockSpec((None, count, 2, 256, 256), lambda m: (m, 0, 0, 0, 0))
    during = lambda begin, *shape: pl.BlockSpec(
        (None,) + shape, lambda i: (jnp.clip(i - begin, 0, micro - 1),) + (0,) * len(shape)
    )
    anywhere = pl.BlockSpec(memory_space=pl.ANY)
    spread = lambda a: jax.ShapeDtypeStruct((wide,) + a.shape, BF16)
    dma = pltpu.SemaphoreType.DMA
    vectors = [a.reshape(1, -1) for a in (ln1_gain, ln1_bias, ln2_gain, ln2_bias, down_bias, up_bias)]
    state_shape = (micro, state_rows(), 128)
    (q, k, v, num, kc, states, state_in, w_qkv, w_out, w_up, w_down, vec) = pl.pallas_call(
        first_kernel,
        grid=(4 * micro,),
        in_specs=[small(), small(), fixed((micro, rows, d))] + [anywhere] * 4 + [whole(a.shape) for a in vectors] + [whole((256, 256))],
        out_specs=[during(micro * j, rows, d) for j in range(3)] + [during(3 * micro, rows, d)] * 2
        + [during(3 * micro, count, 4, 128, 128), whole(state_shape)]
        + [anywhere] * 4 + [whole((16, d))],
        out_shape=[like(BF16)] * 5 + [
            jax.ShapeDtypeStruct((micro, count, 4, 128, 128), BF16), jax.ShapeDtypeStruct(state_shape, F32),
            spread(qkv_weight), spread(out_weight), spread(up_weight), spread(down_weight),
            jax.ShapeDtypeStruct((16, d), F32),
        ],
        scratch_shapes=[pltpu.VMEM((3, wide, each, d), BF16)]
        + [pltpu.VMEM((micro, rows, d), BF16)] * 4
        + [
            pltpu.VMEM((4, 128, 128), F32), pltpu.VMEM((1, d), F32), pltpu.VMEM(state_shape, BF16), pltpu.VMEM((16, 128), BF16), pltpu.VMEM((wide, 16, 128), BF16),
            dma, dma((wide,)), dma((wide,)), dma((3,)),
        ]
        + running_scratch(micro // 2) * 2
        + gather_sems() * 8,
        compiler_params=pltpu.CompilerParams(
            dimension_semantics=("arbitrary",), vmem_limit_bytes=VMEM, collective_id=0, has_side_effects=True
        ),
        name="first",
    )(lens, off, x, qkv_weight, out_weight, up_weight, down_weight, *vectors, ones)
    w_qkv, w_out = w_qkv.reshape(d, 3 * d), w_out.reshape(d, d)
    w_up, w_down = w_up.reshape(d, ff), w_down.reshape(ff, d)

    result, g_middle, gnum, gden, use, grads_up, grads_down, g_vec = pl.pallas_call(
        middle_kernel,
        grid=(micro, tiles),
        in_specs=[small(), small()] + [token] * 5 + [packed, whole((256, 256))] + [
            fixed((d, d)), whole((16, d)), fixed((d, ff)), fixed((ff, d)),
        ],
        out_specs=[token, token, token, token, packed, fixed((wide,) + up_shape), fixed((wide,) + down_shape), whole((16, d))],
        out_shape=[
            like(BF16), like(BF16), like(BF16), like(BF16), jax.ShapeDtypeStruct(state_shape, BF16),
            jax.ShapeDtypeStruct((wide,) + up_shape, BF16), jax.ShapeDtypeStruct((wide,) + down_shape, BF16),
            jax.ShapeDtypeStruct((16, d), F32),
        ],
        scratch_shapes=[
            pltpu.VMEM((2, 256, 256), BF16), pltpu.VMEM((1, d), F32),
            pltpu.VMEM((2, 256, 256), F32), pltpu.VMEM((1, d), F32),
            pltpu.VMEM((d, d), F32), pltpu.VMEM((d + 16, ff), F32), pltpu.VMEM((d, ff), F32),
            pltpu.VMEM((TILE, d), F32), pltpu.VMEM((TILE, d), F32), pltpu.VMEM((TILE, d), BF16),
            pltpu.VMEM((d + 16, TILE), BF16), pltpu.VMEM((d, TILE), BF16),
        ],
        compiler_params=params(2),
        name="middle",
    )(lens, off, q, num, kc, x, cot, state_in, ones, w_out, vec, w_up, w_down)

    spare = 2 if wide <= 8 else 1
    halves = rows // TILE
    p1 = halves * micro
    p2, p4 = p1 + micro, p1 + 2 * micro + 1

    def backward(*shape):
        def at(i):
            i = jnp.minimum(i, p1 - 1)
            return (i // halves, halves - 1 - lax.rem(i, halves)) + (0,) * (len(shape) - 1)

        return pl.BlockSpec((None,) + shape, at)

    def walk(*begins, buffers=2):
        def at(i):
            j = 0
            for b in begins:
                j = j + jnp.where(i >= b, jnp.clip(i - b, 0, micro - 1) - j, 0)
            return (j, 0, 0)

        return pl.BlockSpec((None, rows, d), at, pipeline_mode=pl.Buffered(buffers))

    part_shape = packed_shape(each, d)
    vector_shapes = [(1, each)] * 5 + [(1, 4 * each)]
    summed_shapes = [up_shape, down_shape, part_shape, part_shape, part_shape, (16, 128)]
    result_shapes = [(each, 3 * d), (each, d), (each, ff), (4 * each, d)] + vector_shapes
    part, *summed = pl.pallas_call(
        last_kernel,
        grid=(p4 + micro,),
        in_specs=[small(), small()] + [backward(TILE, d)] * 6 + [backward(count // halves, 4, 128, 128)]
        + [pl.BlockSpec((None, state_rows(), 128), lambda i: (jnp.minimum(i // halves, micro - 1), 0, 0))]
        + [walk(p1, p2, buffers=spare), walk(p1, buffers=spare), walk(p1, p4, buffers=spare)] + [anywhere] * 3
        + [whole((16, d)), whole((256, 256)), whole((16, d)), fixed((d, 3 * d))],
        out_specs=[walk(p4)] + [fixed(s) for s in summed_shapes],
        out_shape=[like(BF16)] + [jax.ShapeDtypeStruct(s, BF16) for s in summed_shapes[:5]]
        + [jax.ShapeDtypeStruct((16, 128), F32)],
        scratch_shapes=[pltpu.VMEM((micro * rows, d), BF16)] * 3
        + [
            pltpu.VMEM((d, micro * rows), BF16), pltpu.VMEM((d, 3 * d), F32),
            pltpu.VMEM((4, 128, 128), F32), pltpu.VMEM((1, d), F32),
            pltpu.VMEM((16, d), F32), pltpu.VMEM((1, 3 * d), F32),
        ]
        + [pltpu.VMEM((wide,) + part_shape, BF16)] * 3
        + running_scratch(micro)
        + scatter_scratch(up_shape) + scatter_scratch(down_shape) + scatter_scratch(part_shape) * 3
        + vector_scratch(),
        compiler_params=pltpu.CompilerParams(
            dimension_semantics=("arbitrary",), vmem_limit_bytes=VMEM, collective_id=1, has_side_effects=True
        ),
        name="last",
    )(lens, off, q, k, v, gnum, gden, kc, states, state_in, k, v, x, use, grads_up, grads_down, g_vec, ones, vec, w_qkv)
    grad_input, g_qkv, g_out, g_up, g_down, *g_vectors = pl.pallas_call(
        result_kernel,
        grid=(micro,),
        in_specs=[block, block] + [whole(s) for s in summed_shapes],
        out_specs=[block] + [whole(s) for s in result_shapes],
        out_shape=[like(F32)] + [jax.ShapeDtypeStruct(s, F32) for s in result_shapes],
        compiler_params=params(1),
        name="result",
    )(g_middle, part, *summed)
    piece = [a.reshape(-1) for a in g_vectors]
    return (
        result.reshape(block_in.shape),
        grad_input.reshape(block_in.shape),
        piece[0],
        piece[1],
        g_qkv,
        g_out,
        piece[2],
        piece[3],
        g_up,
        piece[5],
        g_down,
        piece[4],
    )


def solution(mesh):
    tokens = P(None, "dp", "wide", None)
    vector, matrix = P("wide"), P("wide", None)
    weights = (vector, vector, matrix, matrix, vector, vector, matrix, vector, matrix, vector)
    return jax.shard_map(
        per_device,
        mesh=mesh,
        in_specs=(tokens, tokens) + weights + (P(None, "dp", None),),
        out_specs=(tokens, tokens) + weights,
        check_vma=False,
    )
```

```python
import functools

import jax
import jax.numpy as jnp
from jax import lax
from jax.experimental import pallas as pl
from jax.experimental.pallas import tpu as pltpu
from jax.sharding import PartitionSpec as P

HEADS = 8
EPSILON = 1e-05
F32 = jnp.float32
BF16 = jnp.bfloat16
CHUNK = 128
TILE = 512
FF_TILE = 512
VMEM = 62 * 1024 * 1024


def nn(a, b):
    return lax.dot_general(a, b, (((1,), (0,)), ((), ())), preferred_element_type=F32)


def nt(a, b):
    return lax.dot_general(a, b, (((1,), (1,)), ((), ())), preferred_element_type=F32)


def rows_of(row, width):
    return jnp.concatenate([row] * (width // 128), axis=1)


def start_of(lens, m, place):
    start, end = jnp.zeros_like(place), 0
    for j in range(lens.shape[1]):
        end = end + lens[m, j]
        start = start + jnp.where(end <= place, lens[m, j], 0)
    return start


def place_rows(first, count):
    return first + lax.broadcasted_iota(jnp.int32, (count, 128), 0)


def flag(condition):
    return jnp.where(condition, 1.0, 0.0)


def normed(x):
    average = jnp.mean(x, axis=-1, keepdims=True)
    centred = x - average
    spread = jnp.mean(centred * centred, axis=-1, keepdims=True)
    scale = lax.rsqrt(spread + EPSILON)
    return centred * scale, scale


def norm_back(e, xhat, scale, gain):
    a = gain * e
    return scale * (
        a - jnp.mean(a, axis=-1, keepdims=True) - xhat * jnp.mean(a * xhat, axis=-1, keepdims=True)
    )


def feature(v):
    return jnp.where(v > 0.0, v + 1.0, jnp.exp(jnp.minimum(v, 0.0)))


def column_sum(a):
    return jnp.sum(a, axis=0, keepdims=True)


def by_group(fn, *arrays):
    return jnp.concatenate(
        [fn(g, *[a[:, 256 * g : 256 * g + 256] for a in arrays]) for g in range(2)], axis=1
    )


def lane_half(shape):
    return lax.broadcasted_iota(jnp.int32, shape, 1) < 64


def pack_state(state, norm, out):
    folded = [s + pltpu.roll(s, 64, 1) for s in state]
    half = lane_half((128, 128))
    for j in range(2):
        out[128 * j : 128 * j + 128, :] = jnp.where(half, folded[j], folded[2 + j]).astype(out.dtype)
    row = lax.broadcasted_iota(jnp.int32, (16, 128), 0)
    tail = jnp.zeros((16, 128), F32)
    for j in range(4):
        tail = jnp.where(row == j, norm[:, 128 * j : 128 * j + 128], tail)
    out[256:272, :] = tail.astype(out.dtype)
    if out.shape[0] > 272:
        out[272:, :] = jnp.zeros((out.shape[0] - 272, 128), out.dtype)


def unpack_pairs(packed, ones):
    half = lane_half((128, 128))
    mask = ones[0:128, 0:128].astype(F32)
    pairs = [None] * 4
    for j in range(2):
        z = packed[128 * j : 128 * j + 128, :]
        turned = pltpu.roll(z, 64, 1)
        pairs[j] = jnp.where(half, z, turned) * mask
        pairs[2 + j] = jnp.where(half, turned, z) * mask
    tail = packed[256:272, :]
    norm = jnp.concatenate([tail[j : j + 1, :] for j in range(4)], axis=1)
    return pairs, norm


def unpack_state(packed, ones):
    pairs, norm = unpack_pairs(packed, ones)
    zero = jnp.zeros((128, 128), BF16)
    groups = []
    for g in range(2):
        above = jnp.concatenate([pairs[2 * g].astype(BF16), zero], axis=1)
        below = jnp.concatenate([zero, pairs[2 * g + 1].astype(BF16)], axis=1)
        groups.append(jnp.concatenate([above, below], axis=0))
    return groups, norm


MESH = pl.DeviceIdType.MESH


def place():
    dp = lax.axis_index("dp")
    return lax.rem(dp, 2), dp // 2, lax.axis_index("wide"), lax.axis_size("dp") // 2, lax.axis_size("wide")


def others(count, fn):
    def body(o, carry):
        fn(o)
        return carry

    lax.fori_loop(1, count, body, 0)


def remote(src, dst, send, recv, dp, wide):
    return pltpu.make_async_remote_copy(
        src_ref=src, dst_ref=dst, send_sem=send, recv_sem=recv, device_id=(dp, wide), device_id_type=MESH
    )


def signal_all():
    core, y, me, ny, n = place()
    dp = 2 * y + core
    barrier = pltpu.get_barrier_semaphore()

    def signal(d, w):
        pl.semaphore_signal(barrier, inc=1, device_id=(d, w), device_id_type=MESH)

    others(n, lambda o: signal(dp, lax.rem(me + o, n)))
    others(2 * ny, lambda o: signal(lax.rem(dp + o, 2 * ny), me))


def wait_all():
    _, _, _, ny, n = place()
    pl.semaphore_wait(pltpu.get_barrier_semaphore(), n - 1 + 2 * ny - 1)


class Gather:
    def __init__(self, src, dst, sems):
        self.src, self.dst = src, dst
        self.near, self.send, self.recv, self.y_send, self.y_recv, self.c_send, self.c_recv = sems
        self.core, self.y, self.me, self.ny, self.n = place()
        self.dp = 2 * self.y + self.core
        each = src.shape[0]
        self.split = split_of(each)
        part = each // self.split
        if self.split == 1:
            self.rows, self.half = pl.ds(0, each), None
        else:
            at = self.core * (each // 2) + self.y * part
            self.rows = pl.ds(pl.multiple_of(at, part), part)
            self.half = pl.ds(pl.multiple_of(self.core * (each // 2), each // 2), each // 2)

    def own(self):
        return pltpu.make_async_copy(self.src.at[self.rows], self.dst.at[self.me, self.rows], self.near)

    def out(self, o):
        to = lax.rem(self.me + o, self.n)
        return remote(self.src.at[self.rows], self.dst.at[self.me, self.rows], self.send.at[o], self.recv.at[self.me], self.dp, to)

    def back(self, o):
        frm = lax.rem(self.me + o, self.n)
        part = self.dst.at[frm, self.rows]
        return remote(part, part, self.send.at[o], self.recv.at[frm], self.dp, frm)

    def start_wide(self):
        self.own().start()
        others(self.n, lambda o: self.out(o).start())

    def finish_wide(self):
        self.own().wait()
        others(self.n, lambda o: self.out(o).wait_send())
        others(self.n, lambda o: self.back(o).wait_recv())

    def along_y(self, o):
        part = self.dst.at[:, self.rows]
        to = lax.rem(self.y + o, self.ny)
        return remote(part, part, self.y_send.at[o], self.y_recv.at[self.y], 2 * to + self.core, self.me)

    def along_y_back(self, o):
        frm = lax.rem(self.y + o, self.ny)
        each = self.src.shape[0]
        part = each // self.split
        at = self.core * (each // 2) + frm * part
        ref = self.dst.at[:, pl.ds(pl.multiple_of(at, part), part)]
        return remote(ref, ref, self.y_send.at[o], self.y_recv.at[frm], 2 * frm + self.core, self.me)

    def start_y(self):
        if self.split > 1:
            others(self.ny, lambda o: self.along_y(o).start())

    def finish_y(self):
        if self.split > 1:
            others(self.ny, lambda o: self.along_y(o).wait_send())
            others(self.ny, lambda o: self.along_y_back(o).wait_recv())

    def cross(self):
        part = self.dst.at[:, self.half]
        return remote(part, part, self.c_send, self.c_recv, 2 * self.y + 1 - self.core, self.me)

    def cross_back(self):
        each = self.src.shape[0]
        at = (1 - self.core) * (each // 2)
        part = self.dst.at[:, pl.ds(pl.multiple_of(at, each // 2), each // 2)]
        return remote(part, part, self.c_send, self.c_recv, 2 * self.y + 1 - self.core, self.me)

    def start_core(self):
        if self.split > 1:
            self.cross().start()

    def finish_core(self):
        if self.split > 1:
            self.cross().wait_send()
            self.cross_back().wait_recv()


def split_of(each):
    count = lax.axis_size("dp")
    return count if each % (16 * count) == 0 else 1


def gather_sems():
    n, ny = lax.axis_size("wide"), lax.axis_size("dp") // 2
    dma = pltpu.SemaphoreType.DMA
    return [dma, dma((n,)), dma((n,)), dma((ny,)), dma((ny,)), dma, dma]


def packed_shape(rows, d):
    unit = 16 * lax.axis_size("dp")
    columns = d if rows % unit == 0 else 128
    rows = rows * (d // columns)
    return -(-rows // unit) * unit, columns


def put(block, at, piece):
    rows, d = piece.shape
    columns = block.shape[1]
    for b in range(d // columns):
        begin = at * (d // columns) + rows * b
        block[begin : begin + rows, :] = piece[:, columns * b : columns * b + columns]


def fill(block, rows, d):
    used = rows * (d // block.shape[1])
    if block.shape[0] > used:
        block[used:, :] = jnp.zeros((block.shape[0] - used, block.shape[1]), block.dtype)


def get(block, at, rows, d):
    columns = block.shape[1]
    begin = at * (d // columns)
    return jnp.concatenate(
        [block[begin + rows * b : begin + rows * b + rows, :] for b in range(d // columns)], axis=1
    )


class Scatter:
    def __init__(self, src, refs):
        self.src = src
        (self.half, self.got_core, self.got_y, self.got_wide, self.out, self.near, self.c_sem, self.y_send,
         self.y_recv, self.w_send, self.w_recv, self.b_send, self.b_recv) = refs
        self.core, self.y, self.me, self.ny, self.n = place()
        self.dp = 2 * self.y + self.core
        self.rows = self.out.shape[0]
        self.each = self.rows // (2 * self.ny)
        self.partner = 2 * self.y + 1 - self.core
        self.part = self.got_core.at[:, 0 : self.each]

    def half_rows(self, core):
        return pl.ds(pl.multiple_of(core * (self.rows // 2), self.rows // 2), self.rows // 2)

    def y_rows(self, y):
        return pl.ds(pl.multiple_of(y * self.each, self.each), self.each)

    def own_rows(self, y):
        at = self.core * (self.rows // 2) + y * self.each
        return pl.ds(pl.multiple_of(at, self.each), self.each)

    def load(self):
        return pltpu.make_async_copy(self.src.at[:, self.half_rows(self.core)], self.half, self.near)

    def cross(self):
        return remote(
            self.src.at[:, self.half_rows(1 - self.core)], self.got_core, self.c_sem.at[0], self.c_sem.at[1], self.partner, self.me
        )

    def start1(self):
        self.cross().start()
        self.load().start()

    def along_y(self, o):
        to = lax.rem(self.y + o, self.ny)
        return remote(
            self.half.at[:, self.y_rows(to)], self.got_y.at[o - 1], self.y_send.at[o], self.y_recv.at[o],
            2 * to + self.core, self.me,
        )

    def finish1_start2(self):
        self.load().wait()
        self.cross().wait()

        def add(w, carry):
            self.half[w] = (self.half[w].astype(F32) + self.got_core[w].astype(F32)).astype(BF16)
            return carry

        lax.fori_loop(0, self.n, add, 0)
        others(self.ny, lambda o: self.along_y(o).start())

    def along_wide(self, o):
        to = lax.rem(self.me + o, self.n)
        return remote(self.part.at[to], self.got_wide.at[o - 1], self.w_send.at[o], self.w_recv.at[o], self.dp, to)

    def finish2_start3(self):
        others(self.ny, lambda o: self.along_y(o).wait())

        def add(w, carry):
            total = self.half[w, self.y_rows(self.y)].astype(F32)
            for o in range(self.ny - 1):
                total = total + self.got_y[o, w].astype(F32)
            self.part[w] = total.astype(BF16)
            return carry

        lax.fori_loop(0, self.n, add, 0)
        others(self.n, lambda o: self.along_wide(o).start())

    def back(self, o, wait=False):
        other = lax.rem(self.dp + o, 2 * self.ny)
        slot = other if wait else self.dp
        at = lax.rem(slot, 2) * (self.rows // 2) + (slot // 2) * self.each
        ref = self.out.at[pl.ds(pl.multiple_of(at, self.each), self.each)]
        return remote(ref, ref, self.b_send.at[o], self.b_recv.at[slot], other, self.me)

    def finish3_start4(self):
        others(self.n, lambda o: self.along_wide(o).wait())
        total = self.part[self.me].astype(F32)
        total = lax.fori_loop(0, self.n - 1, lambda o, t: t + self.got_wide[o].astype(F32), total)
        self.out[self.own_rows(self.y)] = total.astype(BF16)
        others(2 * self.ny, lambda o: self.back(o).start())

    def finish4(self):
        others(2 * self.ny, lambda o: self.back(o).wait_send())
        others(2 * self.ny, lambda o: self.back(o, True).wait_recv())


def scatter_scratch(shape):
    rows, d = shape
    n, dp = lax.axis_size("wide"), lax.axis_size("dp")
    ny, part = dp // 2, rows // dp
    dma = pltpu.SemaphoreType.DMA
    return [
        pltpu.VMEM((n, rows // 2, d), BF16),
        pltpu.VMEM((n, rows // 2, d), BF16),
        pltpu.VMEM((ny - 1, n, part, d), BF16),
        pltpu.VMEM((n - 1, part, d), BF16),
        pltpu.VMEM((rows, d), BF16),
        dma, dma((2,)), dma((ny,)), dma((ny,)), dma((n,)), dma((n,)), dma((dp,)), dma((dp,)),
    ]


class VectorSum:
    def __init__(self, refs):
        self.tiles, self.got_core, self.got_y, self.got_wide, self.c_sem, self.y_send, self.y_recv, self.w_send, self.w_recv = refs
        self.core, self.y, self.me, self.ny, self.n = place()
        self.dp = 2 * self.y + self.core

    def cross(self):
        return remote(self.tiles, self.got_core, self.c_sem.at[0], self.c_sem.at[1], 2 * self.y + 1 - self.core, self.me)

    def along_y(self, o):
        to = lax.rem(self.y + o, self.ny)
        return remote(self.tiles, self.got_y.at[o - 1], self.y_send.at[o], self.y_recv.at[o], 2 * to + self.core, self.me)

    def along_wide(self, o):
        to = lax.rem(self.me + o, self.n)
        return remote(self.tiles.at[to], self.got_wide.at[o - 1], self.w_send.at[o], self.w_recv.at[o], self.dp, to)

    def start1(self):
        self.cross().start()

    def finish1_start2(self):
        self.cross().wait()
        self.tiles[...] = self.tiles[...] + self.got_core[...]
        others(self.ny, lambda o: self.along_y(o).start())

    def finish2_start3(self):
        others(self.ny, lambda o: self.along_y(o).wait())
        total = self.tiles[...]
        for o in range(self.ny - 1):
            total = total + self.got_y[o]
        self.tiles[...] = total
        others(self.n, lambda o: self.along_wide(o).start())

    def finish3(self):
        others(self.n, lambda o: self.along_wide(o).wait())
        return lax.fori_loop(0, self.n - 1, lambda o, t: t + self.got_wide[o], self.tiles[self.me])


def vector_scratch():
    n, ny = lax.axis_size("wide"), lax.axis_size("dp") // 2
    dma = pltpu.SemaphoreType.DMA
    return [
        pltpu.VMEM((n, 16, 128), F32),
        pltpu.VMEM((n, 16, 128), F32),
        pltpu.VMEM((ny - 1, n, 16, 128), F32),
        pltpu.VMEM((n - 1, 16, 128), F32),
        dma((2,)), dma((ny,)), dma((ny,)), dma((n,)), dma((n,)),
    ]


def owner_tiles(rows, tiles, each):
    n = tiles.shape[0]
    d = each * n
    per = 4 * each
    row = lax.broadcasted_iota(jnp.int32, (16, 128), 0)
    lane = lax.broadcasted_iota(jnp.int32, (16, 128), 1)
    blocks = [rows[:, 128 * j : 128 * j + 128] for j in range(d // 128)]

    def turned(a, by, axis):
        by = by % a.shape[axis]
        return pltpu.roll(a, by, axis) if by else a

    for w in range(n):
        at = each * w
        tile = jnp.where(row < 5, turned(blocks[at // 128], -(at % 128), 1), 0.0)
        for r in range(4):
            at = per * w + each * r
            from_row, begin = 5 + at // d, at % d
            moved = turned(turned(blocks[begin // 128], -(begin % 128), 1), 5 + r - from_row, 0)
            tile = jnp.where(row == 5 + r, moved, tile)
        tiles[w] = jnp.where(lane < each, tile, 0.0)


HIGH = 4


def low_count():
    return lax.axis_size("wide") // HIGH


def state_rows():
    unit = 16 * low_count()
    return -(-272 // unit) * unit


class Running:
    def __init__(self, own, upward, refs):
        self.own, self.upward = own, upward
        (self.slots, self.group, self.high, self.mine, self.spread, self.result, self.near, self.send1, self.recv1,
         self.send2, self.recv2, self.send3, self.recv3) = refs
        _, _, self.me, _, _ = place()
        self.dp = lax.axis_index("dp")
        self.lo = low_count()
        self.h, self.l = self.me // self.lo, lax.rem(self.me, self.lo)
        self.part = state_rows() // self.lo

    def slice(self, l):
        return pl.ds(pl.multiple_of(l * self.part, self.part), self.part)

    def copy1(self, o, back=False):
        other = lax.rem(self.l + o, self.lo)
        slot = other if back else self.l
        return remote(self.own, self.slots.at[slot], self.send1.at[o], self.recv1.at[slot], self.dp, self.h * self.lo + other)

    def near1(self):
        return pltpu.make_async_copy(self.own, self.slots.at[self.l], self.near.at[0])

    def start1(self):
        self.near1().start()
        others(self.lo, lambda o: self.copy1(o).start())

    def before(self, a, b):
        return a < b if self.upward else a > b

    def finish1_start2(self):
        self.near1().wait()
        others(self.lo, lambda o: self.copy1(o).wait_send())
        others(self.lo, lambda o: self.copy1(o, True).wait_recv())
        every = jnp.zeros(self.own.shape, F32)
        inner = every
        for l in range(self.lo):
            part = self.slots[l].astype(F32)
            every = every + part
            inner = inner + jnp.where(self.before(l, self.l), part, 0.0)
        self.group[...] = every.astype(BF16)
        self.result[...] = inner

        def send(o):
            other = lax.rem(self.h + o, HIGH)

            @pl.when(self.before(self.h, other))
            def _():
                self.copy2(o).start()

        others(HIGH, send)

    def copy2(self, o, back=False):
        other = lax.rem(self.h + o, HIGH)
        slot = other if back else self.h
        return remote(
            self.group.at[:, self.slice(self.l)], self.high.at[slot], self.send2.at[o], self.recv2.at[slot],
            self.dp, other * self.lo + self.l,
        )

    def finish2_start3(self):
        def wait(o):
            other = lax.rem(self.h + o, HIGH)

            @pl.when(self.before(self.h, other))
            def _():
                self.copy2(o).wait_send()

            @pl.when(self.before(other, self.h))
            def _():
                self.copy2(o, True).wait_recv()

        others(HIGH, wait)
        total = jnp.zeros(self.mine.shape, F32)
        for h in range(HIGH):
            total = total + jnp.where(self.before(h, self.h), self.high[h].astype(F32), 0.0)
        self.mine[...] = total.astype(BF16)
        self.near3().start()
        others(self.lo, lambda o: self.copy3(o).start())

    def near3(self):
        return pltpu.make_async_copy(self.mine, self.spread.at[self.l], self.near.at[1])

    def copy3(self, o, back=False):
        other = lax.rem(self.l + o, self.lo)
        slot = other if back else self.l
        return remote(self.mine, self.spread.at[slot], self.send3.at[o], self.recv3.at[slot], self.dp, self.h * self.lo + other)

    def finish3(self):
        self.near3().wait()
        others(self.lo, lambda o: self.copy3(o).wait_send())
        others(self.lo, lambda o: self.copy3(o, True).wait_recv())
        for l in range(self.lo):
            rows = slice(l * self.part, (l + 1) * self.part)
            self.result[:, rows] = self.result[:, rows] + self.spread[l].astype(F32)


def running_scratch(micro):
    lo, rows = low_count(), state_rows()
    dma = pltpu.SemaphoreType.DMA
    return [
        pltpu.VMEM((lo, micro, rows, 128), BF16),
        pltpu.VMEM((micro, rows, 128), BF16),
        pltpu.VMEM((HIGH, micro, rows // lo, 128), BF16),
        pltpu.VMEM((micro, rows // lo, 128), BF16),
        pltpu.VMEM((lo, micro, rows // lo, 128), BF16),
        pltpu.VMEM((micro, rows, 128), F32),
        dma((2,)), dma((lo,)), dma((lo,)), dma((HIGH,)), dma((HIGH,)), dma((lo,)), dma((lo,)),
    ]


def vector_tile(vectors, each):
    row = lax.broadcasted_iota(jnp.int32, (16, 128), 0)

    def padded(piece):
        return jnp.concatenate([piece.astype(F32), jnp.zeros((1, 128 - each), F32)], axis=1)

    pieces = [padded(v[...]) for v in vectors[:5]]
    hidden = vectors[5][...]
    pieces += [padded(hidden[:, each * r : each * r + each]) for r in range(hidden.shape[1] // each)]
    tile = jnp.zeros((16, 128), F32)
    for j, piece in enumerate(pieces):
        tile = jnp.where(row == j, piece, tile)
    return tile.astype(BF16)


def spread_vectors(slots, out, each):
    n = slots.shape[0]
    d = each * n
    per = 4 * each
    row = lax.broadcasted_iota(jnp.int32, (16, 128), 0)
    blocks = [jnp.zeros((16, 128), F32) for _ in range(d // 128)]
    for w in range(n):
        tile = slots[w].astype(F32)
        at = each * w
        moved = pltpu.roll(tile, at % 128, 1) if at % 128 else tile
        blocks[at // 128] = blocks[at // 128] + jnp.where(row < 5, moved, 0.0)
        for r in range(4):
            at = per * w + each * r
            to_row, lane = 5 + at // d, at % d
            only = jnp.where(row == 5 + r, tile, 0.0)
            moved = pltpu.roll(only, lane % 128, 1) if lane % 128 else only
            if to_row != 5 + r:
                moved = pltpu.roll(moved, (to_row - 5 - r) % 16, 0)
            blocks[lane // 128] = blocks[lane // 128] + moved
    for j, block in enumerate(blocks):
        out[:, 128 * j : 128 * j + 128] = block


def first_kernel(lens, off, x, *refs):
    (s_qkv, s_out, s_up, s_down, v0, v1, v2, v3, v4, v5, ones,
     q_out, k_out, v_out, num_out, kc_out, states_out, state_in, w_qkv, w_out, w_up, w_down, vec_out,
     w_ref, h_all, q_all, k_all, v_all, state, norm, local, tile, tiles_ref, tile_near, tile_send, tile_recv,
     save_sem, *rest) = refs
    each = s_qkv.shape[0]
    micro, rows, d = x.shape
    half = micro // 2
    running = []
    for j in range(2):
        running.append(Running(local.at[half * j : half * j + half], True, rest[:13]))
        rest = rest[13:]
    jobs = []
    for j in range(3):
        jobs.append(Gather(s_qkv.at[:, d * j : d * j + d], w_ref.at[j], rest[7 * j : 7 * j + 7]))
    pieces = [(s_out, w_out)]
    for src, dst in ((s_up, w_up), (s_down, w_down)):
        columns = src.shape[1] // 2
        pieces += [(src.at[:, c : c + columns], dst.at[:, :, c : c + columns]) for c in (0, columns)]
    for j, (src, dst) in enumerate(pieces):
        jobs.append(Gather(src, dst, rest[21 + 7 * j : 28 + 7 * j]))
    i = pl.program_id(0)
    core, y, me, ny, n = place()
    dp = 2 * y + core

    def vec_copy(o, back=False):
        other = lax.rem(me + o, n)
        slot = other if back else me
        return remote(tile, tiles_ref.at[slot], tile_send.at[o], tile_recv.at[slot], dp, other)

    def vec_near():
        return pltpu.make_async_copy(tile, tiles_ref.at[me], tile_near)

    def save(j):
        return pltpu.make_async_copy(w_ref.at[j], w_qkv.at[:, :, d * j : d * j + d], save_sem.at[j])

    def weights(j):
        return w_ref[j].reshape(d, d)

    @pl.when(i == 0)
    def _():
        signal_all()
        tile[...] = vector_tile((v0, v1, v2, v3, v4, v5), each)
        wait_all()
        vec_near().start()
        others(n, lambda o: vec_copy(o).start())
        for job in jobs[:3]:
            job.start_wide()
        vec_near().wait()
        others(n, lambda o: vec_copy(o).wait_send())
        others(n, lambda o: vec_copy(o, True).wait_recv())
        spread_vectors(tiles_ref, vec_out, each)

        def norm_micro(m, carry):
            xhat, _ = normed(x[m].astype(F32))
            h_all[m] = (xhat * vec_out[0:1, :] + vec_out[1:2, :]).astype(BF16)
            return carry

        lax.fori_loop(0, micro // 2, norm_micro, 0)
        jobs[0].finish_wide()
        jobs[0].start_y()
        lax.fori_loop(micro // 2, micro, norm_micro, 0)
        for job in jobs[1:3]:
            job.finish_wide()
            job.start_y()
        for job in jobs[3:]:
            job.start_wide()
        jobs[0].finish_y()
        jobs[0].start_core()
        jobs[0].finish_core()

    @pl.when(i == 1)
    def _():
        jobs[1].finish_y()
        jobs[1].start_core()

    @pl.when(i == 2)
    def _():
        jobs[2].finish_y()
        jobs[2].start_core()

    @pl.when(i < micro)
    def _():
        q = feature(nn(h_all[i], weights(0))).astype(BF16)
        q_out[...] = q
        q_all[i] = q

    @pl.when(i == micro)
    def _():
        jobs[1].finish_core()

    @pl.when((i >= micro) & (i < 2 * micro))
    def _():
        m = i - micro
        k = feature(nn(h_all[m], weights(1))).astype(BF16)
        k_out[...] = k
        k_all[m] = k

    @pl.when(i == 2 * micro)
    def _():
        jobs[2].finish_core()
        for j in range(3):
            save(j).start()

    @pl.when((i >= 2 * micro) & (i < 3 * micro))
    def _():
        m = i - 2 * micro
        v = nn(h_all[m], weights(2)).astype(BF16)
        v_out[...] = v
        v_all[m] = v
        base = off[0]
        final = start_of(lens, m, base + rows - 1)
        last = flag(start_of(lens, m, place_rows(base, rows)) == final)
        k_last = k_all[m] * rows_of(last.astype(BF16), d)
        k_turned = k_last.T
        mask = ones[0:128, 0:128].astype(F32)
        parts = [nn(k_turned[128 * p : 128 * p + 128, :], v[:, 128 * p : 128 * p + 128]) * mask for p in range(4)]
        pack_state(parts, column_sum(k_last.astype(F32)), local.at[m])

    @pl.when(i == 2 * micro + half - 1)
    def _():
        running[0].start1()

    @pl.when(i == 3 * micro - 1)
    def _():
        running[1].start1()

    def pass_on(step, *parts):
        @pl.when(i == step)
        def _():
            for job in parts:
                job.finish_wide()
                job.start_y()

    def cross_over(step, *parts):
        @pl.when(i == step)
        def _():
            for job in parts:
                job.finish_y()
                job.start_core()

    pass_on(micro + 1, jobs[3], jobs[4])
    pass_on(2 * micro + 1, jobs[5])
    pass_on(3 * micro, jobs[6])

    @pl.when(i == 3 * micro)
    def _():
        running[0].finish1_start2()

    cross_over(3 * micro, jobs[3], jobs[4])
    pass_on(3 * micro + 1, jobs[7])

    @pl.when(i == 3 * micro + 1)
    def _():
        running[1].finish1_start2()

    cross_over(3 * micro + 2, jobs[5], jobs[6])

    @pl.when(i == 3 * micro + 2)
    def _():
        running[0].finish2_start3()

    @pl.when(i == 3 * micro + 3)
    def _():
        running[1].finish2_start3()

    cross_over(3 * micro + 3, jobs[7])

    @pl.when(i >= 3 * micro)
    def _():
        m = i - 3 * micro
        attend(lens, m, off[0], q_all.at[m], k_all.at[m], v_all.at[m], ones, num_out, kc_out, states_out, state, norm)

    @pl.when(i == 4 * micro - 1)
    def _():
        for j in range(2):
            running[j].finish3()
            state_in[half * j : half * j + half] = running[j].result[...]
        for job in jobs[3:]:
            job.finish_core()
        for j in range(3):
            save(j).wait()


def chunk_masks(lens, m, begin, size):
    by_row = start_of(lens, m, place_rows(begin, size))
    lane = begin + lax.broadcasted_iota(jnp.int32, (8, size), 1)
    by_column = start_of(lens, m, lane)[0:1, :]
    final = start_of(lens, m, begin + size - 1)
    return by_row, by_column, final


def split_pair(a, low, high):
    return jnp.concatenate([a * low, a * high], axis=0)


def attend(lens, m, base, q_ref, k_ref, v_ref, ones, num_out, kc_out, states_out, state, norm):
    rows, d = q_ref.shape
    size = CHUNK
    state[...] = jnp.zeros_like(state)
    norm[...] = jnp.zeros_like(norm)
    half = lane_half((1, 128))
    low = flag(half).astype(BF16)
    high = flag(jnp.logical_not(half)).astype(BF16)

    def step(c, carry):
        at = pl.ds(pl.multiple_of(c * size, size), size)
        begin = base + c * size
        q, k, v = q_ref[at, :], k_ref[at, :], v_ref[at, :]
        by_row, by_column, final = chunk_masks(lens, m, begin, size)
        places = lax.broadcasted_iota(jnp.int32, (size, size), 0)
        columns = lax.broadcasted_iota(jnp.int32, (size, size), 1)
        allowed = flag((places >= columns) & (by_row[:, :size] == by_column)).astype(BF16)
        allowed2 = jnp.concatenate([allowed, allowed], axis=1)
        seen = flag(by_row < begin)
        last = flag(by_row == final).astype(BF16)
        keep = jnp.where(final < begin, 1.0, 0.0)
        kc_out[at, :] = (nn(allowed, k) + rows_of(seen, d) * norm[...]).astype(BF16)
        q_seen = q * rows_of(seen.astype(BF16), d)
        for p in range(4):
            cut = slice(128 * p, 128 * p + 128)
            s = nt(q[:, cut], split_pair(k[:, cut], low, high)).astype(BF16) * allowed2
            inside = nn(s, split_pair(v[:, cut], low, high))
            held = state[p].astype(BF16)
            states_out[c, p] = held
            before = nn(q_seen[:, cut], held)
            num_out[at, cut] = (inside + before).astype(BF16)
        k_last = k * rows_of(last, d)
        k_turned = k_last.T
        mask = ones[0:128, 0:128].astype(F32)
        for p in range(4):
            cut = slice(128 * p, 128 * p + 128)
            state[p] = keep * state[p] + nn(k_turned[cut, :], v[:, cut]) * mask
        norm[...] = keep * norm[...] + column_sum(k_last.astype(F32))
        return carry

    lax.fori_loop(0, rows // size, step, 0, unroll=8)


def middle_kernel(
    lens, off, q_ref, num_ref, kc_ref, x_ref, cot_ref, state_in, ones,
    w_out, vec, w_up, w_down,
    block_out, gm_out, gnum_out, gden_out, use_out, grads_up, grads_down, g_vec,
    groups, norm, use, use_norm, acc_out, acc_up, acc_down, active_all, g_low_all, h2_ref, h2t_ref, ct_ref,
):
    m, t, tiles = pl.program_id(0), pl.program_id(1), pl.num_programs(1)
    rows, d = x_ref.shape
    first = (m == 0) & (t == 0)
    final = (m == pl.num_programs(0) - 1) & (t == tiles - 1)
    base = off[0]

    @pl.when(first)
    def _():
        acc_out[...] = jnp.zeros_like(acc_out)
        acc_up[...] = jnp.zeros_like(acc_up)
        acc_down[...] = jnp.zeros_like(acc_down)
        g_vec[...] = jnp.zeros_like(g_vec)
        h2t_ref[d:, :] = jnp.ones((16, rows), BF16)

    @pl.when(t == 0)
    def _():
        parts, z = unpack_state(state_in[...], ones[...])
        for g in range(2):
            groups[g] = parts[g]
        norm[...] = z
        use[...] = jnp.zeros_like(use)
        use_norm[...] = jnp.zeros_like(use_norm)

    gain, bias, down_bias = vec[2:3, :], vec[3:4, :], vec[4:5, :]
    q = q_ref[...]
    seen = flag(start_of(lens, m, place_rows(base + t * rows, rows)) < base)
    q_seen = q * rows_of(seen.astype(BF16), d)
    num = num_ref[...].astype(F32) + by_group(lambda g, a: nn(a, groups[g]), q_seen)
    kc = kc_ref[...].astype(F32) + rows_of(seen, d) * norm[...]
    den = by_group(lambda g, a: nn(a, ones[...]), (q.astype(F32) * kc).astype(BF16))
    over = 1.0 / den
    mixed = (num * over).astype(BF16)
    middle = x_ref[...].astype(F32) + nn(mixed, w_out[...])
    xhat, scale = normed(middle)
    h2 = (xhat * gain + bias).astype(BF16)
    h2_ref[...] = h2
    h2t_ref[0:d, :] = h2.T
    ct_ref[...] = cot_ref[...].T

    def ffn(f, carry):
        cut = pl.ds(pl.multiple_of(f * FF_TILE, FF_TILE), FF_TILE)
        hidden = nn(h2_ref[...], w_up[:, cut]) + vec[pl.ds(5 + f, 1), :]
        pulled = nt(cot_ref[...], w_down[cut, :])
        square = hidden * hidden
        c0, c1 = 0.7978845608028654, 0.044715
        th = jnp.tanh(hidden * (c0 + (c0 * c1) * square))
        half_up = 0.5 + 0.5 * th
        active = (hidden * half_up).astype(BF16)
        slope = half_up + hidden * (1.0 - th * th) * (0.5 * c0 + (1.5 * c0 * c1) * square)
        g_low = (slope * pulled).astype(BF16)
        active_all[:, cut] = active
        g_low_all[:, cut] = g_low
        acc_down[:, cut] += nn(ct_ref[...], active)
        acc_up[:, cut] += nn(h2t_ref[...], g_low)
        return carry

    lax.fori_loop(0, w_up.shape[1] // FF_TILE, ffn, 0, unroll=True)
    block_out[...] = (middle + down_bias + nn(active_all[...], w_down[...])).astype(BF16)
    e = nt(g_low_all[...], w_up[...])
    cot = cot_ref[...].astype(F32)
    g_middle = cot + norm_back(e, xhat, scale, gain)
    gm_out[...] = g_middle.astype(BF16)
    g_vec[2:3, :] += column_sum(e * xhat)
    g_vec[3:4, :] += column_sum(e)
    g_vec[4:5, :] += column_sum(cot)
    branch = g_middle.astype(BF16)
    acc_out[...] += nn(mixed.T, branch)
    g_mixed = nt(branch, w_out[...])
    gnum = (g_mixed * over).astype(BF16)
    gnum_out[...] = gnum
    gden = -by_group(lambda g, a: nn(a, ones[...]), (g_mixed * num).astype(BF16)) * (over * over)
    gden_out[...] = gden.astype(BF16)
    turned = q_seen.T
    for g in range(2):
        cut = slice(256 * g, 256 * g + 256)
        use[g] += nn(turned[cut, :], gnum[:, cut])
    use_norm[...] += column_sum(q_seen.astype(F32) * gden)

    @pl.when(t == tiles - 1)
    def _():
        mask = ones[0:128, 0:128].astype(F32)
        pack_state([use[p // 2][128 * (p % 2) : 128 * (p % 2) + 128, 128 * (p % 2) : 128 * (p % 2) + 128] * mask for p in range(4)], use_norm[...], use_out)

    @pl.when(final)
    def _():
        for j in range(4):
            g_vec[5 + j : 6 + j, :] = acc_up[d : d + 1, d * j : d * j + d]
        n = grads_up.shape[0]
        each = d // n
        down = acc_down[...].astype(BF16).T
        for w in range(n):
            at = slice(each * w, each * w + each)
            for j in range(4):
                put(grads_up.at[w], each * j, acc_up[at, d * j : d * j + d].astype(BF16))
            put(grads_up.at[w], 4 * each, acc_out[at, :].astype(BF16))
            fill(grads_up.at[w], 5 * each, d)
            put(grads_down.at[w], 0, down[4 * each * w : 4 * each * w + 4 * each, :])
            fill(grads_down.at[w], 4 * each, d)


def attend_back(
    lens, m, base, lead, q_ref, k_ref, v_ref, gnum_ref, gden_ref, kc_ref, states, state_in, ones,
    gq_out, dk_out, dv_out, after, after_norm,
):
    rows, d = q_ref.shape
    size = CHUNK
    count = rows // size
    half = lane_half((1, 128))
    low = flag(half).astype(BF16)
    high = flag(jnp.logical_not(half)).astype(BF16)
    pairs_in, norm_in = unpack_pairs(state_in[...], ones[...])

    def step(i, carry):
        c = count - 1 - i
        at = pl.ds(pl.multiple_of(c * size, size), size)
        begin = lead + c * size
        q, k, v, gnum = q_ref[at, :], k_ref[at, :], v_ref[at, :], gnum_ref[at, :]
        gden = gden_ref[at, :].astype(F32)
        by_row, by_column, final = chunk_masks(lens, m, begin, size)
        places = lax.broadcasted_iota(jnp.int32, (size, size), 0)
        columns = lax.broadcasted_iota(jnp.int32, (size, size), 1)
        same = by_row[:, :size] == by_column
        allowed = flag((places >= columns) & same).astype(BF16)
        allowed2 = jnp.concatenate([allowed, allowed], axis=1)
        turned = flag((places <= columns) & same).astype(BF16)
        turned2 = jnp.concatenate([turned, turned], axis=1)
        seen = rows_of(flag(by_row < begin).astype(BF16), d)
        seen_all = flag(by_row < base)
        last = flag(by_row == final)
        keep = jnp.where(final < begin, 1.0, 0.0)
        last_low = rows_of(last.astype(BF16), d)
        carried = jnp.where((begin == base) | (start_of(lens, m, begin - 1) < base), 1.0, 0.0)
        gnum_seen = gnum * seen
        k_last, v_last = k * last_low, v * last_low
        gden_q = gden * q.astype(F32)
        dk_den = nn(turned, gden_q.astype(BF16)) + rows_of(last, d) * after_norm[...]
        dq_den = gden * (kc_ref[at, :].astype(F32) + rows_of(seen_all, d) * norm_in)
        for p in range(4):
            cut = slice(128 * p, 128 * p + 128)
            held = (states[c, p].astype(F32) + carried * pairs_in[p]).astype(BF16)
            g_after = after[p].astype(BF16)
            qp, kp, vp, gp = q[:, cut], k[:, cut], v[:, cut], gnum[:, cut]
            q2, k2 = split_pair(qp, low, high), split_pair(kp, low, high)
            v2, g2 = split_pair(vp, low, high), split_pair(gp, low, high)
            s_turned = nt(kp, q2).astype(BF16) * turned2
            gs_turned = nt(vp, g2).astype(BF16) * turned2
            gs = nt(gp, v2).astype(BF16) * allowed2
            dq = nn(gs, k2) + nt(gnum_seen[:, cut], held) + dq_den[:, cut]
            gq_out[at, cut] = (jnp.minimum(qp.astype(F32), 1.0) * dq).astype(BF16)
            dk = nn(gs_turned, q2) + nt(v_last[:, cut], g_after) + dk_den[:, cut]
            dk_out[at, cut] = dk.astype(BF16)
            dv = nn(s_turned, g2) + nn(k_last[:, cut], g_after)
            dv_out[at, cut] = dv.astype(BF16)
        q_turned = (q * seen).T
        mask = ones[0:128, 0:128].astype(F32)
        for p in range(4):
            cut = slice(128 * p, 128 * p + 128)
            after[p] = keep * after[p] + nn(q_turned[cut, :], gnum[:, cut]) * mask
        after_norm[...] = keep * after_norm[...] + column_sum(gden_q * seen.astype(F32))
        return carry

    lax.fori_loop(0, count, step, 0, unroll=4)


def last_kernel(lens, off, *refs):
    (q_ref, k_half, v_half, gnum_ref, gden_ref, kc_ref, states, state_in, k_ref, v_ref, x_ref,
     use, grads_up, grads_down, g_vec, ones, vec, w,
     gx_out, up_out, down_out, k_out, v_out, q_out, vector_out,
     gq_all, dk_all, dv_all, h1t_all, acc, after, after_norm, sums, shares, src_k, src_v, src_q, *rest) = refs
    micro = use.shape[0]
    rows, d = k_ref.shape
    part_rows = q_ref.shape[0]
    halves = rows // part_rows
    n = src_q.shape[0]
    each = d // n
    running = Running(use, False, rest[:13])
    rest = rest[13:]
    jobs = [
        Scatter(src, rest[13 * j : 13 * j + 13]) for j, src in enumerate((grads_up, grads_down, src_k, src_v, src_q))
    ]
    of_up, of_down, of_k, of_v, of_q = jobs
    vector = VectorSum(rest[65:])
    i = pl.program_id(0)
    base = off[0]
    p1 = halves * micro
    p2, p3 = p1 + micro, p1 + 2 * micro
    p4, end = p3 + 1, p3 + 1 + micro

    def at_step(step, *actions):
        @pl.when(i == step)
        def _():
            for action in actions:
                action()

    @pl.when(i == 0)
    def _():
        signal_all()
        acc[...] = jnp.zeros_like(acc)
        shares[...] = jnp.zeros_like(shares)

    at_step(1, wait_all, of_up.start1, of_down.start1, running.start1)
    at_step(2, of_up.finish1_start2, of_down.finish1_start2)
    at_step(3, running.finish1_start2)
    at_step(p1 - 2, of_up.finish2_start3)
    at_step(p1 - 1, running.finish2_start3)
    at_step(p1, running.finish3, of_down.finish2_start3)
    at_step(p1 + 3, of_up.finish3_start4)
    at_step(p2 + 1, of_up.finish4, of_k.finish1_start2)
    at_step(p4, of_down.finish3_start4)
    at_step(p4 + 1, of_k.finish3_start4, of_v.finish2_start3, vector.finish1_start2)
    at_step(p4 + 2, of_down.finish4, of_q.finish2_start3)
    at_step(p4 + 3, of_k.finish4, vector.finish2_start3)

    @pl.when(i < p1)
    def _():
        m, t = i // halves, halves - 1 - lax.rem(i, halves)

        @pl.when(t == halves - 1)
        def _():
            after[...] = jnp.zeros_like(after)
            after_norm[...] = jnp.zeros_like(after_norm)

        lead = t * part_rows
        at = pl.ds(pl.multiple_of(m * rows + lead, part_rows), part_rows)
        attend_back(
            lens, m, base, base + lead, q_ref, k_half, v_half, gnum_ref, gden_ref, kc_ref, states, state_in, ones,
            gq_all.at[at], dk_all.at[at], dv_all.at[at], after, after_norm,
        )

    def block(m):
        final = start_of(lens, m, base + rows - 1)
        last = flag(start_of(lens, m, place_rows(base, rows)) == final)
        groups, norm = unpack_state(running.result[m], ones[...])
        return last, rows_of(last.astype(BF16), d), groups, norm

    @pl.when((i >= p1) & (i < p2))
    def _():
        m = i - p1
        at = pl.ds(pl.multiple_of(m * rows, rows), rows)
        last, last_low, groups, norm = block(m)
        dk = dk_all[at, :].astype(F32) + rows_of(last, d) * norm
        dk = dk + by_group(lambda g, a: nt(a, groups[g]), v_ref[...] * last_low)
        gk = (jnp.minimum(k_ref[...].astype(F32), 1.0) * dk).astype(BF16)
        dk_all[at, :] = gk
        xhat, _ = normed(x_ref[...].astype(F32))
        h1t = (xhat * vec[0:1, :] + vec[1:2, :]).astype(BF16).T
        h1t_all[:, at] = h1t
        acc[:, d : 2 * d] += nn(h1t, gk)
        shares[:, d : 2 * d] += column_sum(gk.astype(F32))

    def arrange(src, part):
        for w_ in range(n):
            put(src.at[w_], 0, acc[each * w_ : each * w_ + each, d * part : d * part + d].astype(BF16))
            fill(src.at[w_], each, d)

    @pl.when(i == p2 - 1)
    def _():
        arrange(src_k, 1)
        of_k.start1()

    @pl.when((i >= p2) & (i < p3))
    def _():
        m = i - p2
        at = pl.ds(pl.multiple_of(m * rows, rows), rows)
        _, last_low, groups, _ = block(m)
        gv = dv_all[at, :].astype(F32) + by_group(lambda g, a: nn(a, groups[g]), k_ref[...] * last_low)
        gv = gv.astype(BF16)
        dv_all[at, :] = gv
        acc[:, 2 * d :] += nn(h1t_all[:, at], gv)
        shares[:, 2 * d :] += column_sum(gv.astype(F32))

    @pl.when(i == p3 - 1)
    def _():
        arrange(src_v, 2)
        of_v.start1()

    @pl.when(i == p3)
    def _():
        up_out[...] = of_up.out[...]

        def add(m, carry):
            at = pl.ds(pl.multiple_of(m * rows, rows), rows)
            gq = gq_all[at, :]
            acc[:, 0:d] += nn(h1t_all[:, at], gq)
            shares[:, 0:d] += column_sum(gq.astype(F32))
            return carry

        lax.fori_loop(0, micro // 2, add, 0)
        of_k.finish2_start3()
        of_v.finish1_start2()
        lax.fori_loop(micro // 2, micro, add, 0)
        arrange(src_q, 0)
        of_q.start1()
        both = jnp.zeros((d, 128), F32)
        only = jnp.zeros((d, 128), F32)
        for j in range(3 * d // 128):
            cut = slice(128 * j, 128 * j + 128)
            weight = w[:, cut].astype(F32)
            both = both + weight * acc[:, cut]
            only = only + weight * shares[:, cut]
        both, only = column_sum(both.T), column_sum(only.T)
        sums[...] = g_vec[...]
        sums[0:1, :] = (both - vec[1:2, :] * only) / vec[0:1, :]
        sums[1:2, :] = only
        owner_tiles(sums[...], vector.tiles, each)
        vector.start1()
        of_q.finish1_start2()

    @pl.when(i >= p4)
    def _():
        at = pl.ds(pl.multiple_of((i - p4) * rows, rows), rows)
        e = nt(gq_all[at, :], w[:, 0:d]) + nt(dk_all[at, :], w[:, d : 2 * d]) + nt(dv_all[at, :], w[:, 2 * d :])
        xhat, scale = normed(x_ref[...].astype(F32))
        gx_out[...] = norm_back(e, xhat, scale, vec[0:1, :]).astype(BF16)

    @pl.when(i == end - 1)
    def _():
        of_v.finish3_start4()
        of_q.finish3_start4()
        down_out[...] = of_down.out[...]
        k_out[...] = of_k.out[...]
        vector_out[...] = vector.finish3()
        of_v.finish4()
        v_out[...] = of_v.out[...]
        of_q.finish4()
        q_out[...] = of_q.out[...]


def result_kernel(
    gm_ref, part_ref, of_up, of_down, of_k, of_v, of_q, vector, gx, g_qkv, g_out, g_up, g_down, v0, v1, v2, v3, v4, v5
):
    gx[...] = gm_ref[...].astype(F32) + part_ref[...].astype(F32)

    @pl.when(pl.program_id(0) == 0)
    def _():
        each, d = g_out.shape
        for j in range(4):
            g_up[:, d * j : d * j + d] = get(of_up, each * j, each, d).astype(F32)
        g_out[...] = get(of_up, 4 * each, each, d).astype(F32)
        g_down[...] = get(of_down, 0, 4 * each, d).astype(F32)
        for j, part in enumerate((of_q, of_k, of_v)):
            g_qkv[:, d * j : d * j + d] = get(part, 0, each, d).astype(F32)
        for j, v in enumerate((v0, v1, v2, v3, v4)):
            v[...] = vector[j : j + 1, :each]
        for r in range(4):
            v5[:, each * r : each * r + each] = vector[5 + r : 6 + r, :each]


def params(count):
    return pltpu.CompilerParams(
        dimension_semantics=("arbitrary",) * count, vmem_limit_bytes=VMEM
    )


def small():
    return pl.BlockSpec(memory_space=pltpu.SMEM)


def per_device(
    block_in, cotangent, ln1_gain, ln1_bias, qkv_weight, out_weight, ln2_gain, ln2_bias,
    up_weight, up_bias, down_weight, down_bias, seq_lengths,
):
    micro, rows, d = block_in.shape[0], block_in.shape[2], block_in.shape[3]
    ff = up_weight.shape[1]
    wide, index = lax.axis_size("wide"), lax.axis_index("wide")
    lens = seq_lengths.reshape(micro, -1)
    off = (index * rows).astype(jnp.int32).reshape(1)
    x = block_in.reshape(micro, rows, d)
    cot = cotangent.reshape(micro, rows, d)

    each = d // wide
    lane = jnp.arange(256) // 64
    ones = (lane[:, None] == lane[None, :]).astype(BF16)

    tiles = rows // TILE
    token = pl.BlockSpec((None, TILE, d), lambda m, t: (m, t, 0))
    whole = lambda shape: pl.BlockSpec(shape, lambda *_: (0,) * len(shape))
    fixed = lambda shape: pl.BlockSpec(
        shape, lambda *_: (0,) * len(shape), pipeline_mode=pl.Buffered(1)
    )
    packed = pl.BlockSpec((None, state_rows(), 128), lambda m, *_: (m, 0, 0))
    like = lambda dtype: jax.ShapeDtypeStruct((micro, rows, d), dtype)
    up_shape, down_shape = packed_shape(5 * each, d), packed_shape(4 * each, d)

    block = pl.BlockSpec((None, rows, d), lambda m: (m, 0, 0))
    count = rows // CHUNK
    states_spec = pl.BlockSpec((None, count, 2, 256, 256), lambda m: (m, 0, 0, 0, 0))
    during = lambda begin, *shape: pl.BlockSpec(
        (None,) + shape, lambda i: (jnp.clip(i - begin, 0, micro - 1),) + (0,) * len(shape)
    )
    anywhere = pl.BlockSpec(memory_space=pl.ANY)
    spread = lambda a: jax.ShapeDtypeStruct((wide,) + a.shape, BF16)
    dma = pltpu.SemaphoreType.DMA
    vectors = [a.reshape(1, -1) for a in (ln1_gain, ln1_bias, ln2_gain, ln2_bias, down_bias, up_bias)]
    state_shape = (micro, state_rows(), 128)
    (q, k, v, num, kc, states, state_in, w_qkv, w_out, w_up, w_down, vec) = pl.pallas_call(
        first_kernel,
        grid=(4 * micro,),
        in_specs=[small(), small(), fixed((micro, rows, d))] + [anywhere] * 4 + [whole(a.shape) for a in vectors] + [whole((256, 256))],
        out_specs=[during(micro * j, rows, d) for j in range(3)] + [during(3 * micro, rows, d)] * 2
        + [during(3 * micro, count, 4, 128, 128), whole(state_shape)]
        + [anywhere] * 4 + [whole((16, d))],
        out_shape=[like(BF16)] * 5 + [
            jax.ShapeDtypeStruct((micro, count, 4, 128, 128), BF16), jax.ShapeDtypeStruct(state_shape, F32),
            spread(qkv_weight), spread(out_weight), spread(up_weight), spread(down_weight),
            jax.ShapeDtypeStruct((16, d), F32),
        ],
        scratch_shapes=[pltpu.VMEM((3, wide, each, d), BF16)]
        + [pltpu.VMEM((micro, rows, d), BF16)] * 4
        + [
            pltpu.VMEM((4, 128, 128), F32), pltpu.VMEM((1, d), F32), pltpu.VMEM(state_shape, BF16), pltpu.VMEM((16, 128), BF16), pltpu.VMEM((wide, 16, 128), BF16),
            dma, dma((wide,)), dma((wide,)), dma((3,)),
        ]
        + running_scratch(micro // 2) * 2
        + gather_sems() * 8,
        compiler_params=pltpu.CompilerParams(
            dimension_semantics=("arbitrary",), vmem_limit_bytes=VMEM, collective_id=0, has_side_effects=True
        ),
        name="first",
    )(lens, off, x, qkv_weight, out_weight, up_weight, down_weight, *vectors, ones)
    w_qkv, w_out = w_qkv.reshape(d, 3 * d), w_out.reshape(d, d)
    w_up, w_down = w_up.reshape(d, ff), w_down.reshape(ff, d)

    result, g_middle, gnum, gden, use, grads_up, grads_down, g_vec = pl.pallas_call(
        middle_kernel,
        grid=(micro, tiles),
        in_specs=[small(), small()] + [token] * 5 + [packed, whole((256, 256))] + [
            fixed((d, d)), whole((16, d)), fixed((d, ff)), fixed((ff, d)),
        ],
        out_specs=[token, token, token, token, packed, fixed((wide,) + up_shape), fixed((wide,) + down_shape), whole((16, d))],
        out_shape=[
            like(BF16), like(BF16), like(BF16), like(BF16), jax.ShapeDtypeStruct(state_shape, BF16),
            jax.ShapeDtypeStruct((wide,) + up_shape, BF16), jax.ShapeDtypeStruct((wide,) + down_shape, BF16),
            jax.ShapeDtypeStruct((16, d), F32),
        ],
        scratch_shapes=[
            pltpu.VMEM((2, 256, 256), BF16), pltpu.VMEM((1, d), F32),
            pltpu.VMEM((2, 256, 256), F32), pltpu.VMEM((1, d), F32),
            pltpu.VMEM((d, d), F32), pltpu.VMEM((d + 16, ff), F32), pltpu.VMEM((d, ff), F32),
            pltpu.VMEM((TILE, ff), BF16), pltpu.VMEM((TILE, ff), BF16), pltpu.VMEM((TILE, d), BF16),
            pltpu.VMEM((d + 16, TILE), BF16), pltpu.VMEM((d, TILE), BF16),
        ],
        compiler_params=params(2),
        name="middle",
    )(lens, off, q, num, kc, x, cot, state_in, ones, w_out, vec, w_up, w_down)

    spare = 2 if wide <= 8 else 1
    halves = rows // TILE
    p1 = halves * micro
    p2, p4 = p1 + micro, p1 + 2 * micro + 1

    def backward(*shape):
        def at(i):
            i = jnp.minimum(i, p1 - 1)
            return (i // halves, halves - 1 - lax.rem(i, halves)) + (0,) * (len(shape) - 1)

        return pl.BlockSpec((None,) + shape, at)

    def walk(*begins, buffers=2):
        def at(i):
            j = 0
            for b in begins:
                j = j + jnp.where(i >= b, jnp.clip(i - b, 0, micro - 1) - j, 0)
            return (j, 0, 0)

        return pl.BlockSpec((None, rows, d), at, pipeline_mode=pl.Buffered(buffers))

    part_shape = packed_shape(each, d)
    vector_shapes = [(1, each)] * 5 + [(1, 4 * each)]
    summed_shapes = [up_shape, down_shape, part_shape, part_shape, part_shape, (16, 128)]
    result_shapes = [(each, 3 * d), (each, d), (each, ff), (4 * each, d)] + vector_shapes
    part, *summed = pl.pallas_call(
        last_kernel,
        grid=(p4 + micro,),
        in_specs=[small(), small()] + [backward(TILE, d)] * 6 + [backward(count // halves, 4, 128, 128)]
        + [pl.BlockSpec((None, state_rows(), 128), lambda i: (jnp.minimum(i // halves, micro - 1), 0, 0))]
        + [walk(p1, p2, buffers=spare), walk(p1, buffers=spare), walk(p1, p4, buffers=spare)] + [anywhere] * 3
        + [whole((16, d)), whole((256, 256)), whole((16, d)), fixed((d, 3 * d))],
        out_specs=[walk(p4)] + [fixed(s) for s in summed_shapes],
        out_shape=[like(BF16)] + [jax.ShapeDtypeStruct(s, BF16) for s in summed_shapes[:5]]
        + [jax.ShapeDtypeStruct((16, 128), F32)],
        scratch_shapes=[pltpu.VMEM((micro * rows, d), BF16)] * 3
        + [
            pltpu.VMEM((d, micro * rows), BF16), pltpu.VMEM((d, 3 * d), F32),
            pltpu.VMEM((4, 128, 128), F32), pltpu.VMEM((1, d), F32),
            pltpu.VMEM((16, d), F32), pltpu.VMEM((1, 3 * d), F32),
        ]
        + [pltpu.VMEM((wide,) + part_shape, BF16)] * 3
        + running_scratch(micro)
        + scatter_scratch(up_shape) + scatter_scratch(down_shape) + scatter_scratch(part_shape) * 3
        + vector_scratch(),
        compiler_params=pltpu.CompilerParams(
            dimension_semantics=("arbitrary",), vmem_limit_bytes=VMEM, collective_id=1, has_side_effects=True
        ),
        name="last",
    )(lens, off, q, k, v, gnum, gden, kc, states, state_in, k, v, x, use, grads_up, grads_down, g_vec, ones, vec, w_qkv)
    grad_input, g_qkv, g_out, g_up, g_down, *g_vectors = pl.pallas_call(
        result_kernel,
        grid=(micro,),
        in_specs=[block, block] + [whole(s) for s in summed_shapes],
        out_specs=[block] + [whole(s) for s in result_shapes],
        out_shape=[like(F32)] + [jax.ShapeDtypeStruct(s, F32) for s in result_shapes],
        compiler_params=params(1),
        name="result",
    )(g_middle, part, *summed)
    piece = [a.reshape(-1) for a in g_vectors]
    return (
        result.reshape(block_in.shape),
        grad_input.reshape(block_in.shape),
        piece[0],
        piece[1],
        g_qkv,
        g_out,
        piece[2],
        piece[3],
        g_up,
        piece[5],
        g_down,
        piece[4],
    )


def solution(mesh):
    tokens = P(None, "dp", "wide", None)
    vector, matrix = P("wide"), P("wide", None)
    weights = (vector, vector, matrix, matrix, vector, vector, matrix, vector, matrix, vector)
    return jax.shard_map(
        per_device,
        mesh=mesh,
        in_specs=(tokens, tokens) + weights + (P(None, "dp", None),),
        out_specs=(tokens, tokens) + weights,
        check_vma=False,
    )
```
